32 devices in a mesh: dp: 4 (over z), fsdp: 8 (over y, x, core).
Axes of the slice: x: 2, y: 2, z: 4, core: 2. Of those that a mesh axis runs over, the one named last changes fastest.
Arguments:
- decoder_in: bfloat16 [256, 256, 512], P(('dp', 'fsdp')), may hold values from -6 to 6
- memory: bfloat16 [256, 256, 512], P(('dp', 'fsdp')), may hold values from -6 to 6
- out_grad: bfloat16 [256, 256, 512], P(('dp', 'fsdp')), may hold values from -6 to 6
- tgt_len: int32 [256, 24], P(('dp', 'fsdp')), may hold values from 0 to 250, as said below
- src_len: int32 [256, 24], P(('dp', 'fsdp')), may hold values from 0 to 250, as said below
- self_qkv: bfloat16 [3, 512, 512], P(None, None, ('dp', 'fsdp')), may hold values from -0.25 to 0.25
- self_bias: bfloat16 [3, 512], P(None, ('dp', 'fsdp')), may hold values from -2 to 2
- self_out: bfloat16 [512, 512], P(None, ('dp', 'fsdp')), may hold values from -0.75 to 0.75
- self_norm: bfloat16 [2, 512], P(None, ('dp', 'fsdp')), may hold values from -0.5 to 1.4, as said below
- cross_q: bfloat16 [512, 512], P(None, ('dp', 'fsdp')), may hold values from -0.25 to 0.25
- cross_kv: bfloat16 [2, 512, 512], P(None, None, ('dp', 'fsdp')), may hold values from -0.25 to 0.25
- cross_bias: bfloat16 [3, 512], P(None, ('dp', 'fsdp')), may hold values from -2 to 2
- cross_out: bfloat16 [512, 512], P(None, ('dp', 'fsdp')), may hold values from -0.5 to 0.5
- cross_norm: bfloat16 [2, 512], P(None, ('dp', 'fsdp')), may hold values from -0.5 to 1.4, as said below
- ffn_in: bfloat16 [512, 2048], P(None, ('dp', 'fsdp')), may hold values from -0.25 to 0.25
- ffn_in_bias: bfloat16 [2048], P(('dp', 'fsdp')), may hold values from -2 to 2
- ffn_out: bfloat16 [2048, 512], P(None, ('dp', 'fsdp')), may hold values from -0.1875 to 0.1875
- ffn_out_bias: bfloat16 [512], P(('dp', 'fsdp')), may hold values from -2 to 2
- ffn_norm: bfloat16 [2, 512], P(None, ('dp', 'fsdp')), may hold values from -0.5 to 1.4, as said below
Outputs:
- decoder_out: bfloat16 [256, 256, 512], P(('dp', 'fsdp'))
- grad_decoder_in: bfloat16 [256, 256, 512], P(('dp', 'fsdp'))
- grad_memory: bfloat16 [256, 256, 512], P(('dp', 'fsdp'))
- grad_self_qkv: float32 [3, 512, 512], P(None, None, ('dp', 'fsdp'))
- grad_self_bias: float32 [3, 512], P(None, ('dp', 'fsdp'))
- grad_self_out: float32 [512, 512], P(None, ('dp', 'fsdp'))
- grad_self_norm: float32 [2, 512], P(None, ('dp', 'fsdp'))
- grad_cross_q: float32 [512, 512], P(None, ('dp', 'fsdp'))
- grad_cross_kv: float32 [2, 512, 512], P(None, None, ('dp', 'fsdp'))
- grad_cross_bias: float32 [3, 512], P(None, ('dp', 'fsdp'))
- grad_cross_out: float32 [512, 512], P(None, ('dp', 'fsdp'))
- grad_cross_norm: float32 [2, 512], P(None, ('dp', 'fsdp'))
- grad_ffn_in: float32 [512, 2048], P(None, ('dp', 'fsdp'))
- grad_ffn_in_bias: float32 [2048], P(('dp', 'fsdp'))
- grad_ffn_out: float32 [2048, 512], P(None, ('dp', 'fsdp'))
- grad_ffn_out_bias: float32 [512], P(('dp', 'fsdp'))
- grad_ffn_norm: float32 [2, 512], P(None, ('dp', 'fsdp'))
The draws below stay inside these ranges and needn't reach their ends.
Inputs may be any that keep to these rules, and one draw needn't show every extreme that they name: `tgt_len`: sentence lengths in order; a row's entries sum to 256; zero marks an unused sentence slot. `src_len`: zero exactly where tgt_len is zero, otherwise from 1 to the tgt_len entry of the same slot; a row's entries sum to at most 256. `self_norm`: row 0 holds gains, row 1 shifts. `cross_norm`: row 0 holds gains, row 1 shifts. `ffn_norm`: row 0 holds gains, row 1 shifts.
All inputs are finite; a program needn't handle non-finite values.
Results may differ from the reference program's by a relative error of at most 0.018.
Values may be sent and summed in bfloat16 or wider, within the bound.
A program may use at most 320 MiB of HBM per device.

```python
import jax
import jax.numpy as jnp
from jax import lax

D = 512
HEADS = 8
HEAD_DIM = 64
FF = 2048
SLOTS = 256
SENTS = 24
ROWS = 256


def sentence_lengths(key):
    key_length, key_single, key_shrink = jax.random.split(key, 3)
    drawn_lengths = jax.random.randint(key_length, (ROWS, SENTS), 11, 41, dtype=jnp.int32)
    begin_at = jnp.cumsum(drawn_lengths, axis=1) - drawn_lengths
    clipped = jnp.clip(SLOTS - begin_at, 0, drawn_lengths)
    leading = clipped[:, :-1]
    closing = jnp.maximum(SLOTS - jnp.sum(leading, axis=1, keepdims=True), 0)
    packed = jnp.concatenate([leading, closing], axis=1)
    single_row = jnp.zeros((SENTS,), jnp.int32).at[0].set(SLOTS - 6).at[1].set(6)
    row_number = jnp.arange(ROWS, dtype=jnp.int32)
    solitary = (row_number % 16 == 3) | (jax.random.randint(key_single, (ROWS,), 0, 32, dtype=jnp.int32) == 0)
    target = jnp.where(solitary[:, None], single_row[None, :], packed)
    shrink_factor = jax.random.randint(key_shrink, (ROWS, SENTS), 6, 17, dtype=jnp.int32)
    source = jnp.minimum(target, jnp.maximum(1, target * shrink_factor // 16))
    source = jnp.where(solitary[:, None], target, source)
    return (target, source)


def draw_tgt_len(key, part):
    return sentence_lengths(key)[0]


def draw_src_len(key, part):
    return sentence_lengths(key)[1]


def norm_table(key):
    key_gain, key_shift = jax.random.split(key)
    gains = jax.random.uniform(key_gain, (D,), jnp.float32, 0.6, 1.4)
    shifts = jax.random.uniform(key_shift, (D,), jnp.float32, -0.5, 0.5)
    return jnp.stack([gains, shifts]).astype(jnp.bfloat16)


def draw_self_norm(key, part):
    key = jax.random.fold_in(key, 11)
    return norm_table(key)


def draw_cross_norm(key, part):
    key = jax.random.fold_in(key, 12)
    return norm_table(key)


def draw_ffn_norm(key, part):
    key = jax.random.fold_in(key, 13)
    return norm_table(key)


def spiked(drawn, own_key, source, target, parts, factor):
    def block_of(axis_at):
        return (jnp.arange(drawn.shape[axis_at]) // (drawn.shape[axis_at] // parts)).reshape((-1,) + (1,) * (drawn.ndim - 1 - axis_at))

    first = jax.random.permutation(own_key, parts)[block_of(target)]
    second = (block_of(target) + parts // 2) % parts
    return jnp.where((block_of(source) == first) | (block_of(source) == second), factor * drawn, drawn)


def level_of(key, extent, shards, smallest, largest):
    gain = 1.0
    for axis_at, shards_of in shards:
        draws = jax.random.uniform(jax.random.fold_in(jax.random.fold_in(key, 6), axis_at), (shards_of,), jnp.float32, smallest / len(shards), largest / len(shards))
        gain = gain * jnp.repeat(jnp.exp(draws), extent[axis_at] // shards_of).reshape((-1,) + (1,) * (len(extent) - 1 - axis_at))
    return gain


def bell_draw(rng, shape, deviation, most, cuts=(), held_as=jnp.bfloat16):
    values = deviation * jax.random.normal(rng, shape, jnp.float32)
    if cuts:
        values = values * level_of(rng, shape, cuts, -0.22, 0.18)
    return jnp.clip(values, -most, most).astype(held_as)


def noise_with(key, shape, scale, most, shards, heavy, kind=jnp.bfloat16):
    drawn = scale * jax.random.normal(key, shape, jnp.float32)
    if shards:
        drawn = drawn * level_of(key, shape, shards, -0.22, 0.18)
    return jnp.clip(spiked(drawn, jax.random.fold_in(key, 3), *heavy), -most, most).astype(kind)


def setup_inputs(seed: int = 0) -> dict:
    arg_keys = jax.random.split(jax.random.key(seed), 20)
    return {
        "decoder_in": bell_draw(arg_keys[0], (ROWS, SLOTS, D), 1.0, 6.0, ((0, 32),)),
        "memory": bell_draw(arg_keys[1], (ROWS, SLOTS, D), 1.0, 6.0, ((0, 32),)),
        "out_grad": noise_with(arg_keys[2], (ROWS, SLOTS, D), 1.0, 6.0, ((0, 32),), (0, 2, 32, 2.75)),
        "tgt_len": draw_tgt_len(jax.random.fold_in(arg_keys[19], 71), 0),
        "src_len": draw_src_len(jax.random.fold_in(arg_keys[19], 71), 0),
        "self_qkv": bell_draw(arg_keys[5], (3, D, D), D ** -0.5, 0.25, ((2, 32),)),
        "self_bias": bell_draw(arg_keys[6], (3, D), 0.3, 2.0, ((1, 32),)),
        "self_out": bell_draw(arg_keys[7], (D, D), (D // 8) ** -0.5, 0.75, ((1, 32),)),
        "self_norm": draw_self_norm(jax.random.fold_in(arg_keys[19], 71), 0),
        "cross_q": bell_draw(arg_keys[9], (D, D), D ** -0.5, 0.25, ((1, 32),)),
        "cross_kv": bell_draw(arg_keys[10], (2, D, D), D ** -0.5, 0.25, ((2, 32),)),
        "cross_bias": bell_draw(arg_keys[11], (3, D), 0.3, 2.0, ((1, 32),)),
        "cross_out": bell_draw(arg_keys[12], (D, D), (D // 4) ** -0.5, 0.5, ((1, 32),)),
        "cross_norm": draw_cross_norm(jax.random.fold_in(arg_keys[19], 71), 0),
        "ffn_in": bell_draw(arg_keys[14], (D, FF), D ** -0.5, 0.25, ((1, 32),)),
        "ffn_in_bias": bell_draw(arg_keys[15], (FF,), 0.3, 2.0, ((0, 32),)),
        "ffn_out": bell_draw(arg_keys[16], (FF, D), (FF // 2) ** -0.5, 0.1875, ((1, 32),)),
        "ffn_out_bias": bell_draw(arg_keys[17], (D,), 0.3, 2.0, ((0, 32),)),
        "ffn_norm": draw_ffn_norm(jax.random.fold_in(arg_keys[19], 71), 0),
    }


epsilon = 1e-05
masked_score = -1e+30
highest = lax.Precision.HIGHEST

@jax.custom_vjp
def low(v):
    return lax.optimization_barrier(v.astype(jnp.bfloat16)).astype(jnp.float32)

@jax.custom_vjp
def low_back(v):
    return v

def low_keep(v):
    return (low(v), None)

def low_pass(kept, grad):
    return (grad,)

def back_keep(v):
    return (v, None)

def back_low(kept, grad):
    return (low(grad),)
low.defvjp(low_keep, low_pass)
low_back.defvjp(back_keep, back_low)

def segment_ids(lengths):
    places = jnp.arange(SLOTS, dtype=jnp.int32)
    finish = jnp.cumsum(lengths, axis=-1).astype(jnp.int32)
    return lax.optimization_barrier(jnp.sum((finish[:, None, :] <= places[None, :, None]).astype(jnp.int32), axis=-1))

def project(values, weight):
    return jnp.einsum('gsd,de->gse', values, weight, precision=highest)

def layer_norm(values, table):
    centred = values - lax.optimization_barrier(jnp.mean(values, axis=-1, keepdims=True))
    spread = lax.optimization_barrier(jnp.mean(centred * centred, axis=-1, keepdims=True))
    return centred * lax.rsqrt(spread + epsilon) * table[0] + table[1]

def attend(query, keys, values, allowed):
    groups, length = (query.shape[0], query.shape[1])
    width = keys.shape[1]
    query4 = query.reshape(groups, length, HEADS, HEAD_DIM)
    keys4 = keys.reshape(groups, width, HEADS, HEAD_DIM)
    values4 = values.reshape(groups, width, HEADS, HEAD_DIM)
    scores = jnp.einsum('gqhe,gkhe->ghqk', query4, keys4, precision=highest) * HEAD_DIM ** (-0.5)
    scores = low_back(scores)
    scores = jnp.where(allowed[:, None], scores, masked_score)
    shares = low(jax.nn.softmax(scores, axis=-1))
    mixture = jnp.einsum('ghqk,gkhe->gqhe', shares, values4, precision=highest)
    return mixture.reshape(groups, length, HEADS * HEAD_DIM)

def forward(decoder_in, memory, params, target_ids, source_ids):
    qkv_self, bias_self, out_self, norm_self, query_cross, pair_cross, bias_cross, out_cross, norm_cross, ffn_in, ffn_in_bias, ffn_out, ffn_out_bias, ffn_norm = params
    places = jnp.arange(SLOTS, dtype=jnp.int32)
    causal = places[None, :] <= places[:, None]
    self_allowed = (target_ids[:, :, None] == target_ids[:, None, :]) & causal[None]
    cross_allowed = target_ids[:, :, None] == source_ids[:, None, :]
    query_one = low(low_back(project(decoder_in, qkv_self[0]) + bias_self[0]))
    keys_one = low(low_back(project(decoder_in, qkv_self[1])))
    values_one = low(low_back(project(decoder_in, qkv_self[2]) + bias_self[1]))
    mixture_one = low(low_back(attend(query_one, keys_one, values_one, self_allowed)))
    branch_one = low_back(project(mixture_one, out_self) + bias_self[2])
    hidden_one = layer_norm(decoder_in + branch_one, norm_self)
    query_two = low(low_back(project(low(hidden_one), query_cross) + bias_cross[0]))
    keys_two = low(low_back(project(memory, pair_cross[0])))
    values_two = low(low_back(project(memory, pair_cross[1]) + bias_cross[1]))
    mixture_two = low(low_back(attend(query_two, keys_two, values_two, cross_allowed)))
    branch_two = low_back(project(mixture_two, out_cross) + bias_cross[2])
    hidden_two = layer_norm(hidden_one + branch_two, norm_cross)
    expanded = low_back(project(low(hidden_two), ffn_in) + ffn_in_bias)
    activated = low(jax.nn.gelu(expanded, approximate=True))
    branch_three = low_back(project(activated, ffn_out) + ffn_out_bias)
    return layer_norm(hidden_two + branch_three, ffn_norm)

def reference(decoder_in, memory, out_grad, tgt_len, src_len, self_qkv, self_bias, self_out, self_norm, cross_q, cross_kv, cross_bias, cross_out, cross_norm, ffn_in, ffn_in_bias, ffn_out, ffn_out_bias, ffn_norm):
    params = tuple((part.astype(jnp.float32) for part in (self_qkv, self_bias, self_out, self_norm, cross_q, cross_kv, cross_bias, cross_out, cross_norm, ffn_in, ffn_in_bias, ffn_out, ffn_out_bias, ffn_norm)))
    group_rows = 16

    def regroup(array):
        return array.reshape((ROWS // group_rows, group_rows) + array.shape[1:])

    def one_group(totals, item):
        inputs_group, memory_group, grad_group, target_group, source_group = item
        target_ids = segment_ids(target_group)
        source_ids = segment_ids(source_group)

        def apply(first, second, weights):
            return forward(first, second, weights, target_ids, source_ids)
        result, pullback = jax.vjp(apply, inputs_group.astype(jnp.float32), memory_group.astype(jnp.float32), params)
        grad_inputs, grad_memory, grad_params = pullback(grad_group.astype(jnp.float32))
        totals = jax.tree.map(jnp.add, totals, grad_params)
        return (totals, (result.astype(jnp.bfloat16), grad_inputs.astype(jnp.bfloat16), grad_memory.astype(jnp.bfloat16)))
    initial = jax.tree.map(jnp.zeros_like, params)
    totals, (results, grad_inputs, grad_memory) = lax.scan(one_group, initial, (regroup(decoder_in), regroup(memory), regroup(out_grad), regroup(tgt_len), regroup(src_len)))
    return (results.reshape(decoder_in.shape), grad_inputs.reshape(decoder_in.shape), grad_memory.reshape(memory.shape), totals[0], totals[1], totals[2], totals[3], totals[4], totals[5], totals[6], totals[7], totals[8], totals[9], totals[10], totals[11], totals[12], totals[13])
```

```python
import functools

import jax
import jax.numpy as jnp
from jax import lax
from jax.experimental import pallas as pl
from jax.experimental.pallas import tpu as pltpu
from jax.sharding import PartitionSpec as P

F32 = jnp.float32
BF16 = jnp.bfloat16
EPS = 1e-05
MASKED = -1e30
HEADS = 8
HEAD_DIM = 64
PAIR = 128
QUAD = 256
GELU_A = 0.7978845608028654
GELU_B = 0.044715


def mm(left, right, left_dim, right_dim):
    return lax.dot_general(
        left, right, (((left_dim,), (right_dim,)), ((), ())), preferred_element_type=F32
    )


def mm_nt(left, right):
    return mm(left, right, 1, 1)


def mm_nn(left, right):
    return mm(left, right, 1, 0)


def mm_tn(left, right):
    return mm(left, right, 0, 0)


def norm_stats(summed):
    centred = summed - jnp.mean(summed, axis=-1, keepdims=True)
    inverse = lax.rsqrt(jnp.mean(centred * centred, axis=-1, keepdims=True) + EPS)
    return centred * inverse, inverse


def norm_back(upstream, normed, inverse, gain):
    scaled = upstream * gain
    mean_scaled = jnp.mean(scaled, axis=-1, keepdims=True)
    mean_product = jnp.mean(scaled * normed, axis=-1, keepdims=True)
    return (scaled - mean_scaled - normed * mean_product) * inverse


def column_sum(values):
    return jnp.sum(values.astype(F32), axis=0, keepdims=True)


def lane_band(width, head):
    lane = lax.broadcasted_iota(jnp.int32, (1, width), 1)
    return (lane >= head * HEAD_DIM) & (lane < (head + 1) * HEAD_DIM)


def keep_head(values, head):
    return jnp.where(lane_band(values.shape[1], head), values, jnp.zeros_like(values))


def mask_bias(key_ids, query_ids, causal):
    slots = key_ids.shape[1]
    down = jnp.transpose(jnp.broadcast_to(key_ids, (slots, slots)))
    allowed = down == query_ids
    if causal:
        key_at = lax.broadcasted_iota(jnp.int32, (slots, slots), 0)
        query_at = lax.broadcasted_iota(jnp.int32, (slots, slots), 1)
        allowed = allowed & (key_at <= query_at)
    return jnp.where(allowed, 0.0, MASKED).astype(F32)


def attend_rows(query_ref, keys_ref, values_ref, bias_ref, shares_ref, mixture_ref, row, at):
    for quad in range(HEADS * HEAD_DIM // QUAD):
        lanes = slice(quad * QUAD, (quad + 1) * QUAD)
        values_quad = values_ref[at, lanes]
        parts, wide = [], []
        for inner in range(QUAD // HEAD_DIM):
            head = quad * (QUAD // HEAD_DIM) + inner
            first = head * HEAD_DIM // PAIR * PAIR
            pair = slice(first, first + PAIR)
            keys_head = keep_head(keys_ref[at, pair], head - first // HEAD_DIM)
            scores = mm_nt(keys_head, query_ref[at, pair]) + bias_ref[...]
            top = jnp.max(scores, axis=0, keepdims=True)
            raised = jnp.exp(scores - top)
            total = jnp.sum(raised, axis=0, keepdims=True)
            shares = (raised * (1.0 / total)).astype(BF16)
            shares_ref[row * HEADS + head] = shares
            parts.append(shares)
            wide.append(keep_head(values_quad, inner))
        mixture = mm_tn(jnp.concatenate(parts, 0), jnp.concatenate(wide, 0))
        mixture_ref[at, lanes] = mixture.astype(BF16)


def attend_rows_back(
    upstream_ref, query_ref, keys_ref, values_ref, shares_ref, gq_ref, gk_ref, gv_ref, row, at
):
    for quad in range(HEADS * HEAD_DIM // QUAD):
        lanes = slice(quad * QUAD, (quad + 1) * QUAD)
        query_quad = query_ref[at, lanes]
        keys_quad = keys_ref[at, lanes]
        up_quad = upstream_ref[at, lanes]
        grad_query = grad_keys = grad_values = None
        for inner in range(QUAD // HEAD_DIM):
            head = quad * (QUAD // HEAD_DIM) + inner
            first = head * HEAD_DIM // PAIR * PAIR
            pair = slice(first, first + PAIR)
            values_head = keep_head(values_ref[at, pair], head - first // HEAD_DIM)
            shares = shares_ref[row * HEADS + head]
            grad_shares = mm_nt(values_head, upstream_ref[at, pair])
            wide = shares.astype(F32)
            product = wide * grad_shares
            centre = jnp.sum(product, axis=0, keepdims=True)
            grad_scores = (product - wide * centre).astype(BF16)
            one = mm_nn(grad_scores, keep_head(query_quad, inner))
            two = mm_nn(shares, keep_head(up_quad, inner))
            three = mm_tn(grad_scores, keep_head(keys_quad, inner))
            grad_keys = one if grad_keys is None else grad_keys + one
            grad_values = two if grad_values is None else grad_values + two
            grad_query = three if grad_query is None else grad_query + three
        gq_ref[at, lanes] = (grad_query * HEAD_DIM**-0.5).astype(BF16)
        gk_ref[at, lanes] = grad_keys.astype(BF16)
        gv_ref[at, lanes] = grad_values.astype(BF16)


STEP_ROWS = 2

SELF_BQ, SELF_BV, SELF_BO, SELF_G, SELF_S = 0, 1, 2, 3, 4
CROSS_BQ, CROSS_BV, CROSS_BO, CROSS_G, CROSS_S = 5, 6, 7, 8, 9
FFN_BO, FFN_G, FFN_S, FFN_BI = 10, 11, 12, 13
TABLE = 24


def vrow(table_ref, index):
    return table_ref[index : index + 1, :]


def add_row(ref, index, values):
    ref[index : index + 1, :] += values


def self_forward_kernel(
    source_ref, ids_ref, weight_ref, table_ref,
    query_ref, keys_ref, values_ref, shares_ref, mixture_ref, summed_ref, bias_ref,
):
    slots = ids_ref.shape[2]
    source = source_ref[...]
    query = mm_nt(source, weight_ref[0]) + vrow(table_ref, SELF_BQ)
    query_ref[...] = (query * HEAD_DIM**-0.5).astype(BF16)
    keys_ref[...] = mm_nt(source, weight_ref[1]).astype(BF16)
    values_ref[...] = (mm_nt(source, weight_ref[2]) + vrow(table_ref, SELF_BV)).astype(BF16)

    def one_row(row, carry):
        at = pl.ds(pl.multiple_of(row * slots, slots), slots)
        ids = ids_ref[row]
        bias_ref[...] = mask_bias(ids[0:1], ids[0:1], True)
        attend_rows(query_ref, keys_ref, values_ref, bias_ref, shares_ref, mixture_ref, row, at)
        return carry

    lax.fori_loop(0, STEP_ROWS, one_row, 0)
    summed_ref[...] = (
        source.astype(F32) + mm_nt(mixture_ref[...], weight_ref[3]) + vrow(table_ref, SELF_BO)
    )


def middle_kernel(
    summed_one_ref, remote_ref, upstream_ref, ids_ref, weight_ref, win_ref, wout_ref, table_ref,
    result_ref, grad_remote_ref, sum_one_ref, dweight_ref, dwin_ref, dwout_ref, dtable_ref,
    low_ref, query_ref, keys_ref, values_ref, shares_ref, mixture_ref, bias_ref,
    normed_one_ref, normed_two_ref, hidden_ref, active_ref, slope_ref, accum_ref,
    gq_ref, gk_ref, gv_ref, low_two_ref, grad_low_ref, acc_ref, accin_ref, accout_ref, acct_ref,
):
    step = pl.program_id(0)
    slots = ids_ref.shape[2]
    chunks = win_ref.shape[0] // 512

    @pl.when(step == 0)
    def _():
        acc_ref[...] = jnp.zeros_like(acc_ref)
        accin_ref[...] = jnp.zeros_like(accin_ref)
        accout_ref[...] = jnp.zeros_like(accout_ref)
        acct_ref[...] = jnp.zeros_like(acct_ref)

    normed_one, inverse_one = norm_stats(summed_one_ref[...])
    normed_one_ref[...] = normed_one
    hidden_one = normed_one * vrow(table_ref, SELF_G) + vrow(table_ref, SELF_S)
    low_ref[...] = hidden_one.astype(BF16)
    query = mm_nt(low_ref[...], weight_ref[0]) + vrow(table_ref, CROSS_BQ)
    query_ref[...] = (query * HEAD_DIM**-0.5).astype(BF16)
    remote = remote_ref[...]
    keys_ref[...] = mm_nt(remote, weight_ref[1]).astype(BF16)
    values_ref[...] = (mm_nt(remote, weight_ref[2]) + vrow(table_ref, CROSS_BV)).astype(BF16)

    def one_row(row, carry):
        at = pl.ds(pl.multiple_of(row * slots, slots), slots)
        ids = ids_ref[row]
        bias_ref[...] = mask_bias(ids[1:2], ids[0:1], False)
        attend_rows(query_ref, keys_ref, values_ref, bias_ref, shares_ref, mixture_ref, row, at)
        return carry

    lax.fori_loop(0, STEP_ROWS, one_row, 0)
    hidden_one = normed_one_ref[...] * vrow(table_ref, SELF_G) + vrow(table_ref, SELF_S)
    summed_two = hidden_one + mm_nt(mixture_ref[...], weight_ref[3]) + vrow(table_ref, CROSS_BO)
    normed_two, inverse_two = norm_stats(summed_two)
    normed_two_ref[...] = normed_two
    hidden_two = normed_two * vrow(table_ref, CROSS_G) + vrow(table_ref, CROSS_S)
    hidden_ref[...] = hidden_two
    low_two_ref[...] = hidden_two.astype(BF16)

    accum_ref[...] = jnp.zeros_like(accum_ref)

    def ffn_chunk(chunk, carry):
        units = pl.ds(pl.multiple_of(chunk * 512, 512), 512)
        expanded = mm_nt(low_two_ref[...], win_ref[units, :]) + table_ref[pl.ds(FFN_BI + chunk, 1), :]
        square = expanded * expanded
        inner = expanded * (GELU_A + (GELU_A * GELU_B) * square)
        bent = jnp.tanh(inner)
        half = 0.5 * bent + 0.5
        active_ref[:, units] = (expanded * half).astype(BF16)
        slope = half + (0.5 * expanded) * (1.0 - bent * bent) * (
            GELU_A + (3.0 * GELU_A * GELU_B) * square
        )
        slope_ref[:, units] = slope.astype(BF16)
        accum_ref[...] += mm_nt(active_ref[:, units], wout_ref[:, units])
        return carry

    lax.fori_loop(0, chunks, ffn_chunk, 0)
    normed_three, inverse_three = norm_stats(
        hidden_ref[...] + accum_ref[...] + vrow(table_ref, FFN_BO)
    )
    result = normed_three * vrow(table_ref, FFN_G) + vrow(table_ref, FFN_S)
    result_ref[...] = result.astype(BF16)

    upstream = upstream_ref[...].astype(F32)
    add_row(acct_ref, FFN_G, column_sum(upstream * normed_three))
    add_row(acct_ref, FFN_S, column_sum(upstream))
    sum_three = norm_back(upstream, normed_three, inverse_three, vrow(table_ref, FFN_G))
    grad_low_ref[...] = sum_three.astype(BF16)
    add_row(acct_ref, FFN_BO, column_sum(grad_low_ref[...]))
    accum_ref[...] = sum_three

    def ffn_chunk_back(chunk, carry):
        units = pl.ds(pl.multiple_of(chunk * 512, 512), 512)
        grad_three = grad_low_ref[...]
        accout_ref[:, units] += mm_tn(grad_three, active_ref[:, units])
        grad_active = mm_nn(grad_three, wout_ref[:, units])
        grad_expanded = (grad_active * slope_ref[:, units].astype(F32)).astype(BF16)
        acct_ref[pl.ds(FFN_BI + chunk, 1), :] += column_sum(grad_expanded)
        accin_ref[units, :] += mm_tn(grad_expanded, low_two_ref[...])
        accum_ref[...] += mm_nn(grad_expanded, win_ref[units, :])
        return carry

    lax.fori_loop(0, chunks, ffn_chunk_back, 0)

    grad_hidden_two = accum_ref[...]
    normed_two = normed_two_ref[...]
    add_row(acct_ref, CROSS_G, column_sum(grad_hidden_two * normed_two))
    add_row(acct_ref, CROSS_S, column_sum(grad_hidden_two))
    sum_two = norm_back(grad_hidden_two, normed_two, inverse_two, vrow(table_ref, CROSS_G))
    accum_ref[...] = sum_two
    grad_low_ref[...] = sum_two.astype(BF16)
    grad_two = grad_low_ref[...]
    add_row(acct_ref, CROSS_BO, column_sum(grad_two))
    acc_ref[3] += mm_tn(grad_two, mixture_ref[...])
    mixture_ref[...] = mm_nn(grad_two, weight_ref[3]).astype(BF16)

    def one_row_back(row, carry):
        at = pl.ds(pl.multiple_of(row * slots, slots), slots)
        attend_rows_back(
            mixture_ref, query_ref, keys_ref, values_ref, shares_ref, gq_ref, gk_ref, gv_ref, row, at
        )
        return carry

    lax.fori_loop(0, STEP_ROWS, one_row_back, 0)
    grad_query, grad_keys, grad_values = gq_ref[...], gk_ref[...], gv_ref[...]
    add_row(acct_ref, CROSS_BQ, column_sum(grad_query))
    add_row(acct_ref, CROSS_BV, column_sum(grad_values))
    acc_ref[0] += mm_tn(grad_query, low_ref[...])
    acc_ref[1] += mm_tn(grad_keys, remote_ref[...])
    acc_ref[2] += mm_tn(grad_values, remote_ref[...])
    grad_remote_ref[...] = (
        mm_nn(grad_keys, weight_ref[1]) + mm_nn(grad_values, weight_ref[2])
    ).astype(BF16)

    grad_hidden_one = accum_ref[...] + mm_nn(grad_query, weight_ref[0])
    normed_one = normed_one_ref[...]
    add_row(acct_ref, SELF_G, column_sum(grad_hidden_one * normed_one))
    add_row(acct_ref, SELF_S, column_sum(grad_hidden_one))
    sum_one_ref[...] = norm_back(grad_hidden_one, normed_one, inverse_one, vrow(table_ref, SELF_G))

    @pl.when(step == pl.num_programs(0) - 1)
    def _():
        dweight_ref[...] = acc_ref[...].astype(BF16)
        dwin_ref[...] = accin_ref[...].astype(BF16)
        dwout_ref[...] = accout_ref[...].astype(BF16)
        dtable_ref[...] = acct_ref[...]


def self_backward_kernel(
    sum_one_ref, source_ref, mixture_ref, query_ref, keys_ref, values_ref, shares_ref, weight_ref,
    grad_source_ref, dweight_ref, dtable_ref,
    up_ref, gq_ref, gk_ref, gv_ref, acc_ref, acct_ref,
):
    step = pl.program_id(0)
    slots = shares_ref.shape[1]

    @pl.when(step == 0)
    def _():
        acc_ref[...] = jnp.zeros_like(acc_ref)
        acct_ref[...] = jnp.zeros_like(acct_ref)

    grad_one = sum_one_ref[...].astype(BF16)
    add_row(acct_ref, SELF_BO, column_sum(grad_one))
    acc_ref[3] += mm_tn(grad_one, mixture_ref[...])
    up_ref[...] = mm_nn(grad_one, weight_ref[3]).astype(BF16)

    def one_row_back(row, carry):
        at = pl.ds(pl.multiple_of(row * slots, slots), slots)
        attend_rows_back(
            up_ref, query_ref, keys_ref, values_ref, shares_ref, gq_ref, gk_ref, gv_ref, row, at
        )
        return carry

    lax.fori_loop(0, STEP_ROWS, one_row_back, 0)
    grad_query, grad_keys, grad_values = gq_ref[...], gk_ref[...], gv_ref[...]
    add_row(acct_ref, SELF_BQ, column_sum(grad_query))
    add_row(acct_ref, SELF_BV, column_sum(grad_values))
    source = source_ref[...]
    acc_ref[0] += mm_tn(grad_query, source)
    acc_ref[1] += mm_tn(grad_keys, source)
    acc_ref[2] += mm_tn(grad_values, source)
    grad_source_ref[...] = (
        sum_one_ref[...]
        + mm_nn(grad_query, weight_ref[0])
        + mm_nn(grad_keys, weight_ref[1])
        + mm_nn(grad_values, weight_ref[2])
    ).astype(BF16)

    @pl.when(step == pl.num_programs(0) - 1)
    def _():
        dweight_ref[...] = acc_ref[...].astype(BF16)
        dtable_ref[...] = acct_ref[...]


def whole(shape):
    return pl.BlockSpec(shape, lambda i: (0,) * len(shape), pipeline_mode=pl.Buffered(1))


def tokens_spec(block, width):
    return pl.BlockSpec((block, width), lambda i: (i, 0))


def params(limit):
    return pltpu.CompilerParams(vmem_limit_bytes=limit, dimension_semantics=("arbitrary",))


def layer(decoder_in, memory, out_grad, ids, weight_self, weight_cross, win, wout, table):
    rows, slots, width = decoder_in.shape
    hidden = win.shape[0]
    tokens = rows * slots
    block = STEP_ROWS * slots
    steps = rows // STEP_ROWS
    shares_block = (STEP_ROWS * HEADS, slots, slots)
    source = decoder_in.reshape(tokens, width)
    shape = jax.ShapeDtypeStruct
    low = shape((tokens, width), BF16)
    full = shape((tokens, width), F32)
    tok = tokens_spec(block, width)
    ids_spec = pl.BlockSpec((STEP_ROWS, 2, slots), lambda i: (i, 0, 0))
    shares_spec = pl.BlockSpec(shares_block, lambda i: (i, 0, 0))
    query, keys, values, shares, mixture, summed = pl.pallas_call(
        self_forward_kernel,
        grid=(steps,),
        in_specs=[tok, ids_spec, whole(weight_self.shape), whole(table.shape)],
        out_specs=[tok, tok, tok, shares_spec, tok, tok],
        out_shape=[low, low, low, shape((rows * HEADS, slots, slots), BF16), low, full],
        scratch_shapes=[pltpu.VMEM((slots, slots), F32)],
        compiler_params=params(56 << 20),
        name="self_forward",
    )(source, ids, weight_self, table)
    vm = pltpu.VMEM
    result, grad_remote, sum_one, dcross, dwin, dwout, dtable = pl.pallas_call(
        middle_kernel,
        grid=(steps,),
        in_specs=[tok, tok, tok, ids_spec, whole(weight_cross.shape), whole(win.shape), whole(wout.shape), whole(table.shape)],
        out_specs=[tok, tok, tok, whole(weight_cross.shape), whole(win.shape), whole(wout.shape), whole(table.shape)],
        out_shape=[low, low, full, shape(weight_cross.shape, BF16), shape(win.shape, BF16), shape(wout.shape, BF16), shape(table.shape, F32)],
        scratch_shapes=[
            vm((block, width), BF16), vm((block, width), BF16), vm((block, width), BF16), vm((block, width), BF16),
            vm(shares_block, BF16), vm((block, width), BF16), vm((slots, slots), F32),
            vm((block, width), F32), vm((block, width), F32), vm((block, width), F32),
            vm((block, hidden), BF16), vm((block, hidden), BF16), vm((block, width), F32),
            vm((block, width), BF16), vm((block, width), BF16), vm((block, width), BF16),
            vm((block, width), BF16), vm((block, width), BF16),
            vm(weight_cross.shape, F32), vm(win.shape, F32), vm(wout.shape, F32), vm(table.shape, F32),
        ],
        compiler_params=params(63 << 20),
        name="middle",
    )(summed, memory.reshape(tokens, width), out_grad.reshape(tokens, width), ids, weight_cross, win, wout, table)
    grad_source, dself, dtable_self = pl.pallas_call(
        self_backward_kernel,
        grid=(steps,),
        in_specs=[tok, tok, tok, tok, tok, tok, shares_spec, whole(weight_self.shape)],
        out_specs=[tok, whole(weight_self.shape), whole(table.shape)],
        out_shape=[low, shape(weight_self.shape, BF16), shape(table.shape, F32)],
        scratch_shapes=[
            vm((block, width), BF16), vm((block, width), BF16), vm((block, width), BF16), vm((block, width), BF16),
            vm(weight_self.shape, F32), vm(table.shape, F32),
        ],
        compiler_params=params(56 << 20),
        name="self_backward",
    )(sum_one, source, mixture, query, keys, values, shares, weight_self)
    as_rows = lambda array: array.reshape(rows, slots, width)
    return as_rows(result), as_rows(grad_source), as_rows(grad_remote), dself, dcross, dwin, dwout, dtable + dtable_self


def segment_ids(lengths, slot_count):
    places = jnp.arange(slot_count, dtype=jnp.int32)
    finish = jnp.cumsum(lengths, axis=-1)
    return jnp.sum((finish[:, None, :] <= places[None, :, None]).astype(jnp.int32), axis=-1)


def turn(array):
    return jnp.swapaxes(array, -1, -2)


AXES = ("dp", "fsdp")


def gather_plain(parts, count):
    (self_qkv, self_bias, self_out, self_norm, cross_q, cross_kv, cross_bias, cross_out, cross_norm,
     ffn_in, ffn_in_bias, ffn_out, ffn_out_bias, ffn_norm) = parts
    cols = self_out.shape[1]
    width = self_out.shape[0]
    chunks = ffn_out.shape[0] // width
    small = jnp.concatenate(
        [self_bias, self_norm, cross_bias, cross_norm, ffn_out_bias[None], ffn_norm,
         ffn_in_bias.reshape(chunks, cols)], axis=0)
    small = jnp.pad(turn(small), ((0, 0), (0, width - small.shape[0])))
    packed = jnp.concatenate([
        turn(self_qkv).reshape(-1, width), turn(self_out), turn(cross_q),
        turn(cross_kv).reshape(-1, width), turn(cross_out), turn(ffn_in),
        turn(ffn_out).reshape(cols, chunks, width).swapaxes(0, 1).reshape(-1, width), small], axis=0)
    whole_set = lax.all_gather(packed, AXES, axis=0, tiled=False)
    square = whole_set[:, : 8 * cols].reshape(count, 8, cols, width).swapaxes(0, 1)
    square = square.reshape(8, width, width)
    low = 8 * cols
    win = whole_set[:, low : low + chunks * cols].reshape(chunks * width, width)
    low += chunks * cols
    wout = whole_set[:, low : low + chunks * cols].reshape(count, chunks, cols, width)
    wout = wout.transpose(0, 2, 1, 3).reshape(width, chunks * width)
    low += chunks * cols
    table = whole_set[:, low:]
    first = table[:, :, :13].transpose(2, 0, 1).reshape(13, width)
    second = table[:, :, 13 : 13 + chunks].transpose(0, 2, 1).reshape(chunks, width)
    table = jnp.concatenate([first, second], axis=0).astype(F32)
    table = jnp.pad(table, ((0, TABLE - table.shape[0]), (0, 0)))
    return square[:4], square[4:], win, wout, table


def scatter_plain(dself, dcross, dwin, dwout, dtable, count):
    width = dself.shape[1]
    cols = width // count
    chunks = dwin.shape[0] // width
    squares = jnp.concatenate([dself, dcross], axis=0).reshape(8, count, cols, width).swapaxes(0, 1)
    first = dtable[:13].reshape(13, count, cols).transpose(1, 2, 0)
    second = dtable[13 : 13 + chunks].reshape(count, chunks, cols).transpose(0, 2, 1)
    small = jnp.concatenate([first, second], axis=2)
    small = jnp.pad(small, ((0, 0), (0, 0), (0, width - small.shape[2]))).astype(BF16)
    packed = jnp.concatenate([
        squares.reshape(count, 8 * cols, width), dwin.reshape(count, chunks * cols, width),
        dwout.reshape(count, cols, chunks, width).swapaxes(1, 2).reshape(count, -1, width), small],
        axis=1)
    mine = lax.psum_scatter(packed, AXES, scatter_dimension=0, tiled=False).astype(F32)
    square = turn(mine[: 8 * cols].reshape(8, cols, width))
    low = 8 * cols
    ffn_in = turn(mine[low : low + chunks * cols])
    low += chunks * cols
    ffn_out = mine[low : low + chunks * cols].reshape(chunks, cols, width).swapaxes(0, 1)
    ffn_out = turn(ffn_out.reshape(cols, chunks * width))
    low += chunks * cols
    small = turn(mine[low:, : 13 + chunks])
    return (square[:3], small[0:3], square[3], small[3:5], square[4], square[5:7], small[5:8], square[7],
            small[8:10], ffn_in, small[13:].reshape(-1), ffn_out, small[10], small[11:13])


def on_device(count, decoder_in, memory, out_grad, tgt_len, src_len, *parts):
    slots = decoder_in.shape[1]
    ids = jnp.stack([segment_ids(tgt_len, slots), segment_ids(src_len, slots)], axis=1).astype(F32)
    weights = gather_plain(parts, count)
    result, grad_source, grad_remote, *grads = layer(decoder_in, memory, out_grad, ids, *weights)
    return (result, grad_source, grad_remote, *scatter_plain(*grads, count))


def solution(mesh):
    count = mesh.shape["dp"] * mesh.shape["fsdp"]
    rows = P(AXES, None, None)
    lens = P(AXES, None)
    cube = P(None, None, AXES)
    flat = P(None, AXES)
    line = P(AXES)
    params_in = (cube, flat, flat, flat, flat, cube, flat, flat, flat, flat, line, flat, line, flat)
    return jax.shard_map(
        functools.partial(on_device, count),
        mesh=mesh,
        in_specs=(rows, rows, rows, lens, lens) + params_in,
        out_specs=(rows, rows, rows) + params_in,
        check_vma=False,
    )
```

```python
import functools

import jax
import jax.numpy as jnp
from jax import lax
from jax.experimental import pallas as pl
from jax.experimental.pallas import tpu as pltpu
from jax.sharding import PartitionSpec as P

F32 = jnp.float32
BF16 = jnp.bfloat16
EPS = 1e-05
MASKED = -1e30
HEADS = 8
HEAD_DIM = 64
PAIR = 128
QUAD = 256
GELU_A = 0.7978845608028654
GELU_B = 0.044715


def mm(left, right, left_dim, right_dim):
    return lax.dot_general(
        left, right, (((left_dim,), (right_dim,)), ((), ())), preferred_element_type=F32
    )


def mm_nt(left, right):
    return mm(left, right, 1, 1)


def mm_nn(left, right):
    return mm(left, right, 1, 0)


def mm_tn(left, right):
    return mm(left, right, 0, 0)


def norm_stats(summed):
    centred = summed - jnp.mean(summed, axis=-1, keepdims=True)
    inverse = lax.rsqrt(jnp.mean(centred * centred, axis=-1, keepdims=True) + EPS)
    return centred * inverse, inverse


def norm_back(upstream, normed, inverse, gain):
    scaled = upstream * gain
    mean_scaled = jnp.mean(scaled, axis=-1, keepdims=True)
    mean_product = jnp.mean(scaled * normed, axis=-1, keepdims=True)
    return (scaled - mean_scaled - normed * mean_product) * inverse


def column_sum(values):
    return jnp.sum(values.astype(F32), axis=0, keepdims=True)


def lane_band(width, head):
    lane = lax.broadcasted_iota(jnp.int32, (1, width), 1)
    return (lane >= head * HEAD_DIM) & (lane < (head + 1) * HEAD_DIM)


def keep_head(values, head):
    return jnp.where(lane_band(values.shape[1], head), values, jnp.zeros_like(values))


def mask_bias(key_ids, query_ids, causal):
    slots = key_ids.shape[1]
    down = jnp.transpose(jnp.broadcast_to(key_ids, (slots, slots)))
    allowed = down == query_ids
    if causal:
        key_at = lax.broadcasted_iota(jnp.int32, (slots, slots), 0)
        query_at = lax.broadcasted_iota(jnp.int32, (slots, slots), 1)
        allowed = allowed & (key_at <= query_at)
    return jnp.where(allowed, 0.0, MASKED).astype(F32)


def attend_rows(query_ref, keys_ref, values_ref, bias_ref, shares_ref, mixture_ref, row, at):
    for quad in range(HEADS * HEAD_DIM // QUAD):
        lanes = slice(quad * QUAD, (quad + 1) * QUAD)
        values_quad = values_ref[at, lanes]
        parts, wide = [], []
        for inner in range(QUAD // HEAD_DIM):
            head = quad * (QUAD // HEAD_DIM) + inner
            first = head * HEAD_DIM // PAIR * PAIR
            pair = slice(first, first + PAIR)
            keys_head = keep_head(keys_ref[at, pair], head - first // HEAD_DIM)
            scores = mm_nt(keys_head, query_ref[at, pair]) + bias_ref[...]
            top = jnp.max(scores, axis=0, keepdims=True)
            raised = jnp.exp(scores - top)
            total = jnp.sum(raised, axis=0, keepdims=True)
            shares = (raised * (1.0 / total)).astype(BF16)
            shares_ref[row * HEADS + head] = shares
            parts.append(shares)
            wide.append(keep_head(values_quad, inner))
        mixture = mm_tn(jnp.concatenate(parts, 0), jnp.concatenate(wide, 0))
        mixture_ref[at, lanes] = mixture.astype(BF16)


def attend_rows_back(
    upstream_ref, query_ref, keys_ref, values_ref, shares_ref, gq_ref, gk_ref, gv_ref, row, at
):
    for quad in range(HEADS * HEAD_DIM // QUAD):
        lanes = slice(quad * QUAD, (quad + 1) * QUAD)
        query_quad = query_ref[at, lanes]
        keys_quad = keys_ref[at, lanes]
        up_quad = upstream_ref[at, lanes]
        grad_query = grad_keys = grad_values = None
        for inner in range(QUAD // HEAD_DIM):
            head = quad * (QUAD // HEAD_DIM) + inner
            first = head * HEAD_DIM // PAIR * PAIR
            pair = slice(first, first + PAIR)
            values_head = keep_head(values_ref[at, pair], head - first // HEAD_DIM)
            shares = shares_ref[row * HEADS + head]
            grad_shares = mm_nt(values_head, upstream_ref[at, pair])
            wide = shares.astype(F32)
            product = wide * grad_shares
            centre = jnp.sum(product, axis=0, keepdims=True)
            grad_scores = (product - wide * centre).astype(BF16)
            one = mm_nn(grad_scores, keep_head(query_quad, inner))
            two = mm_nn(shares, keep_head(up_quad, inner))
            three = mm_tn(grad_scores, keep_head(keys_quad, inner))
            grad_keys = one if grad_keys is None else grad_keys + one
            grad_values = two if grad_values is None else grad_values + two
            grad_query = three if grad_query is None else grad_query + three
        gq_ref[at, lanes] = (grad_query * HEAD_DIM**-0.5).astype(BF16)
        gk_ref[at, lanes] = grad_keys.astype(BF16)
        gv_ref[at, lanes] = grad_values.astype(BF16)


STEP_ROWS = 2

SELF_BQ, SELF_BV, SELF_BO, SELF_G, SELF_S = 0, 1, 2, 3, 4
CROSS_BQ, CROSS_BV, CROSS_BO, CROSS_G, CROSS_S = 5, 6, 7, 8, 9
FFN_BO, FFN_G, FFN_S, FFN_BI = 10, 11, 12, 13
TABLE = 24


def vrow(table_ref, index):
    return table_ref[index : index + 1, :]


def add_row(ref, index, values):
    ref[index : index + 1, :] += values


MESH = pl.DeviceIdType.MESH
ALL = slice(None)


def place():
    z = lax.axis_index("dp")
    f = lax.axis_index("fsdp")
    return z, f // 4, (f // 2) % 2, f % 2


def device(z, y, x, core):
    return (z, y * 4 + x * 2 + core)


def greet():
    z, y, x, core = place()
    partners = [device(lax.rem(z + step, 4), y, x, core) for step in (1, 2, 3)]
    partners += [device(z, y, 1 - x, core), device(z, 1 - y, x, core), device(z, y, x, 1 - core)]
    barrier = pltpu.get_barrier_semaphore()
    for partner in partners:
        pl.semaphore_signal(barrier, inc=1, device_id=partner, device_id_type=MESH)
    pl.semaphore_wait(barrier, len(partners))


class Gather:
    def __init__(self, ref, own, first, second, sems, base):
        self.ref, self.own, self.first, self.second = ref, own, first, second
        self.local, self.send, self.recv = sems
        self.base = base
        self.mats = slice(min(m.start for _, m in own), max(m.stop for _, m in own))

    @staticmethod
    def slots(own):
        return 3 * len(own) + 5

    def copy(self, slot, source, target, partner):
        at = self.base + slot
        return pltpu.make_async_remote_copy(
            src_ref=source, dst_ref=target, send_sem=self.send.at[at], recv_sem=self.recv.at[at],
            device_id=partner, device_id_type=MESH)

    def at(self, half, z, y, x, core):
        mats, rows, lanes = half
        return self.ref.at[mats, z, y, x, core, rows, lanes]

    def locals(self):
        z, y, x, core = place()
        return [
            pltpu.make_async_copy(source, self.ref.at[mats, z, y, x, core], self.local.at[self.base + i])
            for i, (source, mats) in enumerate(self.own)
        ]

    def hops(self, stage, incoming):
        z, y, x, core = place()
        full = (self.mats, ALL, ALL)
        found = []
        many = len(self.own)
        if stage == 0:
            for step in (1, 2, 3):
                other = lax.rem(z + (4 - step if incoming else step), 4)
                for i, (source, mats) in enumerate(self.own):
                    target = self.ref.at[mats, other if incoming else z, y, x, core]
                    found.append(self.copy((step - 1) * many + i, source, target, device(other, y, x, core)))
        if stage == 1:
            for slot, (py, px) in enumerate(((y, 1 - x), (1 - y, x))):
                sent = self.at(full, ALL, y, x, core)
                target = self.at(full, ALL, py, px, core) if incoming else sent
                found.append(self.copy(3 * many + slot, sent, target, device(z, py, px, core)))
        if stage == 2:
            for slot, (half, by, bx, py, px) in enumerate((
                (self.first, 1 - y, x, y, 1 - x), (self.second, y, 1 - x, 1 - y, x))):
                sent = self.at(half, ALL, by, bx, core)
                target = self.at(half, ALL, 1 - y, 1 - x, core) if incoming else sent
                found.append(self.copy(3 * many + 2 + slot, sent, target, device(z, py, px, core)))
        if stage == 3:
            sent = self.at(full, ALL, ALL, ALL, core)
            target = self.at(full, ALL, ALL, ALL, 1 - core) if incoming else sent
            found.append(self.copy(3 * many + 4, sent, target, device(z, y, x, 1 - core)))
        return found

    def start(self, stage):
        for hop in self.hops(stage, False):
            hop.start()

    def arrive(self, stage):
        for hop in self.hops(stage, True):
            hop.wait_recv()

    def finish(self):
        for stage in range(4):
            for hop in self.hops(stage, False):
                hop.wait_send()


def gather_pieces(shards, targets, sems):
    qkv, out_one, cross_q, cross_kv, out_two, win, wout, small = shards
    ws, wc, win_all, wout_all, small_all = targets
    one = lambda n: slice(n, n + 1)
    plans = [
        (ws, [(qkv.at[0:2], slice(0, 2))], (one(0), ALL, ALL), (one(1), ALL, ALL)),
        (ws, [(qkv.at[2:3], one(2)), (out_one, one(3))], (one(2), ALL, ALL), (one(3), ALL, ALL)),
        (small_all, [(small, one(0))], (ALL, ALL, slice(0, 128)), (ALL, ALL, slice(128, 256))),
        (wc, [(cross_q, one(0)), (cross_kv, slice(1, 3)), (out_two, one(3))],
         (slice(0, 2), ALL, ALL), (slice(2, 4), ALL, ALL)),
        (win_all, [(win, one(0))], (ALL, slice(0, 32), ALL), (ALL, slice(32, 64), ALL)),
        (wout_all, [(wout, one(0))], (ALL, ALL, slice(0, 1024)), (ALL, ALL, slice(1024, 2048))),
    ]
    pieces, base = [], 0
    for ref, own, first, second in plans:
        pieces.append(Gather(ref, own, first, second, sems, base))
        base += Gather.slots(own)
    return pieces


GATHER_SLOTS = 64

BLOCKS = (4, 2, 2, 2)


def square(ref, index):
    return ref[index].reshape(512, 512)


def prepare_ids(tgt_ref, src_ref, ids_ref):
    rows, sents = tgt_ref.shape
    slots = ids_ref.shape[2]
    before = lax.broadcasted_iota(jnp.int32, (sents, sents), 0)
    after = lax.broadcasted_iota(jnp.int32, (sents, sents), 1)
    ladder = (before <= after).astype(F32)
    slot = lax.broadcasted_iota(jnp.int32, (sents, slots), 1).astype(F32)
    for side, ref in enumerate((tgt_ref, src_ref)):
        lengths = ref[...].astype(F32)
        finish = lax.dot_general(
            ladder, lengths, (((0,), (1,)), ((), ())),
            precision=lax.Precision.HIGHEST, preferred_element_type=F32)
        for row in range(rows):
            ended = (finish[:, row : row + 1] <= slot).astype(F32)
            ids_ref[row, side : side + 1, :] = jnp.sum(ended, axis=0, keepdims=True)


def self_forward(
    step, source_ref, ids_ref, weight_ref, table_ref,
    query_ref, keys_ref, values_ref, shares_ref, mixture_ref, summed_ref, bias_ref,
):
    slots = ids_ref.shape[2]
    source = source_ref[...]
    query = mm_nt(source, square(weight_ref, 0)) + vrow(table_ref, SELF_BQ)
    query_ref[...] = (query * HEAD_DIM**-0.5).astype(BF16)
    keys_ref[...] = mm_nt(source, square(weight_ref, 1)).astype(BF16)
    values_ref[...] = (mm_nt(source, square(weight_ref, 2)) + vrow(table_ref, SELF_BV)).astype(BF16)

    def one_row(row, carry):
        at = pl.ds(pl.multiple_of(row * slots, slots), slots)
        ids = ids_ref[step * STEP_ROWS + row]
        bias_ref[...] = mask_bias(ids[0:1], ids[0:1], True)
        attend_rows(query_ref, keys_ref, values_ref, bias_ref, shares_ref, mixture_ref, row, at)
        return carry

    lax.fori_loop(0, STEP_ROWS, one_row, 0)
    summed_ref[...] = (
        source.astype(F32) + mm_nt(mixture_ref[...], square(weight_ref, 3)) + vrow(table_ref, SELF_BO)
    )


def cross_forward(
    step, summed_one_ref, remote_ref, ids_ref, weight_ref, table_ref,
    query_ref, keys_ref, values_ref, shares_ref, mixture_ref, summed_ref, bias_ref, hidden_ref,
):
    slots = ids_ref.shape[2]
    normed_one, _ = norm_stats(summed_one_ref[...])
    hidden_one = normed_one * vrow(table_ref, SELF_G) + vrow(table_ref, SELF_S)
    hidden_ref[...] = hidden_one
    query = mm_nt(hidden_one.astype(BF16), square(weight_ref, 0)) + vrow(table_ref, CROSS_BQ)
    query_ref[...] = (query * HEAD_DIM**-0.5).astype(BF16)
    remote = remote_ref[...]
    keys_ref[...] = mm_nt(remote, square(weight_ref, 1)).astype(BF16)
    values_ref[...] = (mm_nt(remote, square(weight_ref, 2)) + vrow(table_ref, CROSS_BV)).astype(BF16)

    def one_row(row, carry):
        at = pl.ds(pl.multiple_of(row * slots, slots), slots)
        ids = ids_ref[step * STEP_ROWS + row]
        bias_ref[...] = mask_bias(ids[1:2], ids[0:1], False)
        attend_rows(query_ref, keys_ref, values_ref, bias_ref, shares_ref, mixture_ref, row, at)
        return carry

    lax.fori_loop(0, STEP_ROWS, one_row, 0)
    summed_ref[...] = (
        hidden_ref[...] + mm_nt(mixture_ref[...], square(weight_ref, 3)) + vrow(table_ref, CROSS_BO)
    )


def table_from_columns(columns, table_ref):
    turned = jnp.transpose(columns[:, :128])
    table_ref[0:TABLE, :] = turned[0:TABLE]
    parts = [columns[:, 128 + k : 129 + k].reshape(32, 1, 16, 1) for k in range(4)]
    line = jnp.concatenate(parts, axis=1).reshape(2048, 1)
    line = jnp.transpose(jnp.broadcast_to(line, (2048, 128)))
    for k in range(4):
        table_ref[FFN_BI + k : FFN_BI + k + 1, :] = line[0:1, k * 512 : (k + 1) * 512]


def columns_from_table(rows):
    rows = jnp.concatenate([rows, jnp.zeros((128 - TABLE, 512), F32)], axis=0)
    columns = jnp.transpose(rows)
    lane = lax.broadcasted_iota(jnp.int32, (512, 128), 1)
    line = jnp.concatenate([columns[:, FFN_BI + k : FFN_BI + k + 1] for k in range(4)], axis=0)
    line = line.reshape(32, 4, 16, 1)
    second = jnp.zeros((512, 128), F32)
    for k in range(4):
        second = jnp.where(lane == k, line[:, k].reshape(512, 1), second)
    return jnp.concatenate([columns, second], axis=1)


FIRST_OUT = 12


def first_kernel(gathers, steps, *refs):
    step = pl.program_id(0)
    if gathers:
        (source_ref, remote_ref, tgt_ref, src_ref), shards, refs = refs[:4], refs[4:12], refs[12:]
    else:
        (source_ref, remote_ref, tgt_ref, src_ref, ws_ref, wc_ref, table_ref), refs = refs[:7], refs[7:]
    (q1_ref, k1_ref, v1_ref, p1_ref, m1_ref, s1_ref,
     q2_ref, k2_ref, v2_ref, p2_ref, m2_ref, s2_ref), refs = refs[:FIRST_OUT], refs[FIRST_OUT:]
    if gathers:
        (table_ref, ws_out, wc_out, win_out, wout_out), refs = refs[:5], refs[5:]
        (ws_ref, wc_ref, small_ref, *sems, out_sem), refs = refs[:7], refs[7:]
        pieces = gather_pieces(shards, (ws_ref, wc_ref, win_out, wout_out, small_ref), sems)
        one, two, small, cross, inner, outer = pieces
        saves = [pltpu.make_async_copy(ws_ref, ws_out, out_sem.at[0]), pltpu.make_async_copy(wc_ref, wc_out, out_sem.at[1])]
    bias_ref, hidden_ref, keep_ref, ids_ref = refs

    @pl.when(step == 0)
    def _():
        if gathers:
            greet()
            head = (one, two, small)
            for piece in pieces:
                for copy in piece.locals():
                    copy.start()
            for piece in head:
                piece.start(0)
        prepare_ids(tgt_ref, src_ref, ids_ref)
        if gathers:
            for piece in pieces:
                for copy in piece.locals():
                    copy.wait()
            for piece in head:
                piece.arrive(0)
                piece.start(1)
            cross.start(0)
            inner.start(0)
            for piece in head:
                piece.arrive(1)
                piece.start(2)
            cross.arrive(0)
            cross.start(1)
            for piece in head:
                piece.arrive(2)
                piece.start(3)
            for piece in head:
                piece.arrive(3)
            table_from_columns(small_ref[0].reshape(512, 256).astype(F32), table_ref)
            saves[0].start()

    @pl.when(step < steps)
    def _():
        self_forward(
            step, source_ref, ids_ref, ws_ref, table_ref,
            q1_ref, k1_ref, v1_ref, p1_ref, m1_ref, s1_ref, bias_ref)
        keep_ref[step] = s1_ref[...]

    @pl.when(step >= steps)
    def _():
        at = step - steps
        cross_forward(
            at, keep_ref.at[at], remote_ref, ids_ref, wc_ref, table_ref,
            q2_ref, k2_ref, v2_ref, p2_ref, m2_ref, s2_ref, bias_ref, hidden_ref)

    if gathers:
        @pl.when(step == 0)
        def _():
            cross.arrive(1)
            cross.start(2)
            inner.arrive(0)
            inner.start(1)
            outer.start(0)

        @pl.when(step == 1)
        def _():
            cross.arrive(2)
            cross.start(3)

        @pl.when(step == 2)
        def _():
            inner.arrive(1)
            inner.start(2)
            outer.arrive(0)
            outer.start(1)

        @pl.when(step == steps - 1)
        def _():
            cross.arrive(3)
            saves[1].start()

        @pl.when(step == steps)
        def _():
            inner.arrive(2)
            inner.start(3)
            outer.arrive(1)
            outer.start(2)

        @pl.when(step == 2 * steps - 2)
        def _():
            outer.arrive(2)
            outer.start(3)

        @pl.when(step == 2 * steps - 1)
        def _():
            inner.arrive(3)
            outer.arrive(3)
            for piece in pieces:
                piece.finish()
            for copy in saves:
                copy.wait()


def ffn_kernel(
    summed_two_ref, upstream_ref, win_ref, wout_ref, table_ref,
    result_ref, sum_two_ref, dwin_ref, dwout_ref, dtable_ref,
    normed_two_ref, hidden_ref, active_ref, slope_ref, accum_ref,
    low_two_ref, grad_low_ref, accin_ref, accout_ref, acct_ref,
):
    step = pl.program_id(0)
    chunks = win_ref.shape[0] // 512

    @pl.when(step == 0)
    def _():
        accin_ref[...] = jnp.zeros_like(accin_ref)
        accout_ref[...] = jnp.zeros_like(accout_ref)
        acct_ref[...] = jnp.zeros_like(acct_ref)

    normed_two, inverse_two = norm_stats(summed_two_ref[...])
    normed_two_ref[...] = normed_two
    hidden_two = normed_two * vrow(table_ref, CROSS_G) + vrow(table_ref, CROSS_S)
    hidden_ref[...] = hidden_two
    low_two_ref[...] = hidden_two.astype(BF16)
    accum_ref[...] = jnp.zeros_like(accum_ref)

    def ffn_chunk(chunk, carry):
        units = pl.ds(pl.multiple_of(chunk * 512, 512), 512)
        expanded = mm_nt(low_two_ref[...], win_ref[units, :]) + table_ref[pl.ds(FFN_BI + chunk, 1), :]
        square = expanded * expanded
        inner = expanded * (GELU_A + (GELU_A * GELU_B) * square)
        bent = jnp.tanh(inner)
        half = 0.5 * bent + 0.5
        active_ref[:, units] = (expanded * half).astype(BF16)
        slope = half + (0.5 * expanded) * (1.0 - bent * bent) * (
            GELU_A + (3.0 * GELU_A * GELU_B) * square
        )
        slope_ref[:, units] = slope.astype(BF16)
        accum_ref[...] += mm_nt(active_ref[:, units], wout_ref[:, units])
        return carry

    lax.fori_loop(0, chunks, ffn_chunk, 0)
    normed_three, inverse_three = norm_stats(
        hidden_ref[...] + accum_ref[...] + vrow(table_ref, FFN_BO)
    )
    result = normed_three * vrow(table_ref, FFN_G) + vrow(table_ref, FFN_S)
    result_ref[...] = result.astype(BF16)

    upstream = upstream_ref[...].astype(F32)
    add_row(acct_ref, FFN_G, column_sum(upstream * normed_three))
    add_row(acct_ref, FFN_S, column_sum(upstream))
    sum_three = norm_back(upstream, normed_three, inverse_three, vrow(table_ref, FFN_G))
    grad_low_ref[...] = sum_three.astype(BF16)
    add_row(acct_ref, FFN_BO, column_sum(grad_low_ref[...]))
    accum_ref[...] = sum_three

    def ffn_chunk_back(chunk, carry):
        units = pl.ds(pl.multiple_of(chunk * 512, 512), 512)
        grad_three = grad_low_ref[...]
        accout_ref[:, units] += mm_tn(grad_three, active_ref[:, units])
        grad_active = mm_nn(grad_three, wout_ref[:, units])
        grad_expanded = (grad_active * slope_ref[:, units].astype(F32)).astype(BF16)
        acct_ref[pl.ds(FFN_BI + chunk, 1), :] += column_sum(grad_expanded)
        accin_ref[units, :] += mm_tn(grad_expanded, low_two_ref[...])
        accum_ref[...] += mm_nn(grad_expanded, win_ref[units, :])
        return carry

    lax.fori_loop(0, chunks, ffn_chunk_back, 0)
    grad_hidden_two = accum_ref[...]
    normed_two = normed_two_ref[...]
    add_row(acct_ref, CROSS_G, column_sum(grad_hidden_two * normed_two))
    add_row(acct_ref, CROSS_S, column_sum(grad_hidden_two))
    sum_two_ref[...] = norm_back(grad_hidden_two, normed_two, inverse_two, vrow(table_ref, CROSS_G))

    @pl.when(step == pl.num_programs(0) - 1)
    def _():
        dwin_ref[...] = accin_ref[...].astype(BF16)
        dwout_ref[...] = accout_ref[...].astype(BF16)
        dtable_ref[...] = acct_ref[...]


def cross_backward(
    sum_two_ref, summed_one_ref, remote_ref, mixture_ref, query_ref, keys_ref, values_ref, shares_ref,
    weight_ref, table_ref, grad_remote_ref, sum_one_ref, up_ref, gq_ref, gk_ref, gv_ref, acc_ref, acct_ref,
):
    slots = shares_ref.shape[1]
    grad_two = sum_two_ref[...].astype(BF16)
    add_row(acct_ref, CROSS_BO, column_sum(grad_two))
    acc_ref[3] += mm_tn(grad_two, mixture_ref[...])
    up_ref[...] = mm_nn(grad_two, square(weight_ref, 3)).astype(BF16)

    def one_row_back(row, carry):
        at = pl.ds(pl.multiple_of(row * slots, slots), slots)
        attend_rows_back(
            up_ref, query_ref, keys_ref, values_ref, shares_ref, gq_ref, gk_ref, gv_ref, row, at)
        return carry

    lax.fori_loop(0, STEP_ROWS, one_row_back, 0)
    normed_one, inverse_one = norm_stats(summed_one_ref[...])
    low = (normed_one * vrow(table_ref, SELF_G) + vrow(table_ref, SELF_S)).astype(BF16)
    grad_query, grad_keys, grad_values = gq_ref[...], gk_ref[...], gv_ref[...]
    add_row(acct_ref, CROSS_BQ, column_sum(grad_query))
    add_row(acct_ref, CROSS_BV, column_sum(grad_values))
    acc_ref[0] += mm_tn(grad_query, low)
    acc_ref[1] += mm_tn(grad_keys, remote_ref[...])
    acc_ref[2] += mm_tn(grad_values, remote_ref[...])
    grad_remote_ref[...] = (
        mm_nn(grad_keys, square(weight_ref, 1)) + mm_nn(grad_values, square(weight_ref, 2))
    ).astype(BF16)
    grad_hidden_one = sum_two_ref[...] + mm_nn(grad_query, square(weight_ref, 0))
    add_row(acct_ref, SELF_G, column_sum(grad_hidden_one * normed_one))
    add_row(acct_ref, SELF_S, column_sum(grad_hidden_one))
    sum_one_ref[...] = norm_back(grad_hidden_one, normed_one, inverse_one, vrow(table_ref, SELF_G))


def self_backward(
    sum_one_ref, source_ref, mixture_ref, query_ref, keys_ref, values_ref, shares_ref, weight_ref,
    grad_source_ref, up_ref, gq_ref, gk_ref, gv_ref, acc_ref, acct_ref,
):
    slots = shares_ref.shape[1]
    grad_one = sum_one_ref[...].astype(BF16)
    add_row(acct_ref, SELF_BO, column_sum(grad_one))
    acc_ref[3] += mm_tn(grad_one, mixture_ref[...])
    up_ref[...] = mm_nn(grad_one, square(weight_ref, 3)).astype(BF16)

    def one_row_back(row, carry):
        at = pl.ds(pl.multiple_of(row * slots, slots), slots)
        attend_rows_back(
            up_ref, query_ref, keys_ref, values_ref, shares_ref, gq_ref, gk_ref, gv_ref, row, at)
        return carry

    lax.fori_loop(0, STEP_ROWS, one_row_back, 0)
    grad_query, grad_keys, grad_values = gq_ref[...], gk_ref[...], gv_ref[...]
    add_row(acct_ref, SELF_BQ, column_sum(grad_query))
    add_row(acct_ref, SELF_BV, column_sum(grad_values))
    source = source_ref[...]
    acc_ref[0] += mm_tn(grad_query, source)
    acc_ref[1] += mm_tn(grad_keys, source)
    acc_ref[2] += mm_tn(grad_values, source)
    grad_source_ref[...] = (
        sum_one_ref[...]
        + mm_nn(grad_query, square(weight_ref, 0))
        + mm_nn(grad_keys, square(weight_ref, 1))
        + mm_nn(grad_values, square(weight_ref, 2))
    ).astype(BF16)


class Scatter:
    def __init__(self, full, mine, halves, bufs, units, sems, base):
        self.full, self.mine, self.halves, self.units = full, mine, halves, units
        self.total, self.pair, self.far, self.near = bufs
        self.local, self.send, self.recv = sems
        self.base = base

    def copy(self, slot, source, target, partner):
        at = self.base + slot
        return pltpu.make_async_remote_copy(
            src_ref=source, dst_ref=target, send_sem=self.send.at[at], recv_sem=self.recv.at[at],
            device_id=partner, device_id_type=MESH)

    def hops(self, stage, incoming=False):
        z, y, x, core = place()
        if stage == 0:
            return [self.copy(0, self.full.at[:, :, :, :, 1 - core], self.pair, device(z, y, x, 1 - core))]
        sides = ((y, 1 - x), (1 - y, x))
        if stage == 1:
            return [
                self.copy(1 + i, self.total.at[h[0], :, 1 - y, 1 - x, h[1], h[2]], self.far.at[i], device(z, *side, core))
                for i, (side, h) in enumerate(zip(sides, self.halves))
            ]
        if stage == 2:
            return [
                self.copy(3 + i, self.total.at[:, :, side[0], side[1]], self.near.at[i], device(z, *side, core))
                for i, side in enumerate(sides)
            ]
        found = []
        for step in (1, 2, 3):
            other = lax.rem(z + step, 4)
            found.append(self.copy(4 + step, self.total.at[:, other, y, x], self.units.at[step], device(other, y, x, core)))
        return found

    def own(self):
        z, y, x, _ = place()
        return pltpu.make_async_copy(self.total.at[:, z, y, x], self.units.at[0], self.local.at[self.base])

    def start(self, stage):
        for hop in self.hops(stage):
            hop.start()
        if stage == 3:
            self.own().start()

    def arrive(self, stage):
        for hop in self.hops(stage):
            hop.wait_recv()
        z, y, x, core = place()
        if stage == 0:
            mats = self.total.shape[0]
            for mat in range(mats):
                self.total[mat] = (self.mine(mat, core) + self.pair[mat].astype(F32)).astype(BF16)
        if stage == 1:
            for i, (h, at) in enumerate(zip(self.halves, ((1 - y, x), (y, 1 - x)))):
                old = self.total[h[0], :, at[0], at[1], h[1], h[2]].astype(F32)
                self.total[h[0], :, at[0], at[1], h[1], h[2]] = (old + self.far[i].astype(F32)).astype(BF16)
        if stage == 2:
            old = self.total[:, :, y, x].astype(F32)
            self.total[:, :, y, x] = (
                old + self.near[0].astype(F32) + self.near[1].astype(F32)).astype(BF16)

    def finish(self):
        for stage in range(4):
            for hop in self.hops(stage):
                hop.wait_send()
        self.own().wait()


SCATTER_SLOTS = 8


def last_kernel(scatters, steps, *refs):
    step = pl.program_id(0)
    (sum_two_ref, s1_ref, remote_ref, m2_ref, q2_ref, k2_ref, v2_ref, p2_ref,
     source_ref, m1_ref, q1_ref, k1_ref, v1_ref, p1_ref, ws_ref, wc_ref, table_ref), refs = refs[:17], refs[17:]
    if scatters:
        (dwin, dwout, dtable_in), refs = refs[:3], refs[3:]
    (grad_remote_ref, grad_source_ref), refs = refs[:2], refs[2:]
    if scatters:
        units, refs = refs[:5], refs[5:]
    else:
        (dself_ref, dcross_ref, dtable_ref), refs = refs[:3], refs[3:]
    (up_ref, gq_ref, gk_ref, gv_ref, keep_ref, accs_ref, accc_ref, acct_ref), refs = refs[:8], refs[8:]
    if scatters:
        (lows_ref, lowc_ref, lowt_ref, win_own, wout_own), refs = refs[:5], refs[5:]
        bufs = [refs[4 * i : 4 * i + 4] for i in range(5)]
        local, *sems = refs[20:]
        sems = (local, *sems)
        top = lambda ref: (lambda mat, core: ref[mat].astype(F32))
        acc = lambda ref: (lambda mat, core: ref[mat, :, :, :, core])
        mats = ((slice(0, 2), ALL, ALL), (slice(2, 4), ALL, ALL))
        wide = lambda a, b: ((ALL, ALL, slice(0, a)), (ALL, ALL, slice(a, b)))
        inner = Scatter(dwin, top(win_own), ((ALL, slice(0, 32), ALL), (ALL, slice(32, 64), ALL)), bufs[0], units[0], sems, 0)
        outer = Scatter(dwout, top(wout_own), wide(1024, 2048), bufs[1], units[1], sems, 8)
        cross = Scatter(lowc_ref, acc(accc_ref), mats, bufs[2], units[2], sems, 16)
        own = Scatter(lows_ref, acc(accs_ref), mats, bufs[3], units[3], sems, 24)
        small = Scatter(lowt_ref, lambda mat, core: lowt_ref[mat, :, :, :, core].astype(F32), wide(128, 256), bufs[4], units[4], sems, 32)
        everything = (inner, outer, cross, own, small)
        core = lax.axis_index("fsdp") % 2
        fetch = [
            pltpu.make_async_copy(dwin.at[:, :, :, :, core], win_own, local.at[1]),
            pltpu.make_async_copy(dwout.at[:, :, :, :, core], wout_own, local.at[2]),
        ]

    @pl.when(step == 0)
    def _():
        if scatters:
            greet()
            inner.start(0)
            outer.start(0)
            for copy in fetch:
                copy.start()
        accs_ref[...] = jnp.zeros_like(accs_ref)
        accc_ref[...] = jnp.zeros_like(accc_ref)
        acct_ref[...] = jnp.zeros_like(acct_ref)

    @pl.when(step < steps)
    def _():
        cross_backward(
            sum_two_ref, s1_ref, remote_ref, m2_ref, q2_ref, k2_ref, v2_ref, p2_ref, wc_ref, table_ref,
            grad_remote_ref, keep_ref.at[step], up_ref, gq_ref, gk_ref, gv_ref, Flat(accc_ref), acct_ref)

    @pl.when(step >= steps)
    def _():
        self_backward(
            keep_ref.at[step - steps], source_ref, m1_ref, q1_ref, k1_ref, v1_ref, p1_ref, ws_ref,
            grad_source_ref, up_ref, gq_ref, gk_ref, gv_ref, Flat(accs_ref), acct_ref)

    if not scatters:
        @pl.when(step == 2 * steps - 1)
        def _():
            dself_ref[...] = accs_ref[...].astype(BF16)
            dcross_ref[...] = accc_ref[...].astype(BF16)
            dtable_ref[...] = acct_ref[...]
        return

    @pl.when(step == 0)
    def _():
        for copy in fetch:
            copy.wait()
        for piece in (inner, outer):
            piece.arrive(0)
            piece.start(1)

    @pl.when(step == 1)
    def _():
        for piece in (inner, outer):
            piece.arrive(1)
            piece.start(2)

    @pl.when(step == steps - 1)
    def _():
        for mat in range(4):
            lowc_ref[mat] = accc_ref[mat].astype(BF16)
        cross.start(0)
        for piece in (inner, outer):
            piece.arrive(2)
            piece.start(3)

    @pl.when(step == steps)
    def _():
        cross.arrive(0)
        cross.start(1)

    @pl.when(step == steps + 1)
    def _():
        cross.arrive(1)
        cross.start(2)

    @pl.when(step == 2 * steps - 2)
    def _():
        cross.arrive(2)
        cross.start(3)

    @pl.when(step == 2 * steps - 1)
    def _():
        for mat in range(4):
            lows_ref[mat] = accs_ref[mat].astype(BF16)
        own.start(0)
        table = columns_from_table(acct_ref[...] + dtable_in[...]).astype(BF16)
        lowt_ref[...] = table.reshape(lowt_ref.shape)
        small.start(0)
        for stage in range(3):
            for piece in (own, small):
                piece.arrive(stage)
                piece.start(stage + 1)
        for piece in everything:
            piece.arrive(3)
        for piece in everything:
            piece.finish()


class Flat:
    def __init__(self, ref):
        self.ref = ref

    def __getitem__(self, index):
        return self.ref[index].reshape(512, 512)

    def __setitem__(self, index, values):
        self.ref[index] = values.reshape(self.ref.shape[1:])


def sum_kernel(win_ref, wout_ref, cross_ref, own_ref, small_ref, *outs):
    total = lambda ref: (
        ref[0].astype(F32) + ref[1].astype(F32) + ref[2].astype(F32) + ref[3].astype(F32))
    (qkv, bias_one, out_one, norm_one, cross_q, cross_kv, bias_two, out_two, norm_two,
     win, win_bias, wout, wout_bias, norm_three) = outs
    own, cross = total(own_ref), total(cross_ref)
    qkv[...] = own[0:3]
    out_one[...] = own[3]
    cross_q[...] = cross[0]
    cross_kv[...] = cross[1:3]
    out_two[...] = cross[3]
    win[...] = total(win_ref)[0]
    wout[...] = total(wout_ref)[0]
    small = jnp.transpose(total(small_ref)[0])
    bias_one[...] = small[SELF_BQ : SELF_BQ + 3]
    norm_one[...] = small[SELF_G : SELF_G + 2]
    bias_two[...] = small[CROSS_BQ : CROSS_BQ + 3]
    norm_two[...] = small[CROSS_G : CROSS_G + 2]
    wout_bias[...] = small[FFN_BO : FFN_BO + 1]
    norm_three[...] = small[FFN_G : FFN_G + 2]
    win_bias[...] = small[128:132]


def fixed(shape):
    return pl.BlockSpec(shape, lambda i: (0,) * len(shape), pipeline_mode=pl.Buffered(1))


def shape_of(*shape, dtype=BF16):
    return jax.ShapeDtypeStruct(shape, dtype)


def params(limit, collective=None):
    if collective is None:
        return pltpu.CompilerParams(vmem_limit_bytes=limit, dimension_semantics=("arbitrary",))
    return pltpu.CompilerParams(
        vmem_limit_bytes=limit, dimension_semantics=("arbitrary",), collective_id=collective,
        has_side_effects=True)


ANYWHERE = pl.BlockSpec(memory_space=pl.ANY)
SQUARES = (4,) + BLOCKS + (16, 512)
WIN_BLOCKS = (1,) + BLOCKS + (64, 512)
WOUT_BLOCKS = (1,) + BLOCKS + (16, 2048)
SMALL_BLOCKS = (1,) + BLOCKS + (16, 256)


def layer(decoder_in, memory, out_grad, tgt_len, src_len, shards=None, weights=None):
    rows, slots, width = decoder_in.shape
    tokens = rows * slots
    block = STEP_ROWS * slots
    steps = rows // STEP_ROWS
    shares_block = (STEP_ROWS * HEADS, slots, slots)
    source = decoder_in.reshape(tokens, width)
    remote = memory.reshape(tokens, width)
    low, full = shape_of(tokens, width), shape_of(tokens, width, dtype=F32)
    vm = pltpu.VMEM
    dma = pltpu.SemaphoreType.DMA
    early = lambda i: jnp.minimum(i, steps - 1)
    late = lambda i: jnp.maximum(i - steps, 0)
    tok = lambda when: pl.BlockSpec((block, width), lambda i: (when(i), 0))
    shares = lambda when: pl.BlockSpec(shares_block, lambda i: (when(i), 0, 0))
    half_out = lambda when: [tok(when), tok(when), tok(when), shares(when), tok(when), tok(when)]
    shares_shape = shape_of(rows * HEADS, slots, slots)
    half_shape = [low, low, low, shares_shape, low, full]
    table_shape = shape_of(TABLE, width, dtype=F32)
    table_spec = fixed((TABLE, width))
    ins = [source, remote, tgt_len, src_len]
    in_specs = [tok(early), tok(late), fixed(tgt_len.shape), fixed(src_len.shape)]
    out_shape, out_specs = half_shape * 2, half_out(early) + half_out(late)
    scratch = []
    if shards is not None:
        ins += list(shards)
        in_specs += [ANYWHERE] * 8
        out_shape += [table_shape, shape_of(*SQUARES), shape_of(*SQUARES), shape_of(*WIN_BLOCKS), shape_of(*WOUT_BLOCKS)]
        out_specs += [table_spec] + [ANYWHERE] * 4
        scratch += [vm(SQUARES, BF16), vm(SQUARES, BF16), vm(SMALL_BLOCKS, BF16)]
        scratch += [dma((GATHER_SLOTS,)), dma((GATHER_SLOTS,)), dma((GATHER_SLOTS,)), dma((2,))]
    else:
        ws, wc, win, wout, table = weights
        ws, wc = ws.reshape(SQUARES), wc.reshape(SQUARES)
        ins += [ws, wc, table]
        in_specs += [fixed(SQUARES), fixed(SQUARES), table_spec]
    scratch += [vm((slots, slots), F32), vm((block, width), F32), vm((steps, block, width), F32), vm((rows, 2, slots), F32)]
    outs = pl.pallas_call(
        functools.partial(first_kernel, shards is not None, steps),
        grid=(2 * steps,), in_specs=in_specs, out_specs=out_specs, out_shape=out_shape, scratch_shapes=scratch,
        compiler_params=params(60 << 20, None if shards is None else 1), name="first",
    )(*ins)
    q1, k1, v1, p1, m1, s1, q2, k2, v2, p2, m2, s2 = outs[:FIRST_OUT]
    if shards is not None:
        table, ws, wc, win, wout = outs[FIRST_OUT:]
        win = win.reshape(-1, width)
        wout = wout.reshape(width, -1)
    hidden = win.shape[0]
    now = lambda i: i
    result, sum_two, dwin, dwout, dtable = pl.pallas_call(
        ffn_kernel,
        grid=(steps,),
        in_specs=[tok(now), tok(now), fixed(win.shape), fixed(wout.shape), table_spec],
        out_specs=[tok(now), tok(now), fixed(win.shape), fixed(wout.shape), table_spec],
        out_shape=[low, full, shape_of(*win.shape), shape_of(*wout.shape), table_shape],
        scratch_shapes=[
            vm((block, width), F32), vm((block, width), F32), vm((block, hidden), BF16), vm((block, hidden), BF16),
            vm((block, width), F32), vm((block, width), BF16), vm((block, width), BF16),
            vm(win.shape, F32), vm(wout.shape, F32), vm((TABLE, width), F32),
        ],
        compiler_params=params(60 << 20), name="feed_forward",
    )(s2, out_grad.reshape(tokens, width), win, wout, table)

    ins = [sum_two, s1, remote, m2, q2, k2, v2, p2, source, m1, q1, k1, v1, p1, ws, wc, table]
    in_specs = [tok(early)] * 7 + [shares(early)] + [tok(late)] * 5 + [shares(late)]
    in_specs += [fixed(SQUARES), fixed(SQUARES), table_spec]
    out_shape, out_specs = [low, low], [tok(early), tok(late)]
    scratch = [vm((block, width), BF16)] * 4 + [
        vm((steps, block, width), F32), vm(SQUARES, F32), vm(SQUARES, F32), vm((TABLE, width), F32)]
    if shards is not None:
        ins += [dwin.reshape(WIN_BLOCKS), dwout.reshape(WOUT_BLOCKS), dtable]
        in_specs += [ANYWHERE, ANYWHERE, table_spec]
        every = (WIN_BLOCKS, WOUT_BLOCKS, SQUARES, SQUARES, SMALL_BLOCKS)
        out_shape += [shape_of(4, s[0], s[5], s[6]) for s in every]
        out_specs += [ANYWHERE] * 5
        scratch += [vm(SQUARES, BF16), vm(SQUARES, BF16), vm(SMALL_BLOCKS, BF16)]
        scratch += [vm(s[:4] + s[5:], BF16) for s in every[:2]]
        cut = ((0, 2, 1), (0, 1, 2), (2, 1, 1), (2, 1, 1), (0, 1, 2))
        for s, (m, r, l) in zip(every, cut):
            mats = s[0] // max(m, 1)
            scratch += [
                vm(s[:4] + s[5:], BF16), vm(s[:4] + s[5:], BF16),
                vm((2, mats, 4, s[5] // r, s[6] // l), BF16), vm((2, s[0], 4, s[5], s[6]), BF16)]
        slots_all = 5 * SCATTER_SLOTS
        scratch += [dma((slots_all,)), dma((slots_all,)), dma((slots_all,))]
    else:
        out_shape += [shape_of(*SQUARES), shape_of(*SQUARES), table_shape]
        out_specs += [fixed(SQUARES), fixed(SQUARES), table_spec]
    grad_remote, grad_source, *tail = pl.pallas_call(
        functools.partial(last_kernel, shards is not None, steps),
        grid=(2 * steps,), in_specs=in_specs, out_specs=out_specs, out_shape=out_shape, scratch_shapes=scratch,
        compiler_params=params(63 << 20, None if shards is None else 2), name="last",
    )(*ins)
    as_rows = lambda array: array.reshape(rows, slots, width)
    if shards is None:
        dself, dcross, dtable_last = tail
        grads = (dself.reshape(4, 512, 512), dcross.reshape(4, 512, 512), dwin, dwout, dtable + dtable_last)
    else:
        f = lambda *shape: shape_of(*shape, dtype=F32)
        grads = pl.pallas_call(
            sum_kernel,
            out_shape=[f(3, 16, 512), f(3, 16), f(16, 512), f(2, 16), f(16, 512), f(2, 16, 512), f(3, 16), f(16, 512),
                       f(2, 16), f(64, 512), f(4, 16), f(16, 2048), f(1, 16), f(2, 16)],
            compiler_params=pltpu.CompilerParams(vmem_limit_bytes=16 << 20), name="sum_planes",
        )(*tail)
    return as_rows(result), as_rows(grad_source), as_rows(grad_remote), grads


def turn(array):
    return jnp.swapaxes(array, -1, -2)


AXES = ("dp", "fsdp")


def gather_plain(parts, count):
    (self_qkv, self_bias, self_out, self_norm, cross_q, cross_kv, cross_bias, cross_out, cross_norm,
     ffn_in, ffn_in_bias, ffn_out, ffn_out_bias, ffn_norm) = parts
    cols = self_out.shape[1]
    width = self_out.shape[0]
    chunks = ffn_out.shape[0] // width
    small = jnp.concatenate(
        [self_bias, self_norm, cross_bias, cross_norm, ffn_out_bias[None], ffn_norm,
         ffn_in_bias.reshape(chunks, cols)], axis=0)
    small = jnp.pad(turn(small), ((0, 0), (0, width - small.shape[0])))
    packed = jnp.concatenate([
        turn(self_qkv).reshape(-1, width), turn(self_out), turn(cross_q),
        turn(cross_kv).reshape(-1, width), turn(cross_out), turn(ffn_in),
        turn(ffn_out).reshape(cols, chunks, width).swapaxes(0, 1).reshape(-1, width), small], axis=0)
    whole_set = lax.all_gather(packed, AXES, axis=0, tiled=False)
    square = whole_set[:, : 8 * cols].reshape(count, 8, cols, width).swapaxes(0, 1)
    square = square.reshape(8, width, width)
    low = 8 * cols
    win = whole_set[:, low : low + chunks * cols].reshape(chunks * width, width)
    low += chunks * cols
    wout = whole_set[:, low : low + chunks * cols].reshape(count, chunks, cols, width)
    wout = wout.transpose(0, 2, 1, 3).reshape(width, chunks * width)
    low += chunks * cols
    table = whole_set[:, low:]
    first = table[:, :, :13].transpose(2, 0, 1).reshape(13, width)
    second = table[:, :, 13 : 13 + chunks].transpose(0, 2, 1).reshape(chunks, width)
    table = jnp.concatenate([first, second], axis=0).astype(F32)
    table = jnp.pad(table, ((0, TABLE - table.shape[0]), (0, 0)))
    return square[:4], square[4:], win, wout, table


def scatter_plain(dself, dcross, dwin, dwout, dtable, count):
    width = dself.shape[1]
    cols = width // count
    chunks = dwin.shape[0] // width
    squares = jnp.concatenate([dself, dcross], axis=0).reshape(8, count, cols, width).swapaxes(0, 1)
    first = dtable[:13].reshape(13, count, cols).transpose(1, 2, 0)
    second = dtable[13 : 13 + chunks].reshape(count, chunks, cols).transpose(0, 2, 1)
    small = jnp.concatenate([first, second], axis=2)
    small = jnp.pad(small, ((0, 0), (0, 0), (0, width - small.shape[2]))).astype(BF16)
    packed = jnp.concatenate([
        squares.reshape(count, 8 * cols, width), dwin.reshape(count, chunks * cols, width),
        dwout.reshape(count, cols, chunks, width).swapaxes(1, 2).reshape(count, -1, width), small],
        axis=1)
    mine = lax.psum_scatter(packed, AXES, scatter_dimension=0, tiled=False).astype(F32)
    square = turn(mine[: 8 * cols].reshape(8, cols, width))
    low = 8 * cols
    ffn_in = turn(mine[low : low + chunks * cols])
    low += chunks * cols
    ffn_out = mine[low : low + chunks * cols].reshape(chunks, cols, width).swapaxes(0, 1)
    ffn_out = turn(ffn_out.reshape(cols, chunks * width))
    low += chunks * cols
    small = turn(mine[low:, : 13 + chunks])
    return (square[:3], small[0:3], square[3], small[3:5], square[4], square[5:7], small[5:8], square[7],
            small[8:10], ffn_in, small[13:].reshape(-1), ffn_out, small[10], small[11:13])


def small_block(parts):
    (_, self_bias, _, self_norm, _, _, cross_bias, _, cross_norm, _, ffn_in_bias, _, ffn_out_bias, ffn_norm) = parts
    cols = ffn_out_bias.shape[0]
    first = jnp.concatenate(
        [self_bias, self_norm, cross_bias, cross_norm, ffn_out_bias[None], ffn_norm,
         jnp.zeros((128 - 13, cols), BF16), ffn_in_bias.reshape(-1, cols)], axis=0)
    return turn(jnp.pad(first, ((0, 256 - first.shape[0]), (0, 0))))


def on_device(count, direct, decoder_in, memory, out_grad, tgt_len, src_len, *parts):
    if not direct:
        weights = gather_plain(parts, count)
        result, grad_source, grad_remote, grads = layer(
            decoder_in, memory, out_grad, tgt_len, src_len, weights=weights)
        return (result, grad_source, grad_remote, *scatter_plain(*grads, count))
    (self_qkv, _, self_out, _, cross_q, cross_kv, _, cross_out, _, ffn_in, _, ffn_out, _, _) = parts
    shards = [turn(part) for part in (self_qkv, self_out, cross_q, cross_kv, cross_out, ffn_in, ffn_out)]
    shards.append(small_block(parts))
    shards = [part.reshape((-1,) + part.shape[-2:]) for part in shards]
    result, grad_source, grad_remote, grads = layer(
        decoder_in, memory, out_grad, tgt_len, src_len, shards=shards)
    (qkv, bias_one, out_one, norm_one, query, pair, bias_two, out_two, norm_two, win, win_bias, wout, wout_bias,
     norm_three) = grads
    return (result, grad_source, grad_remote, turn(qkv), bias_one, turn(out_one), norm_one, turn(query), turn(pair),
            bias_two, turn(out_two), norm_two, turn(win), win_bias.reshape(-1), turn(wout), wout_bias.reshape(-1),
            norm_three)


def solution(mesh):
    count = mesh.shape["dp"] * mesh.shape["fsdp"]
    direct = mesh.shape["dp"] == 4 and mesh.shape["fsdp"] == 8
    rows = P(AXES, None, None)
    lens = P(AXES, None)
    cube = P(None, None, AXES)
    flat = P(None, AXES)
    line = P(AXES)
    params_in = (cube, flat, flat, flat, flat, cube, flat, flat, flat, flat, line, flat, line, flat)
    return jax.shard_map(
        functools.partial(on_device, count, direct),
        mesh=mesh,
        in_specs=(rows, rows, rows, lens, lens) + params_in,
        out_specs=(rows, rows, rows) + params_in,
        check_vma=False,
    )
```

```python
import functools

import jax
import jax.numpy as jnp
from jax import lax
from jax.experimental import pallas as pl
from jax.experimental.pallas import tpu as pltpu
from jax.sharding import PartitionSpec as P

F32 = jnp.float32
BF16 = jnp.bfloat16
EPS = 1e-05
MASKED = -1e30
HEADS = 8
HEAD_DIM = 64
PAIR = 128
QUAD = 256
GELU_A = 0.7978845608028654
GELU_B = 0.044715


def mm(left, right, left_dim, right_dim):
    return lax.dot_general(
        left, right, (((left_dim,), (right_dim,)), ((), ())), preferred_element_type=F32
    )


def mm_nt(left, right):
    return mm(left, right, 1, 1)


def mm_nn(left, right):
    return mm(left, right, 1, 0)


def mm_tn(left, right):
    return mm(left, right, 0, 0)


def norm_stats(summed):
    centred = summed - jnp.mean(summed, axis=-1, keepdims=True)
    inverse = lax.rsqrt(jnp.mean(centred * centred, axis=-1, keepdims=True) + EPS)
    return centred * inverse, inverse


def norm_back(upstream, normed, inverse, gain):
    scaled = upstream * gain
    mean_scaled = jnp.mean(scaled, axis=-1, keepdims=True)
    mean_product = jnp.mean(scaled * normed, axis=-1, keepdims=True)
    return (scaled - mean_scaled - normed * mean_product) * inverse


def column_sum(values):
    return jnp.sum(values.astype(F32), axis=0, keepdims=True)


def lane_band(width, head):
    lane = lax.broadcasted_iota(jnp.int32, (1, width), 1)
    return (lane >= head * HEAD_DIM) & (lane < (head + 1) * HEAD_DIM)


def keep_head(values, head):
    return jnp.where(lane_band(values.shape[1], head), values, jnp.zeros_like(values))


def mask_bias(key_ids, query_ids, causal):
    slots = key_ids.shape[1]
    down = jnp.transpose(jnp.broadcast_to(key_ids, (slots, slots)))
    allowed = down == query_ids
    if causal:
        key_at = lax.broadcasted_iota(jnp.int32, (slots, slots), 0)
        query_at = lax.broadcasted_iota(jnp.int32, (slots, slots), 1)
        allowed = allowed & (key_at <= query_at)
    return jnp.where(allowed, 0.0, MASKED).astype(F32)


def attend_rows(query_ref, keys_ref, values_ref, bias_ref, shares_ref, mixture_ref, row, at, into):
    for quad in range(HEADS * HEAD_DIM // QUAD):
        lanes = slice(quad * QUAD, (quad + 1) * QUAD)
        values_quad = values_ref[at, lanes]
        parts, wide = [], []
        for inner in range(QUAD // HEAD_DIM):
            head = quad * (QUAD // HEAD_DIM) + inner
            first = head * HEAD_DIM // PAIR * PAIR
            pair = slice(first, first + PAIR)
            keys_head = keep_head(keys_ref[at, pair], head - first // HEAD_DIM)
            scores = mm_nt(keys_head, query_ref[at, pair]) + bias_ref[...]
            top = jnp.max(scores, axis=0, keepdims=True)
            raised = jnp.exp(scores - top)
            total = jnp.sum(raised, axis=0, keepdims=True)
            shares = (raised * (1.0 / total)).astype(BF16)
            shares_ref[row * HEADS + head] = shares
            parts.append(shares)
            wide.append(keep_head(values_quad, inner))
        mixture = mm_tn(jnp.concatenate(parts, 0), jnp.concatenate(wide, 0))
        mixture_ref[into, lanes] = mixture.astype(BF16)


def attend_rows_back(
    upstream_ref, query_ref, keys_ref, values_ref, shares_ref, gq_ref, gk_ref, gv_ref, row, at, into
):
    for quad in range(HEADS * HEAD_DIM // QUAD):
        lanes = slice(quad * QUAD, (quad + 1) * QUAD)
        query_quad = query_ref[at, lanes]
        keys_quad = keys_ref[at, lanes]
        up_quad = upstream_ref[at, lanes]
        grad_query = grad_keys = grad_values = None
        for inner in range(QUAD // HEAD_DIM):
            head = quad * (QUAD // HEAD_DIM) + inner
            first = head * HEAD_DIM // PAIR * PAIR
            pair = slice(first, first + PAIR)
            values_head = keep_head(values_ref[at, pair], head - first // HEAD_DIM)
            shares = shares_ref[row * HEADS + head]
            grad_shares = mm_nt(values_head, upstream_ref[at, pair])
            wide = shares.astype(F32)
            product = wide * grad_shares
            centre = jnp.sum(product, axis=0, keepdims=True)
            grad_scores = (product - wide * centre).astype(BF16)
            one = mm_nn(grad_scores, keep_head(query_quad, inner))
            two = mm_nn(shares, keep_head(up_quad, inner))
            three = mm_tn(grad_scores, keep_head(keys_quad, inner))
            grad_keys = one if grad_keys is None else grad_keys + one
            grad_values = two if grad_values is None else grad_values + two
            grad_query = three if grad_query is None else grad_query + three
        gq_ref[into, lanes] = (grad_query * HEAD_DIM**-0.5).astype(BF16)
        gk_ref[into, lanes] = grad_keys.astype(BF16)
        gv_ref[into, lanes] = grad_values.astype(BF16)


STEP_ROWS = 2

SELF_BQ, SELF_BV, SELF_BO, SELF_G, SELF_S = 0, 1, 2, 3, 4
CROSS_BQ, CROSS_BV, CROSS_BO, CROSS_G, CROSS_S = 5, 6, 7, 8, 9
FFN_BO, FFN_G, FFN_S, FFN_BI = 10, 11, 12, 13
TABLE = 24


def vrow(table_ref, index):
    return table_ref[index : index + 1, :]


def add_row(ref, index, values):
    ref[index : index + 1, :] += values


MESH = pl.DeviceIdType.MESH
ALL = slice(None)


def place():
    z = lax.axis_index("dp")
    f = lax.axis_index("fsdp")
    return z, f // 4, (f // 2) % 2, f % 2


def device(z, y, x, core):
    return (z, y * 4 + x * 2 + core)


def partners():
    z, y, x, core = place()
    found = [device(lax.rem(z + step, 4), y, x, core) for step in (1, 2, 3)]
    return found + [device(z, y, 1 - x, core), device(z, 1 - y, x, core), device(z, y, x, 1 - core)]


def hail():
    barrier = pltpu.get_barrier_semaphore()
    for partner in partners():
        pl.semaphore_signal(barrier, inc=1, device_id=partner, device_id_type=MESH)


def await_hails():
    pl.semaphore_wait(pltpu.get_barrier_semaphore(), 6)


class Gather:
    def __init__(self, ref, own, first, second, sems, base):
        self.ref, self.own, self.first, self.second = ref, own, first, second
        self.local, self.send, self.recv = sems
        self.base = base
        self.mats = slice(min(m.start for _, m in own), max(m.stop for _, m in own))

    @staticmethod
    def slots(own):
        return 3 * len(own) + 5

    def copy(self, slot, source, target, partner):
        at = self.base + slot
        return pltpu.make_async_remote_copy(
            src_ref=source, dst_ref=target, send_sem=self.send.at[at], recv_sem=self.recv.at[at],
            device_id=partner, device_id_type=MESH)

    def at(self, half, z, y, x, core):
        mats, rows, lanes = half
        return self.ref.at[mats, z, y, x, core, rows, lanes]

    def locals(self):
        z, y, x, core = place()
        return [
            pltpu.make_async_copy(source, self.ref.at[mats, z, y, x, core], self.local.at[self.base + i])
            for i, (source, mats) in enumerate(self.own)
        ]

    def hops(self, stage, incoming):
        z, y, x, core = place()
        full = (self.mats, ALL, ALL)
        found = []
        many = len(self.own)
        if stage == 0:
            for step in (1, 2, 3):
                other = lax.rem(z + (4 - step if incoming else step), 4)
                for i, (source, mats) in enumerate(self.own):
                    target = self.ref.at[mats, other if incoming else z, y, x, core]
                    found.append(self.copy((step - 1) * many + i, source, target, device(other, y, x, core)))
        if stage == 1:
            for slot, (py, px) in enumerate(((y, 1 - x), (1 - y, x))):
                sent = self.at(full, ALL, y, x, core)
                target = self.at(full, ALL, py, px, core) if incoming else sent
                found.append(self.copy(3 * many + slot, sent, target, device(z, py, px, core)))
        if stage == 2:
            for slot, (half, by, bx, py, px) in enumerate((
                (self.first, 1 - y, x, y, 1 - x), (self.second, y, 1 - x, 1 - y, x))):
                sent = self.at(half, ALL, by, bx, core)
                target = self.at(half, ALL, 1 - y, 1 - x, core) if incoming else sent
                found.append(self.copy(3 * many + 2 + slot, sent, target, device(z, py, px, core)))
        if stage == 3:
            sent = self.at(full, ALL, ALL, ALL, core)
            target = self.at(full, ALL, ALL, ALL, 1 - core) if incoming else sent
            found.append(self.copy(3 * many + 4, sent, target, device(z, y, x, 1 - core)))
        return found

    def start(self, stage):
        for hop in self.hops(stage, False):
            hop.start()

    def arrive(self, stage):
        for hop in self.hops(stage, True):
            hop.wait_recv()

    def finish(self):
        for stage in range(4):
            for hop in self.hops(stage, False):
                hop.wait_send()


def gather_pieces(shards, targets, sems):
    qkv, out_one, cross_q, cross_kv, out_two, win, wout, small = shards
    ws, wc, win_all, wout_all, small_all = targets
    one = lambda n: slice(n, n + 1)
    lanes = lambda n: ((ALL, ALL, slice(0, n)), (ALL, ALL, slice(n, 2 * n)))
    single = lambda n: ((one(n), ALL, slice(0, 256)), (one(n), ALL, slice(256, 512)))
    plans = [
        (small_all, [(small, one(0))], *lanes(128)),
        (ws, [(qkv.at[0:1], one(0))], *single(0)),
        (ws, [(qkv.at[1:2], one(1))], *single(1)),
        (ws, [(qkv.at[2:3], one(2))], *single(2)),
        (ws, [(out_one, one(3))], *single(3)),
        (wc, [(cross_q, one(0)), (cross_kv, slice(1, 3)), (out_two, one(3))],
         (slice(0, 2), ALL, ALL), (slice(2, 4), ALL, ALL)),
        (win_all, [(win, one(0))], (ALL, slice(0, 32), ALL), (ALL, slice(32, 64), ALL)),
        (wout_all, [(wout, one(0))], *lanes(1024)),
    ]
    pieces, base = [], 0
    for ref, own, first, second in plans:
        pieces.append(Gather(ref, own, first, second, sems, base))
        base += Gather.slots(own)
    return pieces


GATHER_SLOTS = 80

BLOCKS = (4, 2, 2, 2)


def square(ref, index):
    return ref[index].reshape(512, 512)


def prepare_masks(tgt_ref, src_ref, ids_ref, bias_ref):
    rows, sents = tgt_ref.shape
    slots = ids_ref.shape[2]
    before = lax.broadcasted_iota(jnp.int32, (sents, sents), 0)
    after = lax.broadcasted_iota(jnp.int32, (sents, sents), 1)
    ladder = (before <= after).astype(F32)
    slot = lax.broadcasted_iota(jnp.int32, (sents, slots), 1).astype(F32)
    for side, ref in enumerate((tgt_ref, src_ref)):
        lengths = ref[...].astype(F32)
        finish = lax.dot_general(
            ladder, lengths, (((0,), (1,)), ((), ())),
            precision=lax.Precision.HIGHEST, preferred_element_type=F32)
        for row in range(rows):
            ended = (finish[:, row : row + 1] <= slot).astype(F32)
            ids_ref[row, side : side + 1, :] = jnp.sum(ended, axis=0, keepdims=True)

    def one_row(row, carry):
        ids = ids_ref[row]
        bias_ref[0, row] = mask_bias(ids[0:1], ids[0:1], True)
        bias_ref[1, row] = mask_bias(ids[1:2], ids[0:1], False)
        return carry

    lax.fori_loop(0, rows, one_row, 0)


def tokens_of(block, size):
    start = block * size
    return pl.ds(start if isinstance(start, int) else pl.multiple_of(start, size), size)


def self_forward(
    step, source_ref, weight_ref, table_ref, query_ref, keys_ref, values_ref,
    shares_ref, mixture_ref, summed_ref, bias_ref,
):
    slots = shares_ref.shape[1]
    block = STEP_ROWS * slots
    for row in range(STEP_ROWS):
        attend_rows(
            query_ref, keys_ref, values_ref, bias_ref.at[0, step * STEP_ROWS + row], shares_ref, mixture_ref, row,
            tokens_of(step * STEP_ROWS + row, slots), tokens_of(row, slots))
    summed_ref[...] = (
        source_ref[tokens_of(step, block), :].astype(F32)
        + mm_nt(mixture_ref[...], square(weight_ref, 3)) + vrow(table_ref, SELF_BO)
    )


def cross_forward(
    step, summed_one_ref, remote_ref, weight_ref, table_ref,
    query_ref, keys_ref, values_ref, shares_ref, mixture_ref, summed_ref, bias_ref, hidden_ref,
):
    slots = shares_ref.shape[1]
    normed_one, _ = norm_stats(summed_one_ref[...])
    hidden_one = normed_one * vrow(table_ref, SELF_G) + vrow(table_ref, SELF_S)
    hidden_ref[...] = hidden_one
    query = mm_nt(hidden_one.astype(BF16), square(weight_ref, 0)) + vrow(table_ref, CROSS_BQ)
    query_ref[...] = (query * HEAD_DIM**-0.5).astype(BF16)
    remote = remote_ref[...]
    keys_ref[...] = mm_nt(remote, square(weight_ref, 1)).astype(BF16)
    values_ref[...] = (mm_nt(remote, square(weight_ref, 2)) + vrow(table_ref, CROSS_BV)).astype(BF16)

    for row in range(STEP_ROWS):
        at = tokens_of(row, slots)
        attend_rows(
            query_ref, keys_ref, values_ref, bias_ref.at[1, step * STEP_ROWS + row], shares_ref, mixture_ref, row, at, at)
    summed_ref[...] = (
        hidden_ref[...] + mm_nt(mixture_ref[...], square(weight_ref, 3)) + vrow(table_ref, CROSS_BO)
    )


def table_from_columns(columns, table_ref):
    turned = jnp.transpose(columns[:, :128])
    table_ref[0:TABLE, :] = turned[0:TABLE]
    parts = [columns[:, 128 + k : 129 + k].reshape(32, 1, 16, 1) for k in range(4)]
    line = jnp.concatenate(parts, axis=1).reshape(2048, 1)
    line = jnp.transpose(jnp.broadcast_to(line, (2048, 128)))
    for k in range(4):
        table_ref[FFN_BI + k : FFN_BI + k + 1, :] = line[0:1, k * 512 : (k + 1) * 512]


def columns_from_table(rows):
    rows = jnp.concatenate([rows, jnp.zeros((128 - TABLE, 512), F32)], axis=0)
    columns = jnp.transpose(rows)
    lane = lax.broadcasted_iota(jnp.int32, (512, 128), 1)
    line = jnp.concatenate([columns[:, FFN_BI + k : FFN_BI + k + 1] for k in range(4)], axis=0)
    line = line.reshape(32, 4, 16, 1)
    second = jnp.zeros((512, 128), F32)
    for k in range(4):
        second = jnp.where(lane == k, line[:, k].reshape(512, 1), second)
    return jnp.concatenate([columns, second], axis=1)


def small_columns(parts, lines_ref, small_ref):
    lines_ref[...] = jnp.zeros_like(lines_ref)
    at = 0
    for part in parts[:-1]:
        lines_ref[at : at + part.shape[0], 0:16] = part[...].astype(F32)
        at += part.shape[0]
    line = parts[-1][...].astype(F32)
    for k in range(4):
        lines_ref[128 + k : 129 + k, 0:16] = line[:, k * 16 : k * 16 + 16]
    small_ref[0, :, 0:128] = jnp.transpose(lines_ref[0:128, :])[0:16].astype(BF16)
    small_ref[0, :, 128:256] = jnp.transpose(lines_ref[128:256, :])[0:16].astype(BF16)


FIRST_OUT = 11


def first_kernel(gathers, steps, *refs):
    step = pl.program_id(0)
    (source_ref, remote_ref, tgt_ref, src_ref), refs = refs[:4], refs[4:]
    if gathers:
        shards, smalls, refs = refs[:7], refs[7:14], refs[14:]
    else:
        (ws_ref, wc_ref, table_ref), refs = refs[:3], refs[3:]
    (q1_out, k1_out, v1_out, m1_ref, s1_ref, q2_ref, k2_ref, v2_ref, m2_ref, s2_ref, shares_ref), refs = (
        refs[:FIRST_OUT], refs[FIRST_OUT:])
    if gathers:
        (table_ref, ws_out, wc_out, win_out, wout_out), refs = refs[:5], refs[5:]
        (ws_ref, wc_ref, small_ref, own_ref, lines_ref, *sems), refs = refs[:8], refs[8:]
        pieces = gather_pieces((*shards, own_ref), (ws_ref, wc_ref, win_out, wout_out, small_ref), sems)
        small, query, keys, values, mixed, cross, inner, outer = pieces
        head = (small, query, keys, values, mixed)
    bias_ref, hidden_ref, keep_ref, ids_ref, q1_ref, k1_ref, v1_ref, out_sem = refs
    saves = [
        pltpu.make_async_copy(ref, out, out_sem.at[i])
        for i, (ref, out) in enumerate(((q1_ref, q1_out), (k1_ref, k1_out), (v1_ref, v1_out)))
    ]
    if gathers:
        saves.append(pltpu.make_async_copy(ws_ref, ws_out, out_sem.at[3]))
        late_save = pltpu.make_async_copy(wc_ref, wc_out, out_sem.at[4])
    tokens = source_ref.shape[0]

    def project(index, out_ref, row, factor):
        for part in range(4):
            at = tokens_of(part, tokens // 4)
            found = mm_nt(source_ref[at, :], square(ws_ref, index))
            if row is not None:
                found = found + vrow(table_ref, row)
            if factor is not None:
                found = found * factor
            out_ref[at, :] = found.astype(BF16)

    def project_query():
        project(0, q1_ref, SELF_BQ, HEAD_DIM**-0.5)

    def project_keys():
        project(1, k1_ref, None, None)

    def project_values():
        project(2, v1_ref, SELF_BV, None)

    @pl.when(step == 0)
    def _():
        if not gathers:
            prepare_masks(tgt_ref, src_ref, ids_ref, bias_ref)
            project_query()
            project_keys()
            project_values()
        else:
            hail()
            small_columns(smalls, lines_ref, own_ref)
            for piece in pieces:
                for copy in piece.locals():
                    copy.start()
            await_hails()
            for piece in head:
                piece.start(0)
            prepare_masks(tgt_ref, src_ref, ids_ref, bias_ref)
            for piece in head:
                for copy in piece.locals():
                    copy.wait()

            def move(piece, stage):
                piece.arrive(stage)
                if stage < 3:
                    piece.start(stage + 1)

            move(small, 0)
            move(query, 0)
            move(keys, 0)
            move(small, 1)
            move(query, 1)
            move(values, 0)
            move(keys, 1)
            move(small, 2)
            move(query, 2)
            move(mixed, 0)
            cross.start(0)
            move(values, 1)
            move(keys, 2)
            move(small, 3)
            table_from_columns(small_ref[0].reshape(512, 256).astype(F32), table_ref)
            move(mixed, 1)
            move(query, 3)
            project_query()
            move(values, 2)
            inner.start(0)
            move(keys, 3)
            project_keys()
            move(mixed, 2)
            for piece in (cross, inner, outer):
                for copy in piece.locals():
                    copy.wait()
            cross.arrive(0)
            cross.start(1)
            outer.start(0)
            move(values, 3)
            project_values()
            move(mixed, 3)
        for copy in saves:
            copy.start()

    @pl.when((step >= 1) & (step <= steps))
    def _():
        self_forward(
            step - 1, source_ref, ws_ref, table_ref, q1_ref, k1_ref, v1_ref,
            shares_ref, m1_ref, s1_ref, bias_ref)
        keep_ref[step - 1] = s1_ref[...]

    @pl.when(step > steps)
    def _():
        at = step - steps - 1
        cross_forward(
            at, keep_ref.at[at], remote_ref, wc_ref, table_ref,
            q2_ref, k2_ref, v2_ref, shares_ref, m2_ref, s2_ref, bias_ref, hidden_ref)

    if gathers:
        @pl.when(step == 1)
        def _():
            cross.arrive(1)
            cross.start(2)
            inner.arrive(0)
            inner.start(1)

        @pl.when(step == steps - 1)
        def _():
            cross.arrive(2)
            cross.start(3)
            outer.arrive(0)
            outer.start(1)

        @pl.when(step == steps)
        def _():
            cross.arrive(3)
            late_save.start()

        @pl.when(step == steps + 1)
        def _():
            inner.arrive(1)
            inner.start(2)

        @pl.when(step == steps + 2)
        def _():
            outer.arrive(1)
            outer.start(2)
            inner.arrive(2)
            inner.start(3)

        @pl.when(step == 2 * steps - 1)
        def _():
            outer.arrive(2)
            outer.start(3)

    @pl.when(step == 2 * steps)
    def _():
        if gathers:
            inner.arrive(3)
            outer.arrive(3)
            for piece in pieces:
                piece.finish()
            late_save.wait()
        for copy in saves:
            copy.wait()


def ffn_kernel(
    summed_two_ref, upstream_ref, win_ref, wout_ref, table_ref,
    result_ref, sum_two_ref, dwin_ref, dwout_ref, dtable_ref,
    normed_two_ref, hidden_ref, active_ref, slope_ref, accum_ref,
    low_two_ref, grad_low_ref, accin_ref, accout_ref, acct_ref,
):
    step = pl.program_id(0)
    chunks = win_ref.shape[0] // 512

    @pl.when(step == 0)
    def _():
        accin_ref[...] = jnp.zeros_like(accin_ref)
        accout_ref[...] = jnp.zeros_like(accout_ref)
        acct_ref[...] = jnp.zeros_like(acct_ref)

    normed_two, inverse_two = norm_stats(summed_two_ref[...])
    normed_two_ref[...] = normed_two
    hidden_two = normed_two * vrow(table_ref, CROSS_G) + vrow(table_ref, CROSS_S)
    hidden_ref[...] = hidden_two
    low_two_ref[...] = hidden_two.astype(BF16)
    accum_ref[...] = jnp.zeros_like(accum_ref)

    def expand(chunk):
        units = slice(chunk * 512, chunk * 512 + 512)
        return mm_nt(low_two_ref[...], win_ref[units, :]) + table_ref[FFN_BI + chunk : FFN_BI + chunk + 1, :]

    def bend(chunk, expanded):
        units = slice(chunk * 512, chunk * 512 + 512)
        square = expanded * expanded
        bent = jnp.tanh(expanded * (GELU_A + (GELU_A * GELU_B) * square))
        half = 0.5 * bent + 0.5
        active = expanded * half
        active_ref[:, units] = active.astype(BF16)
        slope = half + (active * (1.0 - half)) * (2.0 * GELU_A + (6.0 * GELU_A * GELU_B) * square)
        slope_ref[:, units] = slope.astype(BF16)

    ahead = expand(0)
    for chunk in range(chunks):
        expanded = ahead
        if chunk + 1 < chunks:
            ahead = expand(chunk + 1)
        bend(chunk, expanded)
    contracted = mm_nt(active_ref[...], wout_ref[...])
    normed_three, inverse_three = norm_stats(
        hidden_ref[...] + contracted + vrow(table_ref, FFN_BO)
    )
    result = normed_three * vrow(table_ref, FFN_G) + vrow(table_ref, FFN_S)
    result_ref[...] = result.astype(BF16)

    upstream = upstream_ref[...].astype(F32)
    add_row(acct_ref, FFN_G, column_sum(upstream * normed_three))
    add_row(acct_ref, FFN_S, column_sum(upstream))
    sum_three = norm_back(upstream, normed_three, inverse_three, vrow(table_ref, FFN_G))
    grad_low_ref[...] = sum_three.astype(BF16)
    add_row(acct_ref, FFN_BO, column_sum(grad_low_ref[...]))
    accum_ref[...] = sum_three

    grad_three = grad_low_ref[...]
    for chunk in range(chunks):
        units = slice(chunk * 512, chunk * 512 + 512)
        grad_active = mm_nn(grad_three, wout_ref[:, units])
        accout_ref[:, units] += mm_tn(grad_three, active_ref[:, units])
        grad_expanded = (grad_active * slope_ref[:, units].astype(F32)).astype(BF16)
        slope_ref[:, units] = grad_expanded
        acct_ref[FFN_BI + chunk : FFN_BI + chunk + 1, :] += column_sum(grad_expanded)
        accin_ref[units, :] += mm_tn(grad_expanded, low_two_ref[...])
    accum_ref[...] += mm_nn(slope_ref[...], win_ref[...])
    grad_hidden_two = accum_ref[...]
    normed_two = normed_two_ref[...]
    add_row(acct_ref, CROSS_G, column_sum(grad_hidden_two * normed_two))
    add_row(acct_ref, CROSS_S, column_sum(grad_hidden_two))
    sum_two_ref[...] = norm_back(grad_hidden_two, normed_two, inverse_two, vrow(table_ref, CROSS_G))

    @pl.when(step == pl.num_programs(0) - 1)
    def _():
        dwin_ref[...] = accin_ref[...].astype(BF16)
        dwout_ref[...] = accout_ref[...].astype(BF16)
        dtable_ref[...] = acct_ref[...]


def cross_backward(
    step, sum_two_ref, summed_one_ref, remote_ref, mixture_ref, query_ref, keys_ref, values_ref, shares_ref,
    weight_ref, table_ref, first_mixture_ref, sum_one_ref, up_ref, gq_ref, gk_ref, gv_ref,
    acc_ref, acc_out_ref, acct_ref,
):
    slots = shares_ref.shape[1]
    block = tokens_of(step, STEP_ROWS * slots)
    grad_two = sum_two_ref[...].astype(BF16)
    add_row(acct_ref, CROSS_BO, column_sum(grad_two))
    up_ref[...] = mm_nn(grad_two, square(weight_ref, 3)).astype(BF16)
    acc_ref[3] += mm_tn(grad_two, mixture_ref[...])
    def one_row(row, carry):
        attend_rows_back(
            up_ref, query_ref, keys_ref, values_ref, shares_ref, gq_ref, gk_ref, gv_ref, row,
            tokens_of(row, slots), tokens_of(step * STEP_ROWS + row, slots))
        return carry
    lax.fori_loop(0, STEP_ROWS, one_row, 0)
    normed_one, inverse_one = norm_stats(summed_one_ref[...])
    low = (normed_one * vrow(table_ref, SELF_G) + vrow(table_ref, SELF_S)).astype(BF16)
    grad_query, grad_keys, grad_values = gq_ref[block, :], gk_ref[block, :], gv_ref[block, :]
    add_row(acct_ref, CROSS_BQ, column_sum(grad_query))
    add_row(acct_ref, CROSS_BV, column_sum(grad_values))
    grad_hidden_one = sum_two_ref[...] + mm_nn(grad_query, square(weight_ref, 0))
    add_row(acct_ref, SELF_G, column_sum(grad_hidden_one * normed_one))
    add_row(acct_ref, SELF_S, column_sum(grad_hidden_one))
    sum_one = norm_back(grad_hidden_one, normed_one, inverse_one, vrow(table_ref, SELF_G))
    sum_one_ref[...] = sum_one
    acc_ref[0] += mm_tn(grad_query, low)
    acc_ref[1] += mm_tn(grad_keys, remote_ref[...])
    acc_ref[2] += mm_tn(grad_values, remote_ref[...])
    grad_one = sum_one.astype(BF16)
    add_row(acct_ref, SELF_BO, column_sum(grad_one))
    acc_out_ref[0] += mm_tn(grad_one, first_mixture_ref[...])


def self_backward(
    step, sum_one_ref, query_ref, keys_ref, values_ref, shares_ref, weight_ref,
    up_ref, gq_ref, gk_ref, gv_ref, acct_ref,
):
    slots = shares_ref.shape[1]
    block = tokens_of(step, STEP_ROWS * slots)
    up_ref[...] = mm_nn(sum_one_ref[...].astype(BF16), square(weight_ref, 3)).astype(BF16)
    def one_row(row, carry):
        attend_rows_back(
            up_ref, query_ref, keys_ref, values_ref, shares_ref, gq_ref, gk_ref, gv_ref, row,
            tokens_of(row, slots), tokens_of(step * STEP_ROWS + row, slots))
        return carry
    lax.fori_loop(0, STEP_ROWS, one_row, 0)
    add_row(acct_ref, SELF_BQ, column_sum(gq_ref[block, :]))
    add_row(acct_ref, SELF_BV, column_sum(gv_ref[block, :]))


class Scatter:
    def __init__(self, theirs, halves, bufs, units, sems, base):
        self.theirs, self.halves, self.units = theirs, halves, units
        self.total, self.pair, self.far, self.near = bufs
        self.local, self.send, self.recv = sems
        self.base = base

    def copy(self, slot, source, target, partner):
        at = self.base + slot
        return pltpu.make_async_remote_copy(
            src_ref=source, dst_ref=target, send_sem=self.send.at[at], recv_sem=self.recv.at[at],
            device_id=partner, device_id_type=MESH)

    def hops(self, stage, incoming=False):
        z, y, x, core = place()
        if stage == 0:
            return [self.copy(0, self.theirs, self.pair, device(z, y, x, 1 - core))]
        sides = ((y, 1 - x), (1 - y, x))
        if stage == 1:
            return [
                self.copy(1 + i, self.total.at[h[0], :, 1 - y, 1 - x, h[1], h[2]], self.far.at[i], device(z, *side, core))
                for i, (side, h) in enumerate(zip(sides, self.halves))
            ]
        if stage == 2:
            return [
                self.copy(3 + i, self.total.at[:, :, side[0], side[1]], self.near.at[i], device(z, *side, core))
                for i, side in enumerate(sides)
            ]
        found = []
        for step in (1, 2, 3):
            other = lax.rem(z + step, 4)
            found.append(self.copy(4 + step, self.total.at[:, other, y, x], self.units.at[step], device(other, y, x, core)))
        return found

    def own(self):
        z, y, x, _ = place()
        return pltpu.make_async_copy(self.total.at[:, z, y, x], self.units.at[0], self.local.at[self.base])

    def divide(self, mat, ref, index):
        _, _, _, core = place()
        self.theirs[mat] = ref[index, :, :, :, 1 - core].astype(BF16)
        self.total[mat] = ref[index, :, :, :, core].astype(BF16)

    def start(self, stage):
        for hop in self.hops(stage):
            hop.start()
        if stage == 3:
            self.own().start()

    def arrive(self, stage):
        for hop in self.hops(stage):
            hop.wait_recv()
        z, y, x, core = place()
        if stage == 0:
            for mat in range(self.total.shape[0]):
                self.total[mat] = (self.total[mat].astype(F32) + self.pair[mat].astype(F32)).astype(BF16)
        if stage == 1:
            for i, (h, at) in enumerate(zip(self.halves, ((1 - y, x), (y, 1 - x)))):
                old = self.total[h[0], :, at[0], at[1], h[1], h[2]].astype(F32)
                self.total[h[0], :, at[0], at[1], h[1], h[2]] = (old + self.far[i].astype(F32)).astype(BF16)
        if stage == 2:
            old = self.total[:, :, y, x].astype(F32)
            self.total[:, :, y, x] = (
                old + self.near[0].astype(F32) + self.near[1].astype(F32)).astype(BF16)

    def finish(self):
        for stage in range(4):
            for hop in self.hops(stage):
                hop.wait_send()
        self.own().wait()


SCATTER_SLOTS = 8


def last_kernel(scatters, steps, *refs):
    step = pl.program_id(0)
    (sum_two_ref, s1_ref, remote_ref, m2_ref, q2_ref, k2_ref, v2_ref, shares_ref, m1_ref,
     source_ref, q1_ref, k1_ref, v1_ref, ws_ref, wc_ref, table_ref), refs = refs[:16], refs[16:]
    if scatters:
        (dwin, dwout, dtable_in), refs = refs[:3], refs[3:]
    (grad_remote_out, grad_source_out), refs = refs[:2], refs[2:]
    if scatters:
        units, refs = refs[:8], refs[8:]
    else:
        (dself_ref, dcross_ref, dtable_ref), refs = refs[:3], refs[3:]
    (up_ref, gq_ref, gk_ref, gv_ref, gk2_ref, gv2_ref, keep_ref, acco_ref, accc_ref, acct_ref, out_sem), refs = (
        refs[:11], refs[11:])
    if scatters:
        (halfc_ref, halfo_ref, halfq_ref, halfk_ref, halfv_ref, halft_ref, low_ref, lowt_ref), refs = refs[:8], refs[8:]
        bufs = [refs[4 * i : 4 * i + 4] for i in range(8)]
        sems = refs[32:]
        local = sems[0]
        lanes = lambda n: ((ALL, ALL, slice(0, n)), (ALL, ALL, slice(n, 2 * n)))
        mats = ((slice(0, 2), ALL, ALL), (slice(2, 4), ALL, ALL))
        rows = ((ALL, slice(0, 32), ALL), (ALL, slice(32, 64), ALL))
        core = lax.axis_index("fsdp") % 2
        plans = [
            (dwin.at[:, :, :, :, 1 - core], rows), (dwout.at[:, :, :, :, 1 - core], lanes(1024)), (halfc_ref, mats),
            (halfo_ref, lanes(256)), (halfq_ref, lanes(256)), (halfk_ref, lanes(256)), (halfv_ref, lanes(256)),
            (halft_ref, lanes(128)),
        ]
        everything = [
            Scatter(theirs, halves, bufs[i], units[i], sems, i * SCATTER_SLOTS)
            for i, (theirs, halves) in enumerate(plans)
        ]
        inner, outer, cross, mixed, query, keys, values, small = everything
        fetch = [
            pltpu.make_async_copy(dwin.at[:, :, :, :, core], bufs[0][0], local.at[1]),
            pltpu.make_async_copy(dwout.at[:, :, :, :, core], bufs[1][0], local.at[2]),
        ]

    @pl.when(step == 0)
    def _():
        if scatters:
            hail()
        acco_ref[...] = jnp.zeros_like(acco_ref)
        accc_ref[...] = jnp.zeros_like(accc_ref)
        acct_ref[...] = jnp.zeros_like(acct_ref)
        if scatters:
            await_hails()
            inner.start(0)
            outer.start(0)
            for copy in fetch:
                copy.start()

    @pl.when(step < steps)
    def _():
        cross_backward(
            step, sum_two_ref, s1_ref, remote_ref, m2_ref, q2_ref, k2_ref, v2_ref, shares_ref, wc_ref, table_ref, m1_ref,
            keep_ref.at[step], up_ref, gq_ref, gk2_ref, gv2_ref, Flat(accc_ref), Flat(acco_ref), acct_ref)

    @pl.when((step >= steps) & (step < 2 * steps))
    def _():
        self_backward(
            step - steps, keep_ref.at[step - steps], q1_ref, k1_ref, v1_ref, shares_ref, ws_ref,
            up_ref, gq_ref, gk_ref, gv_ref, acct_ref)

    tokens = source_ref.shape[0]

    def weight_grad(ref):
        return mm_tn(ref[...], source_ref[...]).astype(BF16)

    def source_grad(block):
        at = tokens_of(block, tokens // steps)
        found = (
            keep_ref[block]
            + mm_nn(gq_ref[at, :], square(ws_ref, 0))
            + mm_nn(gk_ref[at, :], square(ws_ref, 1))
            + mm_nn(gv_ref[at, :], square(ws_ref, 2))
        )
        gq_ref[at, :] = found.astype(BF16)
        copy = pltpu.make_async_copy(gq_ref.at[at, :], grad_source_out.at[at, :], out_sem.at[block])
        copy.start()
        return copy

    def remote_grad(block):
        at = tokens_of(block, tokens // steps)
        found = mm_nn(gk2_ref[at, :], square(wc_ref, 1)) + mm_nn(gv2_ref[at, :], square(wc_ref, 2))
        gk2_ref[at, :] = found.astype(BF16)
        copy = pltpu.make_async_copy(gk2_ref.at[at, :], grad_remote_out.at[at, :], out_sem.at[steps + block])
        copy.start()
        return copy

    if not scatters:
        @pl.when(step == 2 * steps)
        def _():
            for index, ref in enumerate((gq_ref, gk_ref, gv_ref)):
                dself_ref[index] = weight_grad(ref).reshape(dself_ref.shape[1:])
            dself_ref[3] = acco_ref[0].astype(BF16)
            dcross_ref[...] = accc_ref[...].astype(BF16)
            dtable_ref[...] = acct_ref[...]
            copies = [source_grad(block) for block in range(steps)] + [remote_grad(block) for block in range(steps)]
            for copy in copies:
                copy.wait()
        return

    def move(piece, stage):
        piece.arrive(stage)
        piece.start(stage + 1)

    @pl.when(step == 1)
    def _():
        for copy in fetch:
            copy.wait()
        move(inner, 0)
        move(outer, 0)

    @pl.when(step == steps - 2)
    def _():
        move(inner, 1)
        move(outer, 1)

    @pl.when(step == steps - 1)
    def _():
        for mat in range(4):
            cross.divide(mat, accc_ref, mat)
        mixed.divide(0, acco_ref, 0)
        cross.start(0)
        mixed.start(0)

    @pl.when(step == steps)
    def _():
        move(inner, 2)
        move(outer, 2)
        move(cross, 0)
        move(mixed, 0)

    @pl.when(step == steps + 1)
    def _():
        move(cross, 1)
        move(mixed, 1)

    @pl.when(step == 2 * steps - 1)
    def _():
        move(cross, 2)
        move(mixed, 2)

    @pl.when(step == 2 * steps)
    def _():
        low_ref[0] = weight_grad(gq_ref).reshape(low_ref.shape[1:])
        query.divide(0, low_ref, 0)
        query.start(0)
        low_ref[0] = weight_grad(gk_ref).reshape(low_ref.shape[1:])
        keys.divide(0, low_ref, 0)
        keys.start(0)
        table = columns_from_table(acct_ref[...] + dtable_in[...]).astype(BF16)
        lowt_ref[...] = table.reshape(lowt_ref.shape)
        small.divide(0, lowt_ref, 0)
        small.start(0)
        move(query, 0)
        low_ref[0] = weight_grad(gv_ref).reshape(low_ref.shape[1:])
        values.divide(0, low_ref, 0)
        values.start(0)
        move(keys, 0)
        move(small, 0)
        copies = [source_grad(0)]
        move(query, 1)
        move(values, 0)
        copies.append(source_grad(1))
        move(keys, 1)
        move(small, 1)
        copies.append(source_grad(2))
        move(values, 1)
        move(query, 2)
        copies.append(source_grad(3))
        copies.append(remote_grad(0))
        move(keys, 2)
        move(small, 2)
        copies.append(remote_grad(1))
        move(values, 2)
        copies.append(remote_grad(2))
        copies.append(remote_grad(3))
        for piece in everything:
            piece.arrive(3)
        for piece in everything:
            piece.finish()
        for copy in copies:
            copy.wait()


class Flat:
    def __init__(self, ref):
        self.ref = ref

    def __getitem__(self, index):
        return self.ref[index].reshape(512, 512)

    def __setitem__(self, index, values):
        self.ref[index] = values.reshape(self.ref.shape[1:])


def sum_kernel(*refs):
    units, (remote_in, source_in), refs = refs[:8], refs[8:10], refs[10:]
    (qkv, bias_one, out_one, norm_one, cross_q, cross_kv, bias_two, out_two, norm_two,
     win, win_bias, wout, wout_bias, norm_three, remote_out, source_out), refs = refs[:16], refs[16:]
    held, sems = refs[:10], refs[10]
    copies = [
        pltpu.make_async_copy(ref, buf, sems.at[i])
        for i, (ref, buf) in enumerate(zip((*units, remote_in, source_in), held))
    ]
    for copy in copies:
        copy.start()
    for copy in copies[:8]:
        copy.wait()
    total = lambda ref: (
        ref[0].astype(F32) + ref[1].astype(F32) + ref[2].astype(F32) + ref[3].astype(F32))
    win[...] = total(held[0])[0]
    wout[...] = total(held[1])[0]
    cross = total(held[2])
    cross_q[...] = cross[0]
    cross_kv[...] = cross[1:3]
    out_two[...] = cross[3]
    out_one[...] = total(held[3])[0]
    for index in range(3):
        qkv[index] = total(held[4 + index])[0]
    small = jnp.transpose(total(held[7])[0])
    bias_one[...] = small[SELF_BQ : SELF_BQ + 3]
    norm_one[...] = small[SELF_G : SELF_G + 2]
    bias_two[...] = small[CROSS_BQ : CROSS_BQ + 3]
    norm_two[...] = small[CROSS_G : CROSS_G + 2]
    wout_bias[...] = small[FFN_BO : FFN_BO + 1]
    norm_three[...] = small[FFN_G : FFN_G + 2]
    win_bias[...] = small[128:132]
    leaving = [
        pltpu.make_async_copy(buf, ref, sems.at[10 + i])
        for i, (ref, buf) in enumerate(zip((remote_out, source_out), held[8:]))
    ]
    for arrived, copy in zip(copies[8:], leaving):
        arrived.wait()
        copy.start()
    for copy in leaving:
        copy.wait()


def fixed(shape):
    return pl.BlockSpec(shape, lambda i: (0,) * len(shape), pipeline_mode=pl.Buffered(1))


def shape_of(*shape, dtype=BF16):
    return jax.ShapeDtypeStruct(shape, dtype)


def params(limit, collective=None):
    if collective is None:
        return pltpu.CompilerParams(vmem_limit_bytes=limit, dimension_semantics=("arbitrary",))
    return pltpu.CompilerParams(
        vmem_limit_bytes=limit, dimension_semantics=("arbitrary",), collective_id=collective,
        has_side_effects=True)


ANYWHERE = pl.BlockSpec(memory_space=pl.ANY)
SQUARES = (4,) + BLOCKS + (16, 512)
WIN_BLOCKS = (1,) + BLOCKS + (64, 512)
WOUT_BLOCKS = (1,) + BLOCKS + (16, 2048)
SMALL_BLOCKS = (1,) + BLOCKS + (16, 256)


ONE_BLOCKS = (1,) + BLOCKS + (16, 512)


def layer(decoder_in, memory, out_grad, tgt_len, src_len, shards=None, weights=None):
    rows, slots, width = decoder_in.shape
    tokens = rows * slots
    block = STEP_ROWS * slots
    steps = rows // STEP_ROWS
    shares_block = (STEP_ROWS * HEADS, slots, slots)
    source = decoder_in.reshape(tokens, width)
    remote = memory.reshape(tokens, width)
    low, full = shape_of(tokens, width), shape_of(tokens, width, dtype=F32)
    vm = pltpu.VMEM
    dma = pltpu.SemaphoreType.DMA
    part = lambda first: (lambda i: jnp.clip(i - first, 0, steps - 1))
    tok = lambda when: pl.BlockSpec((block, width), lambda i: (when(i), 0))
    shares = lambda when: pl.BlockSpec(shares_block, lambda i: (when(i), 0, 0))
    shares_shape = shape_of(2 * rows * HEADS, slots, slots)
    table_shape = shape_of(TABLE, width, dtype=F32)
    table_spec = fixed((TABLE, width))
    ins = [source, remote, tgt_len, src_len]
    early, late = part(1), part(1 + steps)
    in_specs = [fixed(source.shape), tok(late), fixed(tgt_len.shape), fixed(src_len.shape)]
    out_shape = [low, low, low, low, full] * 2 + [shares_shape]
    out_specs = [ANYWHERE] * 3 + [tok(early)] * 2 + [tok(late)] * 5
    out_specs += [shares(lambda i: jnp.clip(i - 1, 0, 2 * steps - 1))]
    scratch = []
    if shards is not None:
        big, small = shards
        ins += [*big, *small]
        in_specs += [ANYWHERE] * 7 + [fixed(array.shape) for array in small]
        out_shape += [table_shape, shape_of(*SQUARES), shape_of(*SQUARES), shape_of(*WIN_BLOCKS), shape_of(*WOUT_BLOCKS)]
        out_specs += [table_spec] + [ANYWHERE] * 4
        scratch += [vm(SQUARES, BF16), vm(SQUARES, BF16), vm(SMALL_BLOCKS, BF16), vm((1, 16, 256), BF16), vm((256, 128), F32)]
        scratch += [dma((GATHER_SLOTS,)), dma((GATHER_SLOTS,)), dma((GATHER_SLOTS,))]
    else:
        ws, wc, win, wout, table = weights
        ws, wc = ws.reshape(SQUARES), wc.reshape(SQUARES)
        ins += [ws, wc, table]
        in_specs += [fixed(SQUARES), fixed(SQUARES), table_spec]
    scratch += [vm((2, rows, slots, slots), F32), vm((block, width), F32), vm((steps, block, width), F32), vm((rows, 2, slots), F32)]
    scratch += [vm((tokens, width), BF16)] * 3 + [dma((5,))]
    outs = pl.pallas_call(
        functools.partial(first_kernel, shards is not None, steps),
        grid=(1 + 2 * steps,), in_specs=in_specs, out_specs=out_specs, out_shape=out_shape, scratch_shapes=scratch,
        compiler_params=params(60 << 20, None if shards is None else 1), name="first",
    )(*ins)
    q1, k1, v1, m1, s1, q2, k2, v2, m2, s2, both = outs[:FIRST_OUT]
    if shards is not None:
        table, ws, wc, win, wout = outs[FIRST_OUT:]
        win = win.reshape(-1, width)
        wout = wout.reshape(width, -1)
    hidden = win.shape[0]
    now = part(0)
    result, sum_two, dwin, dwout, dtable = pl.pallas_call(
        ffn_kernel,
        grid=(steps,),
        in_specs=[tok(now), tok(now), fixed(win.shape), fixed(wout.shape), table_spec],
        out_specs=[tok(now), tok(now), fixed(win.shape), fixed(wout.shape), table_spec],
        out_shape=[low, full, shape_of(*win.shape), shape_of(*wout.shape), table_shape],
        scratch_shapes=[
            vm((block, width), F32), vm((block, width), F32), vm((block, hidden), BF16), vm((block, hidden), BF16),
            vm((block, width), F32), vm((block, width), BF16), vm((block, width), BF16),
            vm(win.shape, F32), vm(wout.shape, F32), vm((TABLE, width), F32),
        ],
        compiler_params=params(60 << 20), name="feed_forward",
    )(s2, out_grad.reshape(tokens, width), win, wout, table)

    early, late = part(0), part(steps)
    ins = [sum_two, s1, remote, m2, q2, k2, v2, both, m1, source, q1, k1, v1, ws, wc, table]
    in_specs = [tok(early)] * 7 + [shares(lambda i: jnp.where(i < steps, i + steps, jnp.minimum(i - steps, steps - 1)))]
    in_specs += [tok(early), fixed(source.shape)] + [tok(late)] * 3
    in_specs += [fixed(SQUARES), fixed(SQUARES), table_spec]
    out_shape, out_specs = [low, low], [ANYWHERE, ANYWHERE]
    scratch = [vm((block, width), BF16)] + [vm((tokens, width), BF16)] * 5 + [
        vm((steps, block, width), F32), vm(ONE_BLOCKS, F32), vm(SQUARES, F32), vm((TABLE, width), F32), dma((2 * steps,))]
    if shards is not None:
        ins += [dwin.reshape(WIN_BLOCKS), dwout.reshape(WOUT_BLOCKS), dtable]
        in_specs += [ANYWHERE, ANYWHERE, table_spec]
        every = (WIN_BLOCKS, WOUT_BLOCKS, SQUARES, ONE_BLOCKS, ONE_BLOCKS, ONE_BLOCKS, ONE_BLOCKS, SMALL_BLOCKS)
        unit_shapes = [(4, s[0], s[5], s[6]) for s in every]
        out_shape += [shape_of(*s) for s in unit_shapes]
        out_specs += [ANYWHERE] * 8
        scratch += [vm(s[:4] + s[5:], BF16) for s in every[2:]]
        scratch += [vm(ONE_BLOCKS, BF16), vm(SMALL_BLOCKS, BF16)]
        cut = ((1, 2, 1), (1, 1, 2), (2, 1, 1)) + ((1, 1, 2),) * 5
        for s, (m, r, l) in zip(every, cut):
            scratch += [
                vm(s[:4] + s[5:], BF16), vm(s[:4] + s[5:], BF16),
                vm((2, s[0] // m, 4, s[5] // r, s[6] // l), BF16), vm((2, s[0], 4, s[5], s[6]), BF16)]
        scratch += [dma((8 * SCATTER_SLOTS,))] * 3
    else:
        out_shape += [shape_of(*SQUARES), shape_of(*SQUARES), table_shape]
        out_specs += [fixed(SQUARES), fixed(SQUARES), table_spec]
    grad_remote, grad_source, *tail = pl.pallas_call(
        functools.partial(last_kernel, shards is not None, steps),
        grid=(2 * steps + 1,), in_specs=in_specs, out_specs=out_specs, out_shape=out_shape, scratch_shapes=scratch,
        compiler_params=params(63 << 20, None if shards is None else 2), name="last",
    )(*ins)
    as_rows = lambda array: array.reshape(rows, slots, width)
    if shards is None:
        dself, dcross, dtable_last = tail
        grads = (dself.reshape(4, 512, 512), dcross.reshape(4, 512, 512), dwin, dwout, dtable + dtable_last)
    else:
        f = lambda *shape: shape_of(*shape, dtype=F32)
        in_vm = pl.BlockSpec(memory_space=pltpu.VMEM)
        *grads, grad_remote, grad_source = pl.pallas_call(
            sum_kernel,
            in_specs=[pl.BlockSpec(memory_space=pltpu.HBM)] * 10,
            out_specs=[in_vm] * 14 + [pl.BlockSpec(memory_space=pltpu.HBM)] * 2,
            out_shape=[f(3, 16, 512), f(3, 16), f(16, 512), f(2, 16), f(16, 512), f(2, 16, 512), f(3, 16), f(16, 512),
                       f(2, 16), f(64, 512), f(4, 16), f(16, 2048), f(1, 16), f(2, 16), low, low],
            scratch_shapes=[vm(s, BF16) for s in unit_shapes] + [vm((tokens, width), BF16)] * 2 + [dma((12,))],
            compiler_params=pltpu.CompilerParams(vmem_limit_bytes=63 << 20), name="sum_planes",
        )(*tail, grad_remote, grad_source)
    return as_rows(result), as_rows(grad_source), as_rows(grad_remote), grads


def turn(array):
    return jnp.swapaxes(array, -1, -2)


AXES = ("dp", "fsdp")


def gather_plain(parts, count):
    (self_qkv, self_bias, self_out, self_norm, cross_q, cross_kv, cross_bias, cross_out, cross_norm,
     ffn_in, ffn_in_bias, ffn_out, ffn_out_bias, ffn_norm) = parts
    cols = self_out.shape[1]
    width = self_out.shape[0]
    chunks = ffn_out.shape[0] // width
    small = jnp.concatenate(
        [self_bias, self_norm, cross_bias, cross_norm, ffn_out_bias[None], ffn_norm,
         ffn_in_bias.reshape(chunks, cols)], axis=0)
    small = jnp.pad(turn(small), ((0, 0), (0, width - small.shape[0])))
    packed = jnp.concatenate([
        turn(self_qkv).reshape(-1, width), turn(self_out), turn(cross_q),
        turn(cross_kv).reshape(-1, width), turn(cross_out), turn(ffn_in),
        turn(ffn_out).reshape(cols, chunks, width).swapaxes(0, 1).reshape(-1, width), small], axis=0)
    whole_set = lax.all_gather(packed, AXES, axis=0, tiled=False)
    square = whole_set[:, : 8 * cols].reshape(count, 8, cols, width).swapaxes(0, 1)
    square = square.reshape(8, width, width)
    low = 8 * cols
    win = whole_set[:, low : low + chunks * cols].reshape(chunks * width, width)
    low += chunks * cols
    wout = whole_set[:, low : low + chunks * cols].reshape(count, chunks, cols, width)
    wout = wout.transpose(0, 2, 1, 3).reshape(width, chunks * width)
    low += chunks * cols
    table = whole_set[:, low:]
    first = table[:, :, :13].transpose(2, 0, 1).reshape(13, width)
    second = table[:, :, 13 : 13 + chunks].transpose(0, 2, 1).reshape(chunks, width)
    table = jnp.concatenate([first, second], axis=0).astype(F32)
    table = jnp.pad(table, ((0, TABLE - table.shape[0]), (0, 0)))
    return square[:4], square[4:], win, wout, table


def scatter_plain(dself, dcross, dwin, dwout, dtable, count):
    width = dself.shape[1]
    cols = width // count
    chunks = dwin.shape[0] // width
    squares = jnp.concatenate([dself, dcross], axis=0).reshape(8, count, cols, width).swapaxes(0, 1)
    first = dtable[:13].reshape(13, count, cols).transpose(1, 2, 0)
    second = dtable[13 : 13 + chunks].reshape(count, chunks, cols).transpose(0, 2, 1)
    small = jnp.concatenate([first, second], axis=2)
    small = jnp.pad(small, ((0, 0), (0, 0), (0, width - small.shape[2]))).astype(BF16)
    packed = jnp.concatenate([
        squares.reshape(count, 8 * cols, width), dwin.reshape(count, chunks * cols, width),
        dwout.reshape(count, cols, chunks, width).swapaxes(1, 2).reshape(count, -1, width), small],
        axis=1)
    mine = lax.psum_scatter(packed, AXES, scatter_dimension=0, tiled=False).astype(F32)
    square = turn(mine[: 8 * cols].reshape(8, cols, width))
    low = 8 * cols
    ffn_in = turn(mine[low : low + chunks * cols])
    low += chunks * cols
    ffn_out = mine[low : low + chunks * cols].reshape(chunks, cols, width).swapaxes(0, 1)
    ffn_out = turn(ffn_out.reshape(cols, chunks * width))
    low += chunks * cols
    small = turn(mine[low:, : 13 + chunks])
    return (square[:3], small[0:3], square[3], small[3:5], square[4], square[5:7], small[5:8], square[7],
            small[8:10], ffn_in, small[13:].reshape(-1), ffn_out, small[10], small[11:13])


def on_device(count, direct, decoder_in, memory, out_grad, tgt_len, src_len, *parts):
    if not direct:
        weights = gather_plain(parts, count)
        result, grad_source, grad_remote, grads = layer(
            decoder_in, memory, out_grad, tgt_len, src_len, weights=weights)
        return (result, grad_source, grad_remote, *scatter_plain(*grads, count))
    (self_qkv, self_bias, self_out, self_norm, cross_q, cross_kv, cross_bias, cross_out, cross_norm,
     ffn_in, ffn_in_bias, ffn_out, ffn_out_bias, ffn_norm) = parts
    big = [turn(part) for part in (self_qkv, self_out, cross_q, cross_kv, cross_out, ffn_in, ffn_out)]
    big = [part.reshape((-1,) + part.shape[-2:]) for part in big]
    small = [self_bias, self_norm, cross_bias, cross_norm, ffn_out_bias.reshape(1, -1), ffn_norm, ffn_in_bias.reshape(1, -1)]
    shards = big, small
    result, grad_source, grad_remote, grads = layer(
        decoder_in, memory, out_grad, tgt_len, src_len, shards=shards)
    (qkv, bias_one, out_one, norm_one, query, pair, bias_two, out_two, norm_two, win, win_bias, wout, wout_bias,
     norm_three) = grads
    return (result, grad_source, grad_remote, turn(qkv), bias_one, turn(out_one), norm_one, turn(query), turn(pair),
            bias_two, turn(out_two), norm_two, turn(win), win_bias.reshape(-1), turn(wout), wout_bias.reshape(-1),
            norm_three)


def solution(mesh):
    count = mesh.shape["dp"] * mesh.shape["fsdp"]
    direct = mesh.shape["dp"] == 4 and mesh.shape["fsdp"] == 8
    rows = P(AXES, None, None)
    lens = P(AXES, None)
    cube = P(None, None, AXES)
    flat = P(None, AXES)
    line = P(AXES)
    params_in = (cube, flat, flat, flat, flat, cube, flat, flat, flat, flat, line, flat, line, flat)
    return jax.shard_map(
        functools.partial(on_device, count, direct),
        mesh=mesh,
        in_specs=(rows, rows, rows, lens, lens) + params_in,
        out_specs=(rows, rows, rows) + params_in,
        check_vma=False,
    )
```

```python
import functools

import jax
import jax.numpy as jnp
from jax import lax
from jax.experimental import pallas as pl
from jax.experimental.pallas import tpu as pltpu
from jax.sharding import PartitionSpec as P

F32 = jnp.float32
BF16 = jnp.bfloat16
EPS = 1e-05
MASKED = -1e30
HEADS = 8
HEAD_DIM = 64
PAIR = 128
QUAD = 256
GELU_A = 0.7978845608028654
GELU_B = 0.044715


def mm(left, right, left_dim, right_dim):
    return lax.dot_general(
        left, right, (((left_dim,), (right_dim,)), ((), ())), preferred_element_type=F32
    )


def mm_nt(left, right):
    return mm(left, right, 1, 1)


def mm_nn(left, right):
    return mm(left, right, 1, 0)


def mm_tn(left, right):
    return mm(left, right, 0, 0)


def norm_stats(summed):
    centred = summed - jnp.mean(summed, axis=-1, keepdims=True)
    inverse = lax.rsqrt(jnp.mean(centred * centred, axis=-1, keepdims=True) + EPS)
    return centred * inverse, inverse


def norm_back(upstream, normed, inverse, gain):
    scaled = upstream * gain
    mean_scaled = jnp.mean(scaled, axis=-1, keepdims=True)
    mean_product = jnp.mean(scaled * normed, axis=-1, keepdims=True)
    return (scaled - mean_scaled - normed * mean_product) * inverse


def column_sum(values):
    return jnp.sum(values.astype(F32), axis=0, keepdims=True)


def lane_band(width, head):
    lane = lax.broadcasted_iota(jnp.int32, (1, width), 1)
    return (lane >= head * HEAD_DIM) & (lane < (head + 1) * HEAD_DIM)


def keep_head(values, head):
    return jnp.where(lane_band(values.shape[1], head), values, jnp.zeros_like(values))


def mask_bias(key_ids, query_ids, causal):
    slots = key_ids.shape[1]
    down = jnp.transpose(jnp.broadcast_to(key_ids, (slots, slots)))
    allowed = down == query_ids
    if causal:
        key_at = lax.broadcasted_iota(jnp.int32, (slots, slots), 0)
        query_at = lax.broadcasted_iota(jnp.int32, (slots, slots), 1)
        allowed = allowed & (key_at <= query_at)
    return jnp.where(allowed, 0.0, MASKED).astype(F32)


def attend_rows(query_ref, keys_ref, values_ref, bias_ref, shares_ref, mixture_ref, row, at, into):
    for quad in range(HEADS * HEAD_DIM // QUAD):
        lanes = slice(quad * QUAD, (quad + 1) * QUAD)
        values_quad = values_ref[at, lanes]
        parts, wide = [], []
        for inner in range(QUAD // HEAD_DIM):
            head = quad * (QUAD // HEAD_DIM) + inner
            first = head * HEAD_DIM // PAIR * PAIR
            pair = slice(first, first + PAIR)
            keys_head = keep_head(keys_ref[at, pair], head - first // HEAD_DIM)
            scores = mm_nt(keys_head, query_ref[at, pair]) + bias_ref[...]
            top = jnp.max(scores, axis=0, keepdims=True)
            raised = jnp.exp(scores - top)
            total = jnp.sum(raised, axis=0, keepdims=True)
            shares = (raised * (1.0 / total)).astype(BF16)
            shares_ref[row * HEADS + head] = shares
            parts.append(shares)
            wide.append(keep_head(values_quad, inner))
        mixture = mm_tn(jnp.concatenate(parts, 0), jnp.concatenate(wide, 0))
        mixture_ref[into, lanes] = mixture.astype(BF16)


def attend_rows_back(
    upstream_ref, query_ref, keys_ref, values_ref, shares_ref, gq_ref, gk_ref, gv_ref, row, at, into
):
    for quad in range(HEADS * HEAD_DIM // QUAD):
        lanes = slice(quad * QUAD, (quad + 1) * QUAD)
        query_quad = query_ref[at, lanes]
        keys_quad = keys_ref[at, lanes]
        up_quad = upstream_ref[at, lanes]
        grad_query = grad_keys = grad_values = None
        for inner in range(QUAD // HEAD_DIM):
            head = quad * (QUAD // HEAD_DIM) + inner
            first = head * HEAD_DIM // PAIR * PAIR
            pair = slice(first, first + PAIR)
            values_head = keep_head(values_ref[at, pair], head - first // HEAD_DIM)
            shares = shares_ref[row * HEADS + head]
            grad_shares = mm_nt(values_head, upstream_ref[at, pair])
            wide = shares.astype(F32)
            product = wide * grad_shares
            centre = jnp.sum(product, axis=0, keepdims=True)
            grad_scores = (product - wide * centre).astype(BF16)
            one = mm_nn(grad_scores, keep_head(query_quad, inner))
            two = mm_nn(shares, keep_head(up_quad, inner))
            three = mm_tn(grad_scores, keep_head(keys_quad, inner))
            grad_keys = one if grad_keys is None else grad_keys + one
            grad_values = two if grad_values is None else grad_values + two
            grad_query = three if grad_query is None else grad_query + three
        gq_ref[into, lanes] = (grad_query * HEAD_DIM**-0.5).astype(BF16)
        gk_ref[into, lanes] = grad_keys.astype(BF16)
        gv_ref[into, lanes] = grad_values.astype(BF16)


STEP_ROWS = 2

SELF_BQ, SELF_BV, SELF_BO, SELF_G, SELF_S = 0, 1, 2, 3, 4
CROSS_BQ, CROSS_BV, CROSS_BO, CROSS_G, CROSS_S = 5, 6, 7, 8, 9
FFN_BO, FFN_G, FFN_S, FFN_BI = 10, 11, 12, 13
TABLE = 24


def vrow(table_ref, index):
    return table_ref[index : index + 1, :]


def add_row(ref, index, values):
    ref[index : index + 1, :] += values


MESH = pl.DeviceIdType.MESH
ALL = slice(None)


def place():
    z = lax.axis_index("dp")
    f = lax.axis_index("fsdp")
    return z, f // 4, (f // 2) % 2, f % 2


def device(z, y, x, core):
    return (z, y * 4 + x * 2 + core)


def partners():
    z, y, x, core = place()
    found = [device(lax.rem(z + step, 4), y, x, core) for step in (1, 2, 3)]
    return found + [device(z, y, 1 - x, core), device(z, 1 - y, x, core), device(z, y, x, 1 - core)]


def hail():
    barrier = pltpu.get_barrier_semaphore()
    for partner in partners():
        pl.semaphore_signal(barrier, inc=1, device_id=partner, device_id_type=MESH)


def await_hails():
    pl.semaphore_wait(pltpu.get_barrier_semaphore(), 6)


class Gather:
    def __init__(self, ref, own, first, second, sems, base):
        self.ref, self.own, self.first, self.second = ref, own, first, second
        self.local, self.send, self.recv = sems
        self.base = base
        self.mats = slice(min(m.start for _, m in own), max(m.stop for _, m in own))

    @staticmethod
    def slots(own):
        return 3 * len(own) + 5

    def copy(self, slot, source, target, partner):
        at = self.base + slot
        return pltpu.make_async_remote_copy(
            src_ref=source, dst_ref=target, send_sem=self.send.at[at], recv_sem=self.recv.at[at],
            device_id=partner, device_id_type=MESH)

    def at(self, half, z, y, x, core):
        mats, rows, lanes = half
        return self.ref.at[mats, z, y, x, core, rows, lanes]

    def locals(self):
        z, y, x, core = place()
        return [
            pltpu.make_async_copy(source, self.ref.at[mats, z, y, x, core], self.local.at[self.base + i])
            for i, (source, mats) in enumerate(self.own)
        ]

    def hops(self, stage, incoming):
        z, y, x, core = place()
        full = (self.mats, ALL, ALL)
        found = []
        many = len(self.own)
        if stage == 0:
            for step in (1, 2, 3):
                other = lax.rem(z + (4 - step if incoming else step), 4)
                for i, (source, mats) in enumerate(self.own):
                    target = self.ref.at[mats, other if incoming else z, y, x, core]
                    found.append(self.copy((step - 1) * many + i, source, target, device(other, y, x, core)))
        if stage == 1:
            for slot, (py, px) in enumerate(((y, 1 - x), (1 - y, x))):
                sent = self.at(full, ALL, y, x, core)
                target = self.at(full, ALL, py, px, core) if incoming else sent
                found.append(self.copy(3 * many + slot, sent, target, device(z, py, px, core)))
        if stage == 2:
            for slot, (half, by, bx, py, px) in enumerate((
                (self.first, 1 - y, x, y, 1 - x), (self.second, y, 1 - x, 1 - y, x))):
                sent = self.at(half, ALL, by, bx, core)
                target = self.at(half, ALL, 1 - y, 1 - x, core) if incoming else sent
                found.append(self.copy(3 * many + 2 + slot, sent, target, device(z, py, px, core)))
        if stage == 3:
            sent = self.at(full, ALL, ALL, ALL, core)
            target = self.at(full, ALL, ALL, ALL, 1 - core) if incoming else sent
            found.append(self.copy(3 * many + 4, sent, target, device(z, y, x, 1 - core)))
        return found

    def start(self, stage):
        for hop in self.hops(stage, False):
            hop.start()

    def arrive(self, stage):
        for hop in self.hops(stage, True):
            hop.wait_recv()

    def finish(self):
        for stage in range(4):
            for hop in self.hops(stage, False):
                hop.wait_send()


def gather_pieces(shards, targets, sems):
    qkv, out_one, cross_q, cross_kv, out_two, win, wout, small = shards
    ws, wc, win_all, wout_all, small_all = targets
    one = lambda n: slice(n, n + 1)
    lanes = lambda n: ((ALL, ALL, slice(0, n)), (ALL, ALL, slice(n, 2 * n)))
    single = lambda n: ((one(n), ALL, slice(0, 256)), (one(n), ALL, slice(256, 512)))
    plans = [
        (small_all, [(small, one(0))], *lanes(128)),
        (ws, [(qkv.at[0:1], one(0))], *single(0)),
        (ws, [(qkv.at[1:2], one(1))], *single(1)),
        (ws, [(qkv.at[2:3], one(2))], *single(2)),
        (ws, [(out_one, one(3))], *single(3)),
        (wc, [(cross_q, one(0)), (cross_kv, slice(1, 3)), (out_two, one(3))],
         (slice(0, 2), ALL, ALL), (slice(2, 4), ALL, ALL)),
        (win_all, [(win, one(0))], (ALL, slice(0, 32), ALL), (ALL, slice(32, 64), ALL)),
        (wout_all, [(wout, one(0))], *lanes(1024)),
    ]
    pieces, base = [], 0
    for ref, own, first, second in plans:
        pieces.append(Gather(ref, own, first, second, sems, base))
        base += Gather.slots(own)
    return pieces


GATHER_SLOTS = 80

BLOCKS = (4, 2, 2, 2)


def square(ref, index):
    return ref[index].reshape(512, 512)


def prepare_masks(tgt_ref, src_ref, ids_ref, bias_ref):
    rows, sents = tgt_ref.shape
    slots = ids_ref.shape[2]
    before = lax.broadcasted_iota(jnp.int32, (sents, sents), 0)
    after = lax.broadcasted_iota(jnp.int32, (sents, sents), 1)
    ladder = (before <= after).astype(F32)
    slot = lax.broadcasted_iota(jnp.int32, (sents, slots), 1).astype(F32)
    for side, ref in enumerate((tgt_ref, src_ref)):
        lengths = ref[...].astype(F32)
        finish = lax.dot_general(
            ladder, lengths, (((0,), (1,)), ((), ())),
            precision=lax.Precision.HIGHEST, preferred_element_type=F32)
        for row in range(rows):
            ended = (finish[:, row : row + 1] <= slot).astype(F32)
            ids_ref[row, side : side + 1, :] = jnp.sum(ended, axis=0, keepdims=True)

    def one_row(row, carry):
        ids = ids_ref[row]
        bias_ref[0, row] = mask_bias(ids[0:1], ids[0:1], True)
        bias_ref[1, row] = mask_bias(ids[1:2], ids[0:1], False)
        return carry

    lax.fori_loop(0, rows, one_row, 0)


def tokens_of(block, size):
    start = block * size
    return pl.ds(start if isinstance(start, int) else pl.multiple_of(start, size), size)


def self_forward(
    step, source_ref, weight_ref, table_ref, query_ref, keys_ref, values_ref,
    shares_ref, mixture_ref, summed_ref, bias_ref,
):
    slots = shares_ref.shape[1]
    block = STEP_ROWS * slots
    for row in range(STEP_ROWS):
        attend_rows(
            query_ref, keys_ref, values_ref, bias_ref.at[0, step * STEP_ROWS + row], shares_ref, mixture_ref, row,
            tokens_of(step * STEP_ROWS + row, slots), tokens_of(row, slots))
    summed_ref[...] = (
        source_ref[tokens_of(step, block), :].astype(F32)
        + mm_nt(mixture_ref[...], square(weight_ref, 3)) + vrow(table_ref, SELF_BO)
    )


def cross_forward(
    step, summed_one_ref, remote_ref, weight_ref, table_ref,
    query_ref, keys_ref, values_ref, shares_ref, mixture_ref, summed_ref, bias_ref, hidden_ref,
):
    slots = shares_ref.shape[1]
    normed_one, _ = norm_stats(summed_one_ref[...])
    hidden_one = normed_one * vrow(table_ref, SELF_G) + vrow(table_ref, SELF_S)
    hidden_ref[...] = hidden_one
    query = mm_nt(hidden_one.astype(BF16), square(weight_ref, 0)) + vrow(table_ref, CROSS_BQ)
    query_ref[...] = (query * HEAD_DIM**-0.5).astype(BF16)
    remote = remote_ref[...]
    keys_ref[...] = mm_nt(remote, square(weight_ref, 1)).astype(BF16)
    values_ref[...] = (mm_nt(remote, square(weight_ref, 2)) + vrow(table_ref, CROSS_BV)).astype(BF16)

    for row in range(STEP_ROWS):
        at = tokens_of(row, slots)
        attend_rows(
            query_ref, keys_ref, values_ref, bias_ref.at[1, step * STEP_ROWS + row], shares_ref, mixture_ref, row, at, at)
    summed_ref[...] = (
        hidden_ref[...] + mm_nt(mixture_ref[...], square(weight_ref, 3)) + vrow(table_ref, CROSS_BO)
    )


def table_from_columns(columns, table_ref):
    turned = jnp.transpose(columns[:, :128])
    table_ref[0:TABLE, :] = turned[0:TABLE]
    parts = [columns[:, 128 + k : 129 + k].reshape(32, 1, 16, 1) for k in range(4)]
    line = jnp.concatenate(parts, axis=1).reshape(2048, 1)
    line = jnp.transpose(jnp.broadcast_to(line, (2048, 128)))
    for k in range(4):
        table_ref[FFN_BI + k : FFN_BI + k + 1, :] = line[0:1, k * 512 : (k + 1) * 512]


def columns_from_table(rows):
    rows = jnp.concatenate([rows, jnp.zeros((128 - TABLE, 512), F32)], axis=0)
    columns = jnp.transpose(rows)
    lane = lax.broadcasted_iota(jnp.int32, (512, 128), 1)
    line = jnp.concatenate([columns[:, FFN_BI + k : FFN_BI + k + 1] for k in range(4)], axis=0)
    line = line.reshape(32, 4, 16, 1)
    second = jnp.zeros((512, 128), F32)
    for k in range(4):
        second = jnp.where(lane == k, line[:, k].reshape(512, 1), second)
    return jnp.concatenate([columns, second], axis=1)


def small_columns(parts, lines_ref, small_ref):
    lines_ref[...] = jnp.zeros_like(lines_ref)
    at = 0
    for part in parts[:-1]:
        lines_ref[at : at + part.shape[0], 0:16] = part[...].astype(F32)
        at += part.shape[0]
    line = parts[-1][...].astype(F32)
    for k in range(4):
        lines_ref[128 + k : 129 + k, 0:16] = line[:, k * 16 : k * 16 + 16]
    small_ref[0, :, 0:128] = jnp.transpose(lines_ref[0:128, :])[0:16].astype(BF16)
    small_ref[0, :, 128:256] = jnp.transpose(lines_ref[128:256, :])[0:16].astype(BF16)


FIRST_OUT = 11


def first_kernel(gathers, steps, *refs):
    step = pl.program_id(0)
    (source_ref, remote_ref, tgt_ref, src_ref), refs = refs[:4], refs[4:]
    if gathers:
        shards, smalls, refs = refs[:7], refs[7:14], refs[14:]
    else:
        (ws_ref, wc_ref, table_ref), refs = refs[:3], refs[3:]
    (q1_out, k1_out, v1_out, m1_ref, s1_ref, q2_ref, k2_ref, v2_ref, m2_ref, s2_ref, shares_ref), refs = (
        refs[:FIRST_OUT], refs[FIRST_OUT:])
    if gathers:
        (table_ref, ws_out, wc_out, win_out, wout_out), refs = refs[:5], refs[5:]
        (ws_ref, wc_ref, small_ref, own_ref, lines_ref, *sems), refs = refs[:8], refs[8:]
        pieces = gather_pieces((*shards, own_ref), (ws_ref, wc_ref, win_out, wout_out, small_ref), sems)
        small, query, keys, values, mixed, cross, inner, outer = pieces
        head = (small, query, keys, values, mixed)
    bias_ref, hidden_ref, keep_ref, ids_ref, q1_ref, k1_ref, v1_ref, out_sem = refs
    saves = [
        pltpu.make_async_copy(ref, out, out_sem.at[i])
        for i, (ref, out) in enumerate(((q1_ref, q1_out), (k1_ref, k1_out), (v1_ref, v1_out)))
    ]
    if gathers:
        saves.append(pltpu.make_async_copy(ws_ref, ws_out, out_sem.at[3]))
        late_save = pltpu.make_async_copy(wc_ref, wc_out, out_sem.at[4])
    tokens = source_ref.shape[0]

    def project(index, out_ref, row, factor):
        def one_part(part, carry):
            at = tokens_of(part, tokens // steps)
            found = mm_nt(source_ref[at, :], square(ws_ref, index))
            if row is not None:
                found = found + vrow(table_ref, row)
            if factor is not None:
                found = found * factor
            out_ref[at, :] = found.astype(BF16)
            return carry

        lax.fori_loop(0, steps, one_part, 0, unroll=True)

    def project_query():
        project(0, q1_ref, SELF_BQ, HEAD_DIM**-0.5)

    def project_keys():
        project(1, k1_ref, None, None)

    def project_values():
        project(2, v1_ref, SELF_BV, None)

    @pl.when(step == 0)
    def _():
        if not gathers:
            prepare_masks(tgt_ref, src_ref, ids_ref, bias_ref)
            project_query()
            project_keys()
            project_values()
        else:
            hail()
            small_columns(smalls, lines_ref, own_ref)
            for piece in pieces:
                for copy in piece.locals():
                    copy.start()
            await_hails()
            for piece in head:
                piece.start(0)
            prepare_masks(tgt_ref, src_ref, ids_ref, bias_ref)
            for piece in head:
                for copy in piece.locals():
                    copy.wait()

            def move(piece, stage):
                piece.arrive(stage)
                if stage < 3:
                    piece.start(stage + 1)

            move(small, 0)
            move(query, 0)
            move(keys, 0)
            move(small, 1)
            move(query, 1)
            move(values, 0)
            move(keys, 1)
            move(small, 2)
            move(query, 2)
            move(mixed, 0)
            cross.start(0)
            move(values, 1)
            move(keys, 2)
            move(small, 3)
            table_from_columns(small_ref[0].reshape(512, 256).astype(F32), table_ref)
            move(mixed, 1)
            move(query, 3)
            project_query()
            move(values, 2)
            inner.start(0)
            move(keys, 3)
            project_keys()
            move(mixed, 2)
            for piece in (cross, inner, outer):
                for copy in piece.locals():
                    copy.wait()
            cross.arrive(0)
            cross.start(1)
            outer.start(0)
            move(values, 3)
            project_values()
            move(mixed, 3)
        for copy in saves:
            copy.start()

    @pl.when((step >= 1) & (step <= steps))
    def _():
        self_forward(
            step - 1, source_ref, ws_ref, table_ref, q1_ref, k1_ref, v1_ref,
            shares_ref, m1_ref, s1_ref, bias_ref)
        keep_ref[step - 1] = s1_ref[...]

    @pl.when(step > steps)
    def _():
        at = step - steps - 1
        cross_forward(
            at, keep_ref.at[at], remote_ref, wc_ref, table_ref,
            q2_ref, k2_ref, v2_ref, shares_ref, m2_ref, s2_ref, bias_ref, hidden_ref)

    if gathers:
        @pl.when(step == 1)
        def _():
            cross.arrive(1)
            cross.start(2)
            inner.arrive(0)
            inner.start(1)

        @pl.when(step == steps - 1)
        def _():
            cross.arrive(2)
            cross.start(3)
            outer.arrive(0)
            outer.start(1)

        @pl.when(step == steps)
        def _():
            cross.arrive(3)
            late_save.start()

        @pl.when(step == steps + 1)
        def _():
            inner.arrive(1)
            inner.start(2)

        @pl.when(step == steps + 2)
        def _():
            outer.arrive(1)
            outer.start(2)
            inner.arrive(2)
            inner.start(3)

        @pl.when(step == 2 * steps - 1)
        def _():
            outer.arrive(2)
            outer.start(3)

    @pl.when(step == 2 * steps)
    def _():
        if gathers:
            inner.arrive(3)
            outer.arrive(3)
            for piece in pieces:
                piece.finish()
            late_save.wait()
        for copy in saves:
            copy.wait()


def ffn_kernel(
    summed_two_ref, upstream_ref, win_any, wout_any, table_ref,
    result_ref, sum_two_ref, dwin_ref, dwout_ref, dtable_ref,
    normed_two_ref, hidden_ref, active_ref, slope_ref, accum_ref,
    low_two_ref, grad_low_ref, accin_ref, accout_ref, acct_ref, win_ref, wout_ref, in_sem,
):
    step = pl.program_id(0)
    chunks = win_ref.shape[0] // 512
    bring = (pltpu.make_async_copy(win_any, win_ref, in_sem.at[0]), pltpu.make_async_copy(wout_any, wout_ref, in_sem.at[1]))

    @pl.when(step == 0)
    def _():
        for copy in bring:
            copy.start()
        acct_ref[...] = jnp.zeros_like(acct_ref)

    normed_two, inverse_two = norm_stats(summed_two_ref[...])
    normed_two_ref[...] = normed_two
    hidden_two = normed_two * vrow(table_ref, CROSS_G) + vrow(table_ref, CROSS_S)
    hidden_ref[...] = hidden_two
    low_two_ref[...] = hidden_two.astype(BF16)

    @pl.when(step == 0)
    def _():
        for copy in bring:
            copy.wait()

    def expand(chunk):
        units = slice(chunk * 512, chunk * 512 + 512)
        return mm_nt(low_two_ref[...], win_ref[units, :]) + table_ref[FFN_BI + chunk : FFN_BI + chunk + 1, :]

    def bend(chunk, expanded):
        units = slice(chunk * 512, chunk * 512 + 512)
        square = expanded * expanded
        bent = jnp.tanh(expanded * (GELU_A + (GELU_A * GELU_B) * square))
        half = 0.5 * bent + 0.5
        active = expanded * half
        active_ref[:, units] = active.astype(BF16)
        slope = half + (active * (1.0 - half)) * (2.0 * GELU_A + (6.0 * GELU_A * GELU_B) * square)
        slope_ref[:, units] = slope.astype(BF16)

    ahead = expand(0)
    for chunk in range(chunks):
        expanded = ahead
        if chunk + 1 < chunks:
            ahead = expand(chunk + 1)
        bend(chunk, expanded)
    contracted = mm_nt(active_ref[...], wout_ref[...])
    normed_three, inverse_three = norm_stats(
        hidden_ref[...] + contracted + vrow(table_ref, FFN_BO)
    )
    result = normed_three * vrow(table_ref, FFN_G) + vrow(table_ref, FFN_S)
    result_ref[...] = result.astype(BF16)

    upstream = upstream_ref[...].astype(F32)
    add_row(acct_ref, FFN_G, column_sum(upstream * normed_three))
    add_row(acct_ref, FFN_S, column_sum(upstream))
    sum_three = norm_back(upstream, normed_three, inverse_three, vrow(table_ref, FFN_G))
    grad_low_ref[...] = sum_three.astype(BF16)
    add_row(acct_ref, FFN_BO, column_sum(grad_low_ref[...]))
    accum_ref[...] = sum_three

    grad_three = grad_low_ref[...]
    for chunk in range(chunks):
        units = slice(chunk * 512, chunk * 512 + 512)
        grad_active = mm_nn(grad_three, wout_ref[:, units])
        total = jnp.where(step == 0, 0.0, accout_ref[:, units]) + mm_tn(grad_three, active_ref[:, units])
        accout_ref[:, units] = total
        dwout_ref[:, units] = total.astype(BF16)
        grad_expanded = (grad_active * slope_ref[:, units].astype(F32)).astype(BF16)
        slope_ref[:, units] = grad_expanded
        acct_ref[FFN_BI + chunk : FFN_BI + chunk + 1, :] += column_sum(grad_expanded)
        total = jnp.where(step == 0, 0.0, accin_ref[units, :]) + mm_tn(grad_expanded, low_two_ref[...])
        accin_ref[units, :] = total
        dwin_ref[units, :] = total.astype(BF16)
    accum_ref[...] += mm_nn(slope_ref[...], win_ref[...])
    grad_hidden_two = accum_ref[...]
    normed_two = normed_two_ref[...]
    add_row(acct_ref, CROSS_G, column_sum(grad_hidden_two * normed_two))
    add_row(acct_ref, CROSS_S, column_sum(grad_hidden_two))
    sum_two_ref[...] = norm_back(grad_hidden_two, normed_two, inverse_two, vrow(table_ref, CROSS_G))

    @pl.when(step == pl.num_programs(0) - 1)
    def _():
        dtable_ref[...] = acct_ref[...]


def cross_backward(
    step, sum_two_ref, summed_one_ref, remote_ref, mixture_ref, query_ref, keys_ref, values_ref, shares_ref,
    weight_ref, table_ref, first_mixture_ref, sum_one_ref, up_ref, gq_ref, gk_ref, gv_ref,
    acc_ref, acc_out_ref, acct_ref,
):
    slots = shares_ref.shape[1]
    block = tokens_of(step, STEP_ROWS * slots)
    grad_two = sum_two_ref[...].astype(BF16)
    add_row(acct_ref, CROSS_BO, column_sum(grad_two))
    up_ref[...] = mm_nn(grad_two, square(weight_ref, 3)).astype(BF16)
    acc_ref[3] = jnp.where(step == 0, 0.0, acc_ref[3]) + mm_tn(grad_two, mixture_ref[...])
    for row in range(STEP_ROWS):
        attend_rows_back(
            up_ref, query_ref, keys_ref, values_ref, shares_ref, gq_ref, gk_ref, gv_ref, row,
            tokens_of(row, slots), tokens_of(step * STEP_ROWS + row, slots))
    normed_one, inverse_one = norm_stats(summed_one_ref[...])
    low = (normed_one * vrow(table_ref, SELF_G) + vrow(table_ref, SELF_S)).astype(BF16)
    grad_query, grad_keys, grad_values = gq_ref[block, :], gk_ref[block, :], gv_ref[block, :]
    add_row(acct_ref, CROSS_BQ, column_sum(grad_query))
    add_row(acct_ref, CROSS_BV, column_sum(grad_values))
    grad_hidden_one = sum_two_ref[...] + mm_nn(grad_query, square(weight_ref, 0))
    add_row(acct_ref, SELF_G, column_sum(grad_hidden_one * normed_one))
    add_row(acct_ref, SELF_S, column_sum(grad_hidden_one))
    sum_one = norm_back(grad_hidden_one, normed_one, inverse_one, vrow(table_ref, SELF_G))
    sum_one_ref[...] = sum_one
    acc_ref[0] = jnp.where(step == 0, 0.0, acc_ref[0]) + mm_tn(grad_query, low)
    acc_ref[1] = jnp.where(step == 0, 0.0, acc_ref[1]) + mm_tn(grad_keys, remote_ref[...])
    acc_ref[2] = jnp.where(step == 0, 0.0, acc_ref[2]) + mm_tn(grad_values, remote_ref[...])
    grad_one = sum_one.astype(BF16)
    add_row(acct_ref, SELF_BO, column_sum(grad_one))
    acc_out_ref[0] = jnp.where(step == 0, 0.0, acc_out_ref[0]) + mm_tn(grad_one, first_mixture_ref[...])


def self_backward(
    step, sum_one_ref, query_ref, keys_ref, values_ref, shares_ref, weight_ref,
    up_ref, gq_ref, gk_ref, gv_ref, acct_ref,
):
    slots = shares_ref.shape[1]
    block = tokens_of(step, STEP_ROWS * slots)
    up_ref[...] = mm_nn(sum_one_ref[...].astype(BF16), square(weight_ref, 3)).astype(BF16)
    for row in range(STEP_ROWS):
        attend_rows_back(
            up_ref, query_ref, keys_ref, values_ref, shares_ref, gq_ref, gk_ref, gv_ref, row,
            tokens_of(row, slots), tokens_of(step * STEP_ROWS + row, slots))
    add_row(acct_ref, SELF_BQ, column_sum(gq_ref[block, :]))
    add_row(acct_ref, SELF_BV, column_sum(gv_ref[block, :]))


class Scatter:
    def __init__(self, theirs, halves, bufs, units, sems, base):
        self.theirs, self.halves, self.units = theirs, halves, units
        self.total, self.pair, self.far, self.near = bufs
        self.local, self.send, self.recv = sems
        self.base = base

    def copy(self, slot, source, target, partner):
        at = self.base + slot
        return pltpu.make_async_remote_copy(
            src_ref=source, dst_ref=target, send_sem=self.send.at[at], recv_sem=self.recv.at[at],
            device_id=partner, device_id_type=MESH)

    def hops(self, stage, incoming=False):
        z, y, x, core = place()
        if stage == 0:
            return [self.copy(0, self.theirs, self.pair, device(z, y, x, 1 - core))]
        sides = ((y, 1 - x), (1 - y, x))
        if stage == 1:
            return [
                self.copy(1 + i, self.total.at[h[0], :, 1 - y, 1 - x, h[1], h[2]], self.far.at[i], device(z, *side, core))
                for i, (side, h) in enumerate(zip(sides, self.halves))
            ]
        if stage == 2:
            return [
                self.copy(3 + i, self.total.at[:, :, side[0], side[1]], self.near.at[i], device(z, *side, core))
                for i, side in enumerate(sides)
            ]
        found = []
        for step in (1, 2, 3):
            other = lax.rem(z + step, 4)
            found.append(self.copy(4 + step, self.total.at[:, other, y, x], self.units.at[step], device(other, y, x, core)))
        return found

    def own(self):
        z, y, x, _ = place()
        return pltpu.make_async_copy(self.total.at[:, z, y, x], self.units.at[0], self.local.at[self.base])

    def divide(self, mat, ref, index):
        _, _, _, core = place()
        self.theirs[mat] = ref[index, :, :, :, 1 - core].astype(BF16)
        self.total[mat] = ref[index, :, :, :, core].astype(BF16)

    def start(self, stage):
        for hop in self.hops(stage):
            hop.start()
        if stage == 3:
            self.own().start()

    def arrive(self, stage):
        for hop in self.hops(stage):
            hop.wait_recv()
        z, y, x, core = place()
        if stage == 0:
            for mat in range(self.total.shape[0]):
                self.total[mat] = self.total[mat] + self.pair[mat]
        if stage == 1:
            for i, (h, at) in enumerate(zip(self.halves, ((1 - y, x), (y, 1 - x)))):
                old = self.total[h[0], :, at[0], at[1], h[1], h[2]]
                self.total[h[0], :, at[0], at[1], h[1], h[2]] = old + self.far[i]
        if stage == 2:
            old = self.total[:, :, y, x].astype(F32)
            self.total[:, :, y, x] = (
                old + self.near[0].astype(F32) + self.near[1].astype(F32)).astype(BF16)

    def finish(self):
        for stage in range(4):
            for hop in self.hops(stage):
                hop.wait_send()
        self.own().wait()


SCATTER_SLOTS = 8


def last_kernel(scatters, steps, *refs):
    step = pl.program_id(0)
    (sum_two_ref, s1_ref, remote_ref, m2_ref, q2_ref, k2_ref, v2_ref, shares_ref, m1_ref,
     source_any, q1_ref, k1_ref, v1_ref, ws_any, wc_ref, table_ref), refs = refs[:16], refs[16:]
    if scatters:
        (dwin, dwout, dtable_in), refs = refs[:3], refs[3:]
    (grad_remote_out, grad_source_out), refs = refs[:2], refs[2:]
    if scatters:
        units, refs = refs[:8], refs[8:]
    else:
        (dself_ref, dcross_ref, dtable_ref), refs = refs[:3], refs[3:]
    (up_ref, g_ref, gk2_ref, gv2_ref, keep_ref, acco_ref, accc_ref, acct_ref, out_sem, source_ref, ws_ref, in_sem), refs = (
        refs[:12], refs[12:])
    bring = (
        pltpu.make_async_copy(ws_any, ws_ref, in_sem.at[0]), pltpu.make_async_copy(source_any, source_ref, in_sem.at[1]))
    gq_ref, gk_ref, gv_ref = (g_ref.at[i] for i in range(3))
    if scatters:
        (halfc_ref, halfo_ref, halfq_ref, halfk_ref, halfv_ref, halft_ref, low_ref, lowt_ref), refs = refs[:8], refs[8:]
        bufs = [refs[4 * i : 4 * i + 4] for i in range(8)]
        sems = refs[32:]
        local = sems[0]
        lanes = lambda n: ((ALL, ALL, slice(0, n)), (ALL, ALL, slice(n, 2 * n)))
        mats = ((slice(0, 2), ALL, ALL), (slice(2, 4), ALL, ALL))
        rows = ((ALL, slice(0, 32), ALL), (ALL, slice(32, 64), ALL))
        core = lax.axis_index("fsdp") % 2
        plans = [
            (dwin.at[:, :, :, :, 1 - core], rows), (dwout.at[:, :, :, :, 1 - core], lanes(1024)), (halfc_ref, mats),
            (halfo_ref, lanes(256)), (halfq_ref, lanes(256)), (halfk_ref, lanes(256)), (halfv_ref, lanes(256)),
            (halft_ref, lanes(128)),
        ]
        everything = [
            Scatter(theirs, halves, bufs[i], units[i], sems, i * SCATTER_SLOTS)
            for i, (theirs, halves) in enumerate(plans)
        ]
        inner, outer, cross, mixed, query, keys, values, small = everything
        fetch = [
            pltpu.make_async_copy(dwin.at[:, :, :, :, core], bufs[0][0], local.at[1]),
            pltpu.make_async_copy(dwout.at[:, :, :, :, core], bufs[1][0], local.at[2]),
        ]

    @pl.when(step == 0)
    def _():
        if scatters:
            hail()
        acct_ref[...] = jnp.zeros_like(acct_ref)
        if scatters:
            await_hails()
            inner.start(0)
            outer.start(0)
            for copy in fetch:
                copy.start()
        for copy in bring:
            copy.start()

    @pl.when(step < steps)
    def _():
        cross_backward(
            step, sum_two_ref, s1_ref, remote_ref, m2_ref, q2_ref, k2_ref, v2_ref, shares_ref, wc_ref, table_ref, m1_ref,
            keep_ref.at[step], up_ref, gq_ref, gk2_ref, gv2_ref, Flat(accc_ref), Flat(acco_ref), acct_ref)

    @pl.when(step == steps)
    def _():
        for copy in bring:
            copy.wait()

    @pl.when((step >= steps) & (step < 2 * steps))
    def _():
        self_backward(
            step - steps, keep_ref.at[step - steps], q1_ref, k1_ref, v1_ref, shares_ref, ws_ref,
            up_ref, gq_ref, gk_ref, gv_ref, acct_ref)

    tokens = source_ref.shape[0]

    def weight_grad(index):
        return mm_tn(g_ref[index], source_ref[...]).astype(BF16)

    def results(block):
        at = tokens_of(block, tokens // steps)
        return (
            pltpu.make_async_copy(gq_ref.at[at, :], grad_source_out.at[at, :], out_sem.at[block]),
            pltpu.make_async_copy(gk2_ref.at[at, :], grad_remote_out.at[at, :], out_sem.at[steps + block]))

    def source_grad(block):
        at = tokens_of(block, tokens // steps)
        found = (
            keep_ref[block]
            + mm_nn(gq_ref[at, :], square(ws_ref, 0))
            + mm_nn(gk_ref[at, :], square(ws_ref, 1))
            + mm_nn(gv_ref[at, :], square(ws_ref, 2))
        )
        gq_ref[at, :] = found.astype(BF16)
        results(block)[0].start()

    def remote_grad(block):
        at = tokens_of(block, tokens // steps)
        found = mm_nn(gk2_ref[at, :], square(wc_ref, 1)) + mm_nn(gv2_ref[at, :], square(wc_ref, 2))
        gk2_ref[at, :] = found.astype(BF16)
        results(block)[1].start()

    if not scatters:
        @pl.when(step == 2 * steps)
        def _():
            for index in range(3):
                dself_ref[index] = weight_grad(index).reshape(dself_ref.shape[1:])
            dself_ref[3] = acco_ref[0].astype(BF16)
            dcross_ref[...] = accc_ref[...].astype(BF16)
            dtable_ref[...] = acct_ref[...]
            for block in range(steps):
                source_grad(block)
                remote_grad(block)
            for block in range(steps):
                for copy in results(block):
                    copy.wait()
        return

    def move(piece, stage):
        piece.arrive(stage)
        piece.start(stage + 1)

    @pl.when(step == 0)
    def _():
        for copy in fetch:
            copy.wait()
        move(inner, 0)
        move(outer, 0)

    @pl.when(step == steps - 2)
    def _():
        move(inner, 1)
        move(outer, 1)

    @pl.when(step == steps - 1)
    def _():
        for mat in range(4):
            cross.divide(mat, accc_ref, mat)
        mixed.divide(0, acco_ref, 0)
        cross.start(0)
        mixed.start(0)

    @pl.when(step == steps)
    def _():
        move(cross, 0)
        move(mixed, 0)

    @pl.when(step == steps + 1)
    def _():
        move(inner, 2)
        move(outer, 2)
        move(cross, 1)
        move(mixed, 1)

    @pl.when(step == 2 * steps - 1)
    def _():
        move(cross, 2)
        move(mixed, 2)

    @pl.when(step == 2 * steps)
    def _():
        parts = (query, keys, values)

        def one_matrix(index, carry):
            low_ref[0] = weight_grad(index).reshape(low_ref.shape[1:])
            for at, piece in enumerate(parts):
                @pl.when(index == at)
                def _():
                    piece.divide(0, low_ref, 0)
                    piece.start(0)
                    if at > 0:
                        move(parts[at - 1], 0)
            return carry

        lax.fori_loop(0, 3, one_matrix, 0)
        table = columns_from_table(acct_ref[...] + dtable_in[...]).astype(BF16)
        lowt_ref[...] = table.reshape(lowt_ref.shape)
        small.divide(0, lowt_ref, 0)
        small.start(0)
        moves = (
            (((values, 0), (query, 1)), ((keys, 1), (small, 0))),
            ((), ((values, 1),)),
            (((query, 2), (small, 1)), ((keys, 2),)),
            (((values, 2), (small, 2)), ()),
        )

        def one_block(block, carry):
            for half, work in enumerate((source_grad, remote_grad)):
                work(block)
                for at in range(4):
                    if moves[at][half]:
                        @pl.when(block == at)
                        def _():
                            for piece, stage in moves[at][half]:
                                move(piece, stage)
            return carry

        lax.fori_loop(0, steps, one_block, 0)
        for piece in everything:
            piece.arrive(3)
        for piece in everything:
            piece.finish()
        for block in range(steps):
            for copy in results(block):
                copy.wait()


class Flat:
    def __init__(self, ref):
        self.ref = ref

    def __getitem__(self, index):
        return self.ref[index].reshape(512, 512)

    def __setitem__(self, index, values):
        self.ref[index] = values.reshape(self.ref.shape[1:])


def sum_kernel(*refs):
    units, (remote_in, source_in), refs = refs[:8], refs[8:10], refs[10:]
    (qkv, bias_one, out_one, norm_one, cross_q, cross_kv, bias_two, out_two, norm_two,
     win, win_bias, wout, wout_bias, norm_three, remote_out, source_out), refs = refs[:16], refs[16:]
    held, sems = refs[:10], refs[10]
    copies = [
        pltpu.make_async_copy(ref, buf, sems.at[i])
        for i, (ref, buf) in enumerate(zip((*units, remote_in, source_in), held))
    ]
    for copy in copies:
        copy.start()
    for copy in copies[:8]:
        copy.wait()
    total = lambda ref: (
        ref[0].astype(F32) + ref[1].astype(F32) + ref[2].astype(F32) + ref[3].astype(F32))
    win[...] = total(held[0])[0]
    wout[...] = total(held[1])[0]
    cross = total(held[2])
    cross_q[...] = cross[0]
    cross_kv[...] = cross[1:3]
    out_two[...] = cross[3]
    out_one[...] = total(held[3])[0]
    for index in range(3):
        qkv[index] = total(held[4 + index])[0]
    small = jnp.transpose(total(held[7])[0])
    bias_one[...] = small[SELF_BQ : SELF_BQ + 3]
    norm_one[...] = small[SELF_G : SELF_G + 2]
    bias_two[...] = small[CROSS_BQ : CROSS_BQ + 3]
    norm_two[...] = small[CROSS_G : CROSS_G + 2]
    wout_bias[...] = small[FFN_BO : FFN_BO + 1]
    norm_three[...] = small[FFN_G : FFN_G + 2]
    for k in range(4):
        win_bias[:, k * 16 : k * 16 + 16] = small[128 + k : 129 + k]
    leaving = [
        pltpu.make_async_copy(buf, ref, sems.at[10 + i])
        for i, (ref, buf) in enumerate(zip((remote_out, source_out), held[8:]))
    ]
    for arrived, copy in zip(copies[8:], leaving):
        arrived.wait()
        copy.start()
    for copy in leaving:
        copy.wait()


def fixed(shape):
    return pl.BlockSpec(shape, lambda i: (0,) * len(shape), pipeline_mode=pl.Buffered(1))


def shape_of(*shape, dtype=BF16):
    return jax.ShapeDtypeStruct(shape, dtype)


def params(limit, collective=None):
    if collective is None:
        return pltpu.CompilerParams(vmem_limit_bytes=limit, dimension_semantics=("arbitrary",))
    return pltpu.CompilerParams(
        vmem_limit_bytes=limit, dimension_semantics=("arbitrary",), collective_id=collective,
        has_side_effects=True)


ANYWHERE = pl.BlockSpec(memory_space=pl.ANY)
SQUARES = (4,) + BLOCKS + (16, 512)
WIN_BLOCKS = (1,) + BLOCKS + (64, 512)
WOUT_BLOCKS = (1,) + BLOCKS + (16, 2048)
SMALL_BLOCKS = (1,) + BLOCKS + (16, 256)


ONE_BLOCKS = (1,) + BLOCKS + (16, 512)


def layer(decoder_in, memory, out_grad, tgt_len, src_len, shards=None, weights=None):
    rows, slots, width = decoder_in.shape
    tokens = rows * slots
    block = STEP_ROWS * slots
    steps = rows // STEP_ROWS
    shares_block = (STEP_ROWS * HEADS, slots, slots)
    source = decoder_in.reshape(tokens, width)
    remote = memory.reshape(tokens, width)
    low, full = shape_of(tokens, width), shape_of(tokens, width, dtype=F32)
    vm = pltpu.VMEM
    dma = pltpu.SemaphoreType.DMA
    part = lambda first: (lambda i: jnp.clip(i - first, 0, steps - 1))
    tok = lambda when: pl.BlockSpec((block, width), lambda i: (when(i), 0))
    shares = lambda when: pl.BlockSpec(shares_block, lambda i: (when(i), 0, 0))
    shares_shape = shape_of(2 * rows * HEADS, slots, slots)
    table_shape = shape_of(TABLE, width, dtype=F32)
    table_spec = fixed((TABLE, width))
    ins = [source, remote, tgt_len, src_len]
    early, late = part(1), part(1 + steps)
    in_specs = [fixed(source.shape), tok(late), fixed(tgt_len.shape), fixed(src_len.shape)]
    out_shape = [low, low, low, low, full] * 2 + [shares_shape]
    out_specs = [ANYWHERE] * 3 + [tok(early)] * 2 + [tok(late)] * 5
    out_specs += [shares(lambda i: jnp.clip(i - 1, 0, 2 * steps - 1))]
    scratch = []
    if shards is not None:
        big, small = shards
        ins += [*big, *small]
        in_specs += [ANYWHERE] * 7 + [fixed(array.shape) for array in small]
        out_shape += [table_shape, shape_of(*SQUARES), shape_of(*SQUARES), shape_of(*WIN_BLOCKS), shape_of(*WOUT_BLOCKS)]
        out_specs += [table_spec] + [ANYWHERE] * 4
        scratch += [vm(SQUARES, BF16), vm(SQUARES, BF16), vm(SMALL_BLOCKS, BF16), vm((1, 16, 256), BF16), vm((256, 128), F32)]
        scratch += [dma((GATHER_SLOTS,)), dma((GATHER_SLOTS,)), dma((GATHER_SLOTS,))]
    else:
        ws, wc, win, wout, table = weights
        ws, wc = ws.reshape(SQUARES), wc.reshape(SQUARES)
        ins += [ws, wc, table]
        in_specs += [fixed(SQUARES), fixed(SQUARES), table_spec]
    scratch += [vm((2, rows, slots, slots), F32), vm((block, width), F32), vm((steps, block, width), F32), vm((rows, 2, slots), F32)]
    scratch += [vm((tokens, width), BF16)] * 3 + [dma((5,))]
    outs = pl.pallas_call(
        functools.partial(first_kernel, shards is not None, steps),
        grid=(1 + 2 * steps,), in_specs=in_specs, out_specs=out_specs, out_shape=out_shape, scratch_shapes=scratch,
        compiler_params=params(60 << 20, None if shards is None else 1), name="first",
    )(*ins)
    q1, k1, v1, m1, s1, q2, k2, v2, m2, s2, both = outs[:FIRST_OUT]
    if shards is not None:
        table, ws, wc, win, wout = outs[FIRST_OUT:]
        win = win.reshape(-1, width)
        wout = wout.reshape(width, -1)
    hidden = win.shape[0]
    now = part(0)
    result, sum_two, dwin, dwout, dtable = pl.pallas_call(
        ffn_kernel,
        grid=(steps,),
        in_specs=[tok(now), tok(now), ANYWHERE, ANYWHERE, table_spec],
        out_specs=[tok(now), tok(now), fixed(win.shape), fixed(wout.shape), table_spec],
        out_shape=[low, full, shape_of(*win.shape), shape_of(*wout.shape), table_shape],
        scratch_shapes=[
            vm((block, width), F32), vm((block, width), F32), vm((block, hidden), BF16), vm((block, hidden), BF16),
            vm((block, width), F32), vm((block, width), BF16), vm((block, width), BF16),
            vm(win.shape, F32), vm(wout.shape, F32), vm((TABLE, width), F32),
            vm(win.shape, BF16), vm(wout.shape, BF16), dma((2,)),
        ],
        compiler_params=params(60 << 20), name="feed_forward",
    )(s2, out_grad.reshape(tokens, width), win, wout, table)

    early, late = part(0), part(steps)
    ins = [sum_two, s1, remote, m2, q2, k2, v2, both, m1, source, q1, k1, v1, ws, wc, table]
    in_specs = [tok(early)] * 7 + [shares(lambda i: jnp.where(i < steps, i + steps, jnp.minimum(i - steps, steps - 1)))]
    in_specs += [tok(early), ANYWHERE] + [tok(late)] * 3
    in_specs += [ANYWHERE, fixed(SQUARES), table_spec]
    out_shape, out_specs = [low, low], [ANYWHERE, ANYWHERE]
    scratch = [vm((block, width), BF16), vm((3, tokens, width), BF16)] + [vm((tokens, width), BF16)] * 2 + [
        vm((steps, block, width), F32), vm(ONE_BLOCKS, F32), vm(SQUARES, F32), vm((TABLE, width), F32), dma((2 * steps,)),
        vm((tokens, width), BF16), vm(SQUARES, BF16), dma((2,))]
    if shards is not None:
        ins += [dwin.reshape(WIN_BLOCKS), dwout.reshape(WOUT_BLOCKS), dtable]
        in_specs += [ANYWHERE, ANYWHERE, table_spec]
        every = (WIN_BLOCKS, WOUT_BLOCKS, SQUARES, ONE_BLOCKS, ONE_BLOCKS, ONE_BLOCKS, ONE_BLOCKS, SMALL_BLOCKS)
        unit_shapes = [(4, s[0], s[5], s[6]) for s in every]
        out_shape += [shape_of(*s) for s in unit_shapes]
        out_specs += [ANYWHERE] * 8
        scratch += [vm(s[:4] + s[5:], BF16) for s in every[2:]]
        scratch += [vm(ONE_BLOCKS, BF16), vm(SMALL_BLOCKS, BF16)]
        cut = ((1, 2, 1), (1, 1, 2), (2, 1, 1)) + ((1, 1, 2),) * 5
        for s, (m, r, l) in zip(every, cut):
            scratch += [
                vm(s[:4] + s[5:], BF16), vm(s[:4] + s[5:], BF16),
                vm((2, s[0] // m, 4, s[5] // r, s[6] // l), BF16), vm((2, s[0], 4, s[5], s[6]), BF16)]
        scratch += [dma((8 * SCATTER_SLOTS,))] * 3
    else:
        out_shape += [shape_of(*SQUARES), shape_of(*SQUARES), table_shape]
        out_specs += [fixed(SQUARES), fixed(SQUARES), table_spec]
    grad_remote, grad_source, *tail = pl.pallas_call(
        functools.partial(last_kernel, shards is not None, steps),
        grid=(2 * steps + 1,), in_specs=in_specs, out_specs=out_specs, out_shape=out_shape, scratch_shapes=scratch,
        compiler_params=params(63 << 20, None if shards is None else 2), name="last",
    )(*ins)
    as_rows = lambda array: array.reshape(rows, slots, width)
    if shards is None:
        dself, dcross, dtable_last = tail
        grads = (dself.reshape(4, 512, 512), dcross.reshape(4, 512, 512), dwin, dwout, dtable + dtable_last)
    else:
        f = lambda *shape: shape_of(*shape, dtype=F32)
        in_vm = pl.BlockSpec(memory_space=pltpu.VMEM)
        *grads, grad_remote, grad_source = pl.pallas_call(
            sum_kernel,
            in_specs=[pl.BlockSpec(memory_space=pltpu.HBM)] * 10,
            out_specs=[in_vm] * 14 + [pl.BlockSpec(memory_space=pltpu.HBM)] * 2,
            out_shape=[f(3, 16, 512), f(3, 16), f(16, 512), f(2, 16), f(16, 512), f(2, 16, 512), f(3, 16), f(16, 512),
                       f(2, 16), f(64, 512), f(1, 64), f(16, 2048), f(1, 16), f(2, 16), low, low],
            scratch_shapes=[vm(s, BF16) for s in unit_shapes] + [vm((tokens, width), BF16)] * 2 + [dma((12,))],
            compiler_params=pltpu.CompilerParams(vmem_limit_bytes=63 << 20), name="sum_planes",
        )(*tail, grad_remote, grad_source)
    return as_rows(result), as_rows(grad_source), as_rows(grad_remote), grads


def turn(array):
    return jnp.swapaxes(array, -1, -2)


AXES = ("dp", "fsdp")


def gather_plain(parts, count):
    (self_qkv, self_bias, self_out, self_norm, cross_q, cross_kv, cross_bias, cross_out, cross_norm,
     ffn_in, ffn_in_bias, ffn_out, ffn_out_bias, ffn_norm) = parts
    cols = self_out.shape[1]
    width = self_out.shape[0]
    chunks = ffn_out.shape[0] // width
    small = jnp.concatenate(
        [self_bias, self_norm, cross_bias, cross_norm, ffn_out_bias[None], ffn_norm,
         ffn_in_bias.reshape(chunks, cols)], axis=0)
    small = jnp.pad(turn(small), ((0, 0), (0, width - small.shape[0])))
    packed = jnp.concatenate([
        turn(self_qkv).reshape(-1, width), turn(self_out), turn(cross_q),
        turn(cross_kv).reshape(-1, width), turn(cross_out), turn(ffn_in),
        turn(ffn_out).reshape(cols, chunks, width).swapaxes(0, 1).reshape(-1, width), small], axis=0)
    whole_set = lax.all_gather(packed, AXES, axis=0, tiled=False)
    square = whole_set[:, : 8 * cols].reshape(count, 8, cols, width).swapaxes(0, 1)
    square = square.reshape(8, width, width)
    low = 8 * cols
    win = whole_set[:, low : low + chunks * cols].reshape(chunks * width, width)
    low += chunks * cols
    wout = whole_set[:, low : low + chunks * cols].reshape(count, chunks, cols, width)
    wout = wout.transpose(0, 2, 1, 3).reshape(width, chunks * width)
    low += chunks * cols
    table = whole_set[:, low:]
    first = table[:, :, :13].transpose(2, 0, 1).reshape(13, width)
    second = table[:, :, 13 : 13 + chunks].transpose(0, 2, 1).reshape(chunks, width)
    table = jnp.concatenate([first, second], axis=0).astype(F32)
    table = jnp.pad(table, ((0, TABLE - table.shape[0]), (0, 0)))
    return square[:4], square[4:], win, wout, table


def scatter_plain(dself, dcross, dwin, dwout, dtable, count):
    width = dself.shape[1]
    cols = width // count
    chunks = dwin.shape[0] // width
    squares = jnp.concatenate([dself, dcross], axis=0).reshape(8, count, cols, width).swapaxes(0, 1)
    first = dtable[:13].reshape(13, count, cols).transpose(1, 2, 0)
    second = dtable[13 : 13 + chunks].reshape(count, chunks, cols).transpose(0, 2, 1)
    small = jnp.concatenate([first, second], axis=2)
    small = jnp.pad(small, ((0, 0), (0, 0), (0, width - small.shape[2]))).astype(BF16)
    packed = jnp.concatenate([
        squares.reshape(count, 8 * cols, width), dwin.reshape(count, chunks * cols, width),
        dwout.reshape(count, cols, chunks, width).swapaxes(1, 2).reshape(count, -1, width), small],
        axis=1)
    mine = lax.psum_scatter(packed, AXES, scatter_dimension=0, tiled=False).astype(F32)
    square = turn(mine[: 8 * cols].reshape(8, cols, width))
    low = 8 * cols
    ffn_in = turn(mine[low : low + chunks * cols])
    low += chunks * cols
    ffn_out = mine[low : low + chunks * cols].reshape(chunks, cols, width).swapaxes(0, 1)
    ffn_out = turn(ffn_out.reshape(cols, chunks * width))
    low += chunks * cols
    small = turn(mine[low:, : 13 + chunks])
    return (square[:3], small[0:3], square[3], small[3:5], square[4], square[5:7], small[5:8], square[7],
            small[8:10], ffn_in, small[13:].reshape(-1), ffn_out, small[10], small[11:13])


def on_device(count, direct, decoder_in, memory, out_grad, tgt_len, src_len, *parts):
    if not direct:
        weights = gather_plain(parts, count)
        result, grad_source, grad_remote, grads = layer(
            decoder_in, memory, out_grad, tgt_len, src_len, weights=weights)
        return (result, grad_source, grad_remote, *scatter_plain(*grads, count))
    (self_qkv, self_bias, self_out, self_norm, cross_q, cross_kv, cross_bias, cross_out, cross_norm,
     ffn_in, ffn_in_bias, ffn_out, ffn_out_bias, ffn_norm) = parts
    big = [turn(part) for part in (self_qkv, self_out, cross_q, cross_kv, cross_out, ffn_in, ffn_out)]
    big = [part.reshape((-1,) + part.shape[-2:]) for part in big]
    small = [self_bias, self_norm, cross_bias, cross_norm, ffn_out_bias.reshape(1, -1), ffn_norm, ffn_in_bias.reshape(1, -1)]
    shards = big, small
    result, grad_source, grad_remote, grads = layer(
        decoder_in, memory, out_grad, tgt_len, src_len, shards=shards)
    (qkv, bias_one, out_one, norm_one, query, pair, bias_two, out_two, norm_two, win, win_bias, wout, wout_bias,
     norm_three) = grads
    return (result, grad_source, grad_remote, turn(qkv), bias_one, turn(out_one), norm_one, turn(query), turn(pair),
            bias_two, turn(out_two), norm_two, turn(win), win_bias.reshape(-1), turn(wout), wout_bias.reshape(-1),
            norm_three)


def solution(mesh):
    count = mesh.shape["dp"] * mesh.shape["fsdp"]
    direct = mesh.shape["dp"] == 4 and mesh.shape["fsdp"] == 8
    rows = P(AXES, None, None)
    lens = P(AXES, None)
    cube = P(None, None, AXES)
    flat = P(None, AXES)
    line = P(AXES)
    params_in = (cube, flat, flat, flat, flat, cube, flat, flat, flat, flat, line, flat, line, flat)
    return jax.shard_map(
        functools.partial(on_device, count, direct),
        mesh=mesh,
        in_specs=(rows, rows, rows, lens, lens) + params_in,
        out_specs=(rows, rows, rows) + params_in,
        check_vma=False,
    )
```

```python
import functools

import jax
import jax.numpy as jnp
from jax import lax
from jax.experimental import pallas as pl
from jax.experimental.pallas import tpu as pltpu
from jax.sharding import PartitionSpec as P

F32 = jnp.float32
BF16 = jnp.bfloat16
EPS = 1e-05
MASKED = -1e30
HEADS = 8
HEAD_DIM = 64
PAIR = 128
QUAD = 256
GELU_A = 0.7978845608028654
GELU_B = 0.044715


def mm(left, right, left_dim, right_dim):
    return lax.dot_general(
        left, right, (((left_dim,), (right_dim,)), ((), ())), preferred_element_type=F32
    )


def mm_nt(left, right):
    return mm(left, right, 1, 1)


def mm_nn(left, right):
    return mm(left, right, 1, 0)


def mm_tn(left, right):
    return mm(left, right, 0, 0)


def norm_stats(summed):
    centred = summed - jnp.mean(summed, axis=-1, keepdims=True)
    inverse = lax.rsqrt(jnp.mean(centred * centred, axis=-1, keepdims=True) + EPS)
    return centred * inverse, inverse


def norm_back(upstream, normed, inverse, gain):
    scaled = upstream * gain
    mean_scaled = jnp.mean(scaled, axis=-1, keepdims=True)
    mean_product = jnp.mean(scaled * normed, axis=-1, keepdims=True)
    return (scaled - mean_scaled - normed * mean_product) * inverse


def column_sum(values):
    return jnp.sum(values.astype(F32), axis=0, keepdims=True)


def lane_band(width, head):
    lane = lax.broadcasted_iota(jnp.int32, (1, width), 1)
    return (lane >= head * HEAD_DIM) & (lane < (head + 1) * HEAD_DIM)


def keep_head(values, head):
    return jnp.where(lane_band(values.shape[1], head), values, jnp.zeros_like(values))


def mask_bias(key_ids, query_ids, causal):
    slots = key_ids.shape[1]
    down = jnp.transpose(jnp.broadcast_to(key_ids, (slots, slots)))
    allowed = down == query_ids
    if causal:
        key_at = lax.broadcasted_iota(jnp.int32, (slots, slots), 0)
        query_at = lax.broadcasted_iota(jnp.int32, (slots, slots), 1)
        allowed = allowed & (key_at <= query_at)
    return jnp.where(allowed, 0.0, MASKED).astype(F32)


def attend_rows(query_ref, keys_ref, values_ref, bias_ref, shares_ref, mixture_ref, row, at, into):
    for quad in range(HEADS * HEAD_DIM // QUAD):
        lanes = slice(quad * QUAD, (quad + 1) * QUAD)
        values_quad = values_ref[at, lanes]
        parts, wide = [], []
        for inner in range(QUAD // HEAD_DIM):
            head = quad * (QUAD // HEAD_DIM) + inner
            first = head * HEAD_DIM // PAIR * PAIR
            pair = slice(first, first + PAIR)
            keys_head = keep_head(keys_ref[at, pair], head - first // HEAD_DIM)
            scores = mm_nt(keys_head, query_ref[at, pair]) + bias_ref[...]
            top = jnp.max(scores, axis=0, keepdims=True)
            raised = jnp.exp(scores - top)
            total = jnp.sum(raised, axis=0, keepdims=True)
            shares = (raised * (1.0 / total)).astype(BF16)
            shares_ref[row * HEADS + head] = shares
            parts.append(shares)
            wide.append(keep_head(values_quad, inner))
        mixture = mm_tn(jnp.concatenate(parts, 0), jnp.concatenate(wide, 0))
        mixture_ref[into, lanes] = mixture.astype(BF16)


def attend_rows_back(
    upstream_ref, query_ref, keys_ref, values_ref, shares_ref, gq_ref, gk_ref, gv_ref, row, at, into
):
    for quad in range(HEADS * HEAD_DIM // QUAD):
        lanes = slice(quad * QUAD, (quad + 1) * QUAD)
        query_quad = query_ref[at, lanes]
        keys_quad = keys_ref[at, lanes]
        up_quad = upstream_ref[at, lanes]
        grad_query = grad_keys = grad_values = None
        for inner in range(QUAD // HEAD_DIM):
            head = quad * (QUAD // HEAD_DIM) + inner
            first = head * HEAD_DIM // PAIR * PAIR
            pair = slice(first, first + PAIR)
            values_head = keep_head(values_ref[at, pair], head - first // HEAD_DIM)
            shares = shares_ref[row * HEADS + head]
            grad_shares = mm_nt(values_head, upstream_ref[at, pair])
            wide = shares.astype(F32)
            product = wide * grad_shares
            centre = jnp.sum(product, axis=0, keepdims=True)
            grad_scores = (product - wide * centre).astype(BF16)
            one = mm_nn(grad_scores, keep_head(query_quad, inner))
            two = mm_nn(shares, keep_head(up_quad, inner))
            three = mm_tn(grad_scores, keep_head(keys_quad, inner))
            grad_keys = one if grad_keys is None else grad_keys + one
            grad_values = two if grad_values is None else grad_values + two
            grad_query = three if grad_query is None else grad_query + three
        gq_ref[into, lanes] = (grad_query * HEAD_DIM**-0.5).astype(BF16)
        gk_ref[into, lanes] = grad_keys.astype(BF16)
        gv_ref[into, lanes] = grad_values.astype(BF16)


STEP_ROWS = 2

SELF_BQ, SELF_BV, SELF_BO, SELF_G, SELF_S = 0, 1, 2, 3, 4
CROSS_BQ, CROSS_BV, CROSS_BO, CROSS_G, CROSS_S = 5, 6, 7, 8, 9
FFN_BO, FFN_G, FFN_S, FFN_BI = 10, 11, 12, 13
TABLE = 24


def vrow(table_ref, index):
    return table_ref[index : index + 1, :]


def add_row(ref, index, values):
    ref[index : index + 1, :] += values


MESH = pl.DeviceIdType.MESH
ALL = slice(None)


def place():
    z = lax.axis_index("dp")
    f = lax.axis_index("fsdp")
    return z, f // 4, (f // 2) % 2, f % 2


def device(z, y, x, core):
    return (z, y * 4 + x * 2 + core)


def partners():
    z, y, x, core = place()
    found = [device(lax.rem(z + step, 4), y, x, core) for step in (1, 2, 3)]
    return found + [device(z, y, 1 - x, core), device(z, 1 - y, x, core), device(z, y, x, 1 - core)]


def hail():
    barrier = pltpu.get_barrier_semaphore()
    for partner in partners():
        pl.semaphore_signal(barrier, inc=1, device_id=partner, device_id_type=MESH)


def await_hails():
    pl.semaphore_wait(pltpu.get_barrier_semaphore(), 6)


class Gather:
    def __init__(self, ref, own, first, second, sems, base):
        self.ref, self.own, self.first, self.second = ref, own, first, second
        self.local, self.send, self.recv = sems
        self.base = base
        self.mats = slice(min(m.start for _, m in own), max(m.stop for _, m in own))

    @staticmethod
    def slots(own):
        return 3 * len(own) + 5

    def copy(self, slot, source, target, partner):
        at = self.base + slot
        return pltpu.make_async_remote_copy(
            src_ref=source, dst_ref=target, send_sem=self.send.at[at], recv_sem=self.recv.at[at],
            device_id=partner, device_id_type=MESH)

    def at(self, half, z, y, x, core):
        mats, rows, lanes = half
        return self.ref.at[mats, z, y, x, core, rows, lanes]

    def locals(self):
        z, y, x, core = place()
        return [
            pltpu.make_async_copy(source, self.ref.at[mats, z, y, x, core], self.local.at[self.base + i])
            for i, (source, mats) in enumerate(self.own)
        ]

    def hops(self, stage, incoming):
        z, y, x, core = place()
        full = (self.mats, ALL, ALL)
        found = []
        many = len(self.own)
        if stage == 0:
            for step in (1, 2, 3):
                other = lax.rem(z + (4 - step if incoming else step), 4)
                for i, (source, mats) in enumerate(self.own):
                    target = self.ref.at[mats, other if incoming else z, y, x, core]
                    found.append(self.copy((step - 1) * many + i, source, target, device(other, y, x, core)))
        if stage == 1:
            for slot, (py, px) in enumerate(((y, 1 - x), (1 - y, x))):
                sent = self.at(full, ALL, y, x, core)
                target = self.at(full, ALL, py, px, core) if incoming else sent
                found.append(self.copy(3 * many + slot, sent, target, device(z, py, px, core)))
        if stage == 2:
            for slot, (half, by, bx, py, px) in enumerate((
                (self.first, 1 - y, x, y, 1 - x), (self.second, y, 1 - x, 1 - y, x))):
                sent = self.at(half, ALL, by, bx, core)
                target = self.at(half, ALL, 1 - y, 1 - x, core) if incoming else sent
                found.append(self.copy(3 * many + 2 + slot, sent, target, device(z, py, px, core)))
        if stage == 3:
            sent = self.at(full, ALL, ALL, ALL, core)
            target = self.at(full, ALL, ALL, ALL, 1 - core) if incoming else sent
            found.append(self.copy(3 * many + 4, sent, target, device(z, y, x, 1 - core)))
        return found

    def start(self, stage):
        for hop in self.hops(stage, False):
            hop.start()

    def arrive(self, stage):
        for hop in self.hops(stage, True):
            hop.wait_recv()

    def finish(self):
        for stage in range(4):
            for hop in self.hops(stage, False):
                hop.wait_send()


def gather_pieces(shards, targets, sems):
    qkv, out_one, cross_q, cross_kv, out_two, win, wout, small = shards
    ws, wc, win_all, wout_all, small_all = targets
    one = lambda n: slice(n, n + 1)
    lanes = lambda n: ((ALL, ALL, slice(0, n)), (ALL, ALL, slice(n, 2 * n)))
    single = lambda n: ((one(n), ALL, slice(0, 256)), (one(n), ALL, slice(256, 512)))
    plans = [
        (small_all, [(small, one(0))], *lanes(128)),
        (ws, [(qkv.at[0:1], one(0))], *single(0)),
        (ws, [(qkv.at[1:2], one(1))], *single(1)),
        (ws, [(qkv.at[2:3], one(2))], *single(2)),
        (ws, [(out_one, one(3))], *single(3)),
        (wc, [(cross_q, one(0)), (cross_kv, slice(1, 3)), (out_two, one(3))],
         (slice(0, 2), ALL, ALL), (slice(2, 4), ALL, ALL)),
        (win_all, [(win, one(0))], (ALL, slice(0, 32), ALL), (ALL, slice(32, 64), ALL)),
        (wout_all, [(wout, one(0))], *lanes(1024)),
    ]
    pieces, base = [], 0
    for ref, own, first, second in plans:
        pieces.append(Gather(ref, own, first, second, sems, base))
        base += Gather.slots(own)
    return pieces


GATHER_SLOTS = 80

BLOCKS = (4, 2, 2, 2)


def square(ref, index):
    return ref[index].reshape(512, 512)


def prepare_masks(tgt_ref, src_ref, ids_ref, bias_ref):
    rows, sents = tgt_ref.shape
    slots = ids_ref.shape[2]
    before = lax.broadcasted_iota(jnp.int32, (sents, sents), 0)
    after = lax.broadcasted_iota(jnp.int32, (sents, sents), 1)
    ladder = (before <= after).astype(F32)
    slot = lax.broadcasted_iota(jnp.int32, (sents, slots), 1).astype(F32)
    for side, ref in enumerate((tgt_ref, src_ref)):
        lengths = ref[...].astype(F32)
        finish = lax.dot_general(
            ladder, lengths, (((0,), (1,)), ((), ())),
            precision=lax.Precision.HIGHEST, preferred_element_type=F32)
        for row in range(rows):
            ended = (finish[:, row : row + 1] <= slot).astype(F32)
            ids_ref[row, side : side + 1, :] = jnp.sum(ended, axis=0, keepdims=True)

    def one_row(row, carry):
        ids = ids_ref[row]
        bias_ref[0, row] = mask_bias(ids[0:1], ids[0:1], True)
        bias_ref[1, row] = mask_bias(ids[1:2], ids[0:1], False)
        return carry

    lax.fori_loop(0, rows, one_row, 0)


def tokens_of(block, size):
    start = block * size
    return pl.ds(start if isinstance(start, int) else pl.multiple_of(start, size), size)


def self_forward(
    step, source_ref, weight_ref, table_ref, query_ref, keys_ref, values_ref,
    shares_ref, mixture_ref, summed_ref, bias_ref,
):
    slots = shares_ref.shape[1]
    block = STEP_ROWS * slots
    for row in range(STEP_ROWS):
        attend_rows(
            query_ref, keys_ref, values_ref, bias_ref.at[0, step * STEP_ROWS + row], shares_ref, mixture_ref, row,
            tokens_of(step * STEP_ROWS + row, slots), tokens_of(row, slots))
    summed_ref[...] = (
        source_ref[tokens_of(step, block), :].astype(F32)
        + mm_nt(mixture_ref[...], square(weight_ref, 3)) + vrow(table_ref, SELF_BO)
    )


def cross_forward(
    step, summed_one_ref, remote_ref, weight_ref, table_ref,
    query_ref, keys_ref, values_ref, shares_ref, mixture_ref, summed_ref, bias_ref, hidden_ref,
):
    slots = shares_ref.shape[1]
    normed_one, _ = norm_stats(summed_one_ref[...])
    hidden_one = normed_one * vrow(table_ref, SELF_G) + vrow(table_ref, SELF_S)
    hidden_ref[...] = hidden_one
    query = mm_nt(hidden_one.astype(BF16), square(weight_ref, 0)) + vrow(table_ref, CROSS_BQ)
    query_ref[...] = (query * HEAD_DIM**-0.5).astype(BF16)
    remote = remote_ref[...]
    keys_ref[...] = mm_nt(remote, square(weight_ref, 1)).astype(BF16)
    values_ref[...] = (mm_nt(remote, square(weight_ref, 2)) + vrow(table_ref, CROSS_BV)).astype(BF16)

    for row in range(STEP_ROWS):
        at = tokens_of(row, slots)
        attend_rows(
            query_ref, keys_ref, values_ref, bias_ref.at[1, step * STEP_ROWS + row], shares_ref, mixture_ref, row, at, at)
    summed_ref[...] = (
        hidden_ref[...] + mm_nt(mixture_ref[...], square(weight_ref, 3)) + vrow(table_ref, CROSS_BO)
    )


def table_from_columns(columns, table_ref):
    turned = jnp.transpose(columns[:, :128])
    table_ref[0:TABLE, :] = turned[0:TABLE]
    parts = [columns[:, 128 + k : 129 + k].reshape(32, 1, 16, 1) for k in range(4)]
    line = jnp.concatenate(parts, axis=1).reshape(2048, 1)
    line = jnp.transpose(jnp.broadcast_to(line, (2048, 128)))
    for k in range(4):
        table_ref[FFN_BI + k : FFN_BI + k + 1, :] = line[0:1, k * 512 : (k + 1) * 512]


def columns_from_table(rows):
    rows = jnp.concatenate([rows, jnp.zeros((128 - TABLE, 512), F32)], axis=0)
    columns = jnp.transpose(rows)
    lane = lax.broadcasted_iota(jnp.int32, (512, 128), 1)
    line = jnp.concatenate([columns[:, FFN_BI + k : FFN_BI + k + 1] for k in range(4)], axis=0)
    line = line.reshape(32, 4, 16, 1)
    second = jnp.zeros((512, 128), F32)
    for k in range(4):
        second = jnp.where(lane == k, line[:, k].reshape(512, 1), second)
    return jnp.concatenate([columns, second], axis=1)


def small_columns(parts, lines_ref, small_ref):
    lines_ref[...] = jnp.zeros_like(lines_ref)
    at = 0
    for part in parts[:-1]:
        lines_ref[at : at + part.shape[0], 0:16] = part[...].astype(F32)
        at += part.shape[0]
    line = parts[-1][...].astype(F32)
    for k in range(4):
        lines_ref[128 + k : 129 + k, 0:16] = line[:, k * 16 : k * 16 + 16]
    small_ref[0, :, 0:128] = jnp.transpose(lines_ref[0:128, :])[0:16].astype(BF16)
    small_ref[0, :, 128:256] = jnp.transpose(lines_ref[128:256, :])[0:16].astype(BF16)


FIRST_OUT = 11


def first_kernel(gathers, steps, *refs):
    step = pl.program_id(0)
    (source_ref, remote_ref, tgt_ref, src_ref), refs = refs[:4], refs[4:]
    if gathers:
        shards, smalls, refs = refs[:7], refs[7:14], refs[14:]
    else:
        (ws_ref, wc_ref, table_ref), refs = refs[:3], refs[3:]
    (q1_out, k1_out, v1_out, m1_ref, s1_ref, q2_ref, k2_ref, v2_ref, m2_ref, s2_ref, shares_ref), refs = (
        refs[:FIRST_OUT], refs[FIRST_OUT:])
    if gathers:
        (table_ref, ws_out, wc_out, win_out, wout_out), refs = refs[:5], refs[5:]
        (ws_ref, wc_ref, small_ref, own_ref, lines_ref, *sems), refs = refs[:8], refs[8:]
        pieces = gather_pieces((*shards, own_ref), (ws_ref, wc_ref, win_out, wout_out, small_ref), sems)
        small, query, keys, values, mixed, cross, inner, outer = pieces
        head = (small, query, keys, values, mixed)
    bias_ref, hidden_ref, keep_ref, ids_ref, q1_ref, k1_ref, v1_ref, out_sem = refs
    saves = [
        pltpu.make_async_copy(ref, out, out_sem.at[i])
        for i, (ref, out) in enumerate(((q1_ref, q1_out), (k1_ref, k1_out), (v1_ref, v1_out)))
    ]
    if gathers:
        saves.append(pltpu.make_async_copy(ws_ref, ws_out, out_sem.at[3]))
        late_save = pltpu.make_async_copy(wc_ref, wc_out, out_sem.at[4])
    tokens = source_ref.shape[0]

    def project(index, out_ref, row, factor):
        def one_part(part, carry):
            at = tokens_of(part, tokens // steps)
            found = mm_nt(source_ref[at, :], square(ws_ref, index))
            if row is not None:
                found = found + vrow(table_ref, row)
            if factor is not None:
                found = found * factor
            out_ref[at, :] = found.astype(BF16)
            return carry

        lax.fori_loop(0, steps, one_part, 0, unroll=True)

    def project_query():
        project(0, q1_ref, SELF_BQ, HEAD_DIM**-0.5)

    def project_keys():
        project(1, k1_ref, None, None)

    def project_values():
        project(2, v1_ref, SELF_BV, None)

    @pl.when(step == 0)
    def _():
        if not gathers:
            prepare_masks(tgt_ref, src_ref, ids_ref, bias_ref)
            project_query()
            project_keys()
            project_values()
        else:
            hail()
            small_columns(smalls, lines_ref, own_ref)
            for piece in pieces:
                for copy in piece.locals():
                    copy.start()
            await_hails()
            for piece in head:
                piece.start(0)
            prepare_masks(tgt_ref, src_ref, ids_ref, bias_ref)
            for piece in head:
                for copy in piece.locals():
                    copy.wait()

            def move(piece, stage):
                piece.arrive(stage)
                if stage < 3:
                    piece.start(stage + 1)

            move(small, 0)
            move(query, 0)
            move(keys, 0)
            move(small, 1)
            move(query, 1)
            move(values, 0)
            cross.start(0)
            move(keys, 1)
            move(small, 2)
            move(query, 2)
            move(mixed, 0)
            move(values, 1)
            inner.start(0)
            move(keys, 2)
            move(small, 3)
            table_from_columns(small_ref[0].reshape(512, 256).astype(F32), table_ref)
            move(mixed, 1)
            move(query, 3)
            move(values, 2)
            move(keys, 3)
            project_query()
            for piece in (cross, inner, outer):
                for copy in piece.locals():
                    copy.wait()
            move(cross, 0)
            outer.start(0)
            move(mixed, 2)
            project_keys()
            move(values, 3)
            project_values()
            move(mixed, 3)
        for copy in saves:
            copy.start()

    @pl.when((step >= 1) & (step <= steps))
    def _():
        self_forward(
            step - 1, source_ref, ws_ref, table_ref, q1_ref, k1_ref, v1_ref,
            shares_ref, m1_ref, s1_ref, bias_ref)
        keep_ref[step - 1] = s1_ref[...]

    @pl.when(step > steps)
    def _():
        at = step - steps - 1
        cross_forward(
            at, keep_ref.at[at], remote_ref, wc_ref, table_ref,
            q2_ref, k2_ref, v2_ref, shares_ref, m2_ref, s2_ref, bias_ref, hidden_ref)

    if gathers:
        @pl.when(step == 1)
        def _():
            cross.arrive(1)
            cross.start(2)
            inner.arrive(0)
            inner.start(1)

        @pl.when(step == steps - 1)
        def _():
            cross.arrive(2)
            cross.start(3)
            outer.arrive(0)
            outer.start(1)

        @pl.when(step == steps)
        def _():
            cross.arrive(3)
            late_save.start()

        @pl.when(step == steps + 1)
        def _():
            inner.arrive(1)
            inner.start(2)

        @pl.when(step == steps + 2)
        def _():
            outer.arrive(1)
            outer.start(2)
            inner.arrive(2)
            inner.start(3)

        @pl.when(step == 2 * steps - 1)
        def _():
            outer.arrive(2)
            outer.start(3)

    @pl.when(step == 2 * steps)
    def _():
        if gathers:
            inner.arrive(3)
            outer.arrive(3)
            for piece in pieces:
                piece.finish()
            late_save.wait()
        for copy in saves:
            copy.wait()


def ffn_kernel(
    summed_two_ref, upstream_ref, win_any, wout_any, table_ref,
    result_ref, sum_two_ref, dwin_ref, dwout_ref, dtable_ref,
    normed_two_ref, hidden_ref, active_ref, slope_ref, accum_ref,
    low_two_ref, grad_low_ref, accin_ref, accout_ref, acct_ref, win_ref, wout_ref, in_sem,
):
    step = pl.program_id(0)
    chunks = win_ref.shape[0] // 512
    bring = (pltpu.make_async_copy(win_any, win_ref, in_sem.at[0]), pltpu.make_async_copy(wout_any, wout_ref, in_sem.at[1]))

    @pl.when(step == 0)
    def _():
        for copy in bring:
            copy.start()
        acct_ref[...] = jnp.zeros_like(acct_ref)

    normed_two, inverse_two = norm_stats(summed_two_ref[...])
    normed_two_ref[...] = normed_two
    hidden_two = normed_two * vrow(table_ref, CROSS_G) + vrow(table_ref, CROSS_S)
    hidden_ref[...] = hidden_two
    low_two_ref[...] = hidden_two.astype(BF16)

    @pl.when(step == 0)
    def _():
        for copy in bring:
            copy.wait()

    def expand(chunk):
        units = slice(chunk * 512, chunk * 512 + 512)
        return mm_nt(low_two_ref[...], win_ref[units, :]) + table_ref[FFN_BI + chunk : FFN_BI + chunk + 1, :]

    def bend(chunk, expanded):
        units = slice(chunk * 512, chunk * 512 + 512)
        square = expanded * expanded
        bent = jnp.tanh(expanded * (GELU_A + (GELU_A * GELU_B) * square))
        half = 0.5 * bent + 0.5
        active = expanded * half
        active_ref[:, units] = active.astype(BF16)
        slope = half + (active * (1.0 - half)) * (2.0 * GELU_A + (6.0 * GELU_A * GELU_B) * square)
        slope_ref[:, units] = slope.astype(BF16)

    ahead = expand(0)
    for chunk in range(chunks):
        expanded = ahead
        if chunk + 1 < chunks:
            ahead = expand(chunk + 1)
        bend(chunk, expanded)
    contracted = mm_nt(active_ref[...], wout_ref[...])
    normed_three, inverse_three = norm_stats(
        hidden_ref[...] + contracted + vrow(table_ref, FFN_BO)
    )
    result = normed_three * vrow(table_ref, FFN_G) + vrow(table_ref, FFN_S)
    result_ref[...] = result.astype(BF16)

    upstream = upstream_ref[...].astype(F32)
    add_row(acct_ref, FFN_G, column_sum(upstream * normed_three))
    add_row(acct_ref, FFN_S, column_sum(upstream))
    sum_three = norm_back(upstream, normed_three, inverse_three, vrow(table_ref, FFN_G))
    grad_low_ref[...] = sum_three.astype(BF16)
    add_row(acct_ref, FFN_BO, column_sum(grad_low_ref[...]))
    accum_ref[...] = sum_three

    grad_three = grad_low_ref[...]
    for chunk in range(chunks):
        units = slice(chunk * 512, chunk * 512 + 512)
        grad_active = mm_nn(grad_three, wout_ref[:, units])
        total = jnp.where(step == 0, 0.0, accout_ref[:, units]) + mm_tn(grad_three, active_ref[:, units])
        accout_ref[:, units] = total
        dwout_ref[:, units] = total.astype(BF16)
        grad_expanded = (grad_active * slope_ref[:, units].astype(F32)).astype(BF16)
        slope_ref[:, units] = grad_expanded
        acct_ref[FFN_BI + chunk : FFN_BI + chunk + 1, :] += column_sum(grad_expanded)
        total = jnp.where(step == 0, 0.0, accin_ref[units, :]) + mm_tn(grad_expanded, low_two_ref[...])
        accin_ref[units, :] = total
        dwin_ref[units, :] = total.astype(BF16)
    accum_ref[...] += mm_nn(slope_ref[...], win_ref[...])
    grad_hidden_two = accum_ref[...]
    normed_two = normed_two_ref[...]
    add_row(acct_ref, CROSS_G, column_sum(grad_hidden_two * normed_two))
    add_row(acct_ref, CROSS_S, column_sum(grad_hidden_two))
    sum_two_ref[...] = norm_back(grad_hidden_two, normed_two, inverse_two, vrow(table_ref, CROSS_G))

    @pl.when(step == pl.num_programs(0) - 1)
    def _():
        dtable_ref[...] = acct_ref[...]


def cross_backward(
    step, sum_two_ref, summed_one_ref, remote_ref, mixture_ref, query_ref, keys_ref, values_ref, shares_ref,
    weight_ref, table_ref, first_mixture_ref, sum_one_ref, up_ref, gq_ref, gk_ref, gv_ref,
    acc_ref, acc_out_ref, acct_ref,
):
    slots = shares_ref.shape[1]
    block = tokens_of(step, STEP_ROWS * slots)
    grad_two = sum_two_ref[...].astype(BF16)
    add_row(acct_ref, CROSS_BO, column_sum(grad_two))
    up_ref[...] = mm_nn(grad_two, square(weight_ref, 3)).astype(BF16)
    acc_ref[3] = jnp.where(step == 0, 0.0, acc_ref[3]) + mm_tn(grad_two, mixture_ref[...])
    for row in range(STEP_ROWS):
        attend_rows_back(
            up_ref, query_ref, keys_ref, values_ref, shares_ref, gq_ref, gk_ref, gv_ref, row,
            tokens_of(row, slots), tokens_of(step * STEP_ROWS + row, slots))
    normed_one, inverse_one = norm_stats(summed_one_ref[...])
    low = (normed_one * vrow(table_ref, SELF_G) + vrow(table_ref, SELF_S)).astype(BF16)
    grad_query, grad_keys, grad_values = gq_ref[block, :], gk_ref[block, :], gv_ref[block, :]
    add_row(acct_ref, CROSS_BQ, column_sum(grad_query))
    add_row(acct_ref, CROSS_BV, column_sum(grad_values))
    grad_hidden_one = sum_two_ref[...] + mm_nn(grad_query, square(weight_ref, 0))
    add_row(acct_ref, SELF_G, column_sum(grad_hidden_one * normed_one))
    add_row(acct_ref, SELF_S, column_sum(grad_hidden_one))
    sum_one = norm_back(grad_hidden_one, normed_one, inverse_one, vrow(table_ref, SELF_G))
    sum_one_ref[...] = sum_one
    acc_ref[0] = jnp.where(step == 0, 0.0, acc_ref[0]) + mm_tn(grad_query, low)
    acc_ref[1] = jnp.where(step == 0, 0.0, acc_ref[1]) + mm_tn(grad_keys, remote_ref[...])
    acc_ref[2] = jnp.where(step == 0, 0.0, acc_ref[2]) + mm_tn(grad_values, remote_ref[...])
    grad_one = sum_one.astype(BF16)
    add_row(acct_ref, SELF_BO, column_sum(grad_one))
    acc_out_ref[0] = jnp.where(step == 0, 0.0, acc_out_ref[0]) + mm_tn(grad_one, first_mixture_ref[...])


def self_backward(
    step, sum_one_ref, query_ref, keys_ref, values_ref, shares_ref, weight_ref,
    up_ref, gq_ref, gk_ref, gv_ref, acct_ref,
):
    slots = shares_ref.shape[1]
    block = tokens_of(step, STEP_ROWS * slots)
    up_ref[...] = mm_nn(sum_one_ref[...].astype(BF16), square(weight_ref, 3)).astype(BF16)
    for row in range(STEP_ROWS):
        attend_rows_back(
            up_ref, query_ref, keys_ref, values_ref, shares_ref, gq_ref, gk_ref, gv_ref, row,
            tokens_of(row, slots), tokens_of(step * STEP_ROWS + row, slots))
    add_row(acct_ref, SELF_BQ, column_sum(gq_ref[block, :]))
    add_row(acct_ref, SELF_BV, column_sum(gv_ref[block, :]))


class Scatter:
    def __init__(self, theirs, halves, bufs, units, sems, base):
        self.theirs, self.halves, self.units = theirs, halves, units
        self.total, self.pair, self.far, self.near = bufs
        self.local, self.send, self.recv = sems
        self.base = base

    def copy(self, slot, source, target, partner):
        at = self.base + slot
        return pltpu.make_async_remote_copy(
            src_ref=source, dst_ref=target, send_sem=self.send.at[at], recv_sem=self.recv.at[at],
            device_id=partner, device_id_type=MESH)

    def hops(self, stage, incoming=False):
        z, y, x, core = place()
        if stage == 0:
            return [self.copy(0, self.theirs, self.pair, device(z, y, x, 1 - core))]
        sides = ((y, 1 - x), (1 - y, x))
        if stage == 1:
            return [
                self.copy(1 + i, self.total.at[h[0], :, 1 - y, 1 - x, h[1], h[2]], self.far.at[i], device(z, *side, core))
                for i, (side, h) in enumerate(zip(sides, self.halves))
            ]
        if stage == 2:
            return [
                self.copy(3 + i, self.total.at[:, :, side[0], side[1]], self.near.at[i], device(z, *side, core))
                for i, side in enumerate(sides)
            ]
        found = []
        for step in (1, 2, 3):
            other = lax.rem(z + step, 4)
            found.append(self.copy(4 + step, self.total.at[:, other, y, x], self.units.at[step], device(other, y, x, core)))
        return found

    def own(self):
        z, y, x, _ = place()
        return pltpu.make_async_copy(self.total.at[:, z, y, x], self.units.at[0], self.local.at[self.base])

    def divide(self, mat, ref, index):
        _, _, _, core = place()
        self.theirs[mat] = ref[index, :, :, :, 1 - core].astype(BF16)
        self.total[mat] = ref[index, :, :, :, core].astype(BF16)

    def start(self, stage):
        for hop in self.hops(stage):
            hop.start()
        if stage == 3:
            self.own().start()

    def arrive(self, stage):
        for hop in self.hops(stage):
            hop.wait_recv()
        z, y, x, core = place()
        if stage == 0:
            for mat in range(self.total.shape[0]):
                self.total[mat] = self.total[mat] + self.pair[mat]
        if stage == 1:
            for i, (h, at) in enumerate(zip(self.halves, ((1 - y, x), (y, 1 - x)))):
                old = self.total[h[0], :, at[0], at[1], h[1], h[2]]
                self.total[h[0], :, at[0], at[1], h[1], h[2]] = old + self.far[i]
        if stage == 2:
            old = self.total[:, :, y, x].astype(F32)
            self.total[:, :, y, x] = (
                old + self.near[0].astype(F32) + self.near[1].astype(F32)).astype(BF16)

    def finish(self):
        for stage in range(4):
            for hop in self.hops(stage):
                hop.wait_send()
        self.own().wait()


SCATTER_SLOTS = 8


def last_kernel(scatters, steps, *refs):
    step = pl.program_id(0)
    (sum_two_ref, s1_ref, remote_ref, m2_ref, q2_ref, k2_ref, v2_ref, shares_ref, m1_ref,
     source_any, q1_ref, k1_ref, v1_ref, ws_any, wc_ref, table_ref), refs = refs[:16], refs[16:]
    if scatters:
        (dwin, dwout, dtable_in), refs = refs[:3], refs[3:]
    (grad_remote_out, grad_source_out), refs = refs[:2], refs[2:]
    if scatters:
        units, refs = refs[:8], refs[8:]
    else:
        (dself_ref, dcross_ref, dtable_ref), refs = refs[:3], refs[3:]
    (up_ref, g_ref, gk2_ref, gv2_ref, keep_ref, acco_ref, accc_ref, acct_ref, out_sem, source_ref, ws_ref, in_sem), refs = (
        refs[:12], refs[12:])
    bring = (
        pltpu.make_async_copy(ws_any, ws_ref, in_sem.at[0]), pltpu.make_async_copy(source_any, source_ref, in_sem.at[1]))
    gq_ref, gk_ref, gv_ref = (g_ref.at[i] for i in range(3))
    if scatters:
        (halfc_ref, halfo_ref, halfq_ref, halfk_ref, halfv_ref, halft_ref, low_ref, lowt_ref), refs = refs[:8], refs[8:]
        bufs = [refs[4 * i : 4 * i + 4] for i in range(8)]
        sems = refs[32:]
        local = sems[0]
        lanes = lambda n: ((ALL, ALL, slice(0, n)), (ALL, ALL, slice(n, 2 * n)))
        mats = ((slice(0, 2), ALL, ALL), (slice(2, 4), ALL, ALL))
        rows = ((ALL, slice(0, 32), ALL), (ALL, slice(32, 64), ALL))
        core = lax.axis_index("fsdp") % 2
        plans = [
            (dwin.at[:, :, :, :, 1 - core], rows), (dwout.at[:, :, :, :, 1 - core], lanes(1024)), (halfc_ref, mats),
            (halfo_ref, lanes(256)), (halfq_ref, lanes(256)), (halfk_ref, lanes(256)), (halfv_ref, lanes(256)),
            (halft_ref, lanes(128)),
        ]
        everything = [
            Scatter(theirs, halves, bufs[i], units[i], sems, i * SCATTER_SLOTS)
            for i, (theirs, halves) in enumerate(plans)
        ]
        inner, outer, cross, mixed, query, keys, values, small = everything
        fetch = [
            pltpu.make_async_copy(dwin.at[:, :, :, :, core], bufs[0][0], local.at[1]),
            pltpu.make_async_copy(dwout.at[:, :, :, :, core], bufs[1][0], local.at[2]),
        ]

    @pl.when(step == 0)
    def _():
        if scatters:
            hail()
        acct_ref[...] = jnp.zeros_like(acct_ref)
        if scatters:
            await_hails()
            inner.start(0)
            outer.start(0)
            for copy in fetch:
                copy.start()
        for copy in bring:
            copy.start()

    @pl.when(step < steps)
    def _():
        cross_backward(
            step, sum_two_ref, s1_ref, remote_ref, m2_ref, q2_ref, k2_ref, v2_ref, shares_ref, wc_ref, table_ref, m1_ref,
            keep_ref.at[step], up_ref, gq_ref, gk2_ref, gv2_ref, Flat(accc_ref), Flat(acco_ref), acct_ref)

    @pl.when(step == steps)
    def _():
        for copy in bring:
            copy.wait()

    @pl.when((step >= steps) & (step < 2 * steps))
    def _():
        self_backward(
            step - steps, keep_ref.at[step - steps], q1_ref, k1_ref, v1_ref, shares_ref, ws_ref,
            up_ref, gq_ref, gk_ref, gv_ref, acct_ref)

    tokens = source_ref.shape[0]

    def weight_grad(index):
        return mm_tn(g_ref[index], source_ref[...]).astype(BF16)

    def results(block):
        at = tokens_of(block, tokens // steps)
        return (
            pltpu.make_async_copy(gq_ref.at[at, :], grad_source_out.at[at, :], out_sem.at[block]),
            pltpu.make_async_copy(gk2_ref.at[at, :], grad_remote_out.at[at, :], out_sem.at[steps + block]))

    def source_grad(block):
        at = tokens_of(block, tokens // steps)
        found = (
            keep_ref[block]
            + mm_nn(gq_ref[at, :], square(ws_ref, 0))
            + mm_nn(gk_ref[at, :], square(ws_ref, 1))
            + mm_nn(gv_ref[at, :], square(ws_ref, 2))
        )
        gq_ref[at, :] = found.astype(BF16)
        results(block)[0].start()

    def remote_grad(block):
        at = tokens_of(block, tokens // steps)
        found = mm_nn(gk2_ref[at, :], square(wc_ref, 1)) + mm_nn(gv2_ref[at, :], square(wc_ref, 2))
        gk2_ref[at, :] = found.astype(BF16)
        results(block)[1].start()

    if not scatters:
        @pl.when(step == 2 * steps)
        def _():
            for index in range(3):
                dself_ref[index] = weight_grad(index).reshape(dself_ref.shape[1:])
            dself_ref[3] = acco_ref[0].astype(BF16)
            dcross_ref[...] = accc_ref[...].astype(BF16)
            dtable_ref[...] = acct_ref[...]
            for block in range(steps):
                source_grad(block)
                remote_grad(block)
            for block in range(steps):
                for copy in results(block):
                    copy.wait()
        return

    def move(piece, stage):
        piece.arrive(stage)
        piece.start(stage + 1)

    @pl.when(step == 0)
    def _():
        for copy in fetch:
            copy.wait()
        move(inner, 0)
        move(outer, 0)

    @pl.when(step == steps - 2)
    def _():
        move(inner, 1)
        move(outer, 1)

    @pl.when(step == steps - 1)
    def _():
        for mat in range(4):
            cross.divide(mat, accc_ref, mat)
        mixed.divide(0, acco_ref, 0)
        cross.start(0)
        mixed.start(0)

    @pl.when(step == steps)
    def _():
        move(cross, 0)
        move(mixed, 0)

    @pl.when(step == steps + 1)
    def _():
        move(inner, 2)
        move(outer, 2)
        move(cross, 1)
        move(mixed, 1)

    @pl.when(step == 2 * steps - 1)
    def _():
        move(cross, 2)
        move(mixed, 2)

    @pl.when(step == 2 * steps)
    def _():
        parts = (query, keys, values)

        def one_matrix(index, carry):
            low_ref[0] = weight_grad(index).reshape(low_ref.shape[1:])
            for at, piece in enumerate(parts):
                @pl.when(index == at)
                def _():
                    piece.divide(0, low_ref, 0)
                    piece.start(0)
                    if at > 0:
                        move(parts[at - 1], 0)
            return carry

        lax.fori_loop(0, 3, one_matrix, 0)
        table = columns_from_table(acct_ref[...] + dtable_in[...]).astype(BF16)
        lowt_ref[...] = table.reshape(lowt_ref.shape)
        small.divide(0, lowt_ref, 0)
        small.start(0)
        moves = (
            (((values, 0), (query, 1)), ((keys, 1), (small, 0))),
            ((), ((values, 1),)),
            (((query, 2), (small, 1)), ((keys, 2),)),
            (((values, 2), (small, 2)), ()),
        )

        def one_block(block, carry):
            for half, work in enumerate((source_grad, remote_grad)):
                work(block)
                for at in range(4):
                    if moves[at][half]:
                        @pl.when(block == at)
                        def _():
                            for piece, stage in moves[at][half]:
                                move(piece, stage)
            return carry

        lax.fori_loop(0, steps, one_block, 0)
        for piece in everything:
            piece.arrive(3)
        for piece in everything:
            piece.finish()
        for block in range(steps):
            for copy in results(block):
                copy.wait()


class Flat:
    def __init__(self, ref):
        self.ref = ref

    def __getitem__(self, index):
        return self.ref[index].reshape(512, 512)

    def __setitem__(self, index, values):
        self.ref[index] = values.reshape(self.ref.shape[1:])


def sum_kernel(*refs):
    units, (remote_in, source_in), refs = refs[:8], refs[8:10], refs[10:]
    (qkv, bias_one, out_one, norm_one, cross_q, cross_kv, bias_two, out_two, norm_two,
     win, win_bias, wout, wout_bias, norm_three, remote_out, source_out), refs = refs[:16], refs[16:]
    held, sems = refs[:10], refs[10]
    copies = [
        pltpu.make_async_copy(ref, buf, sems.at[i])
        for i, (ref, buf) in enumerate(zip((*units, remote_in, source_in), held))
    ]
    for copy in copies:
        copy.start()
    for copy in copies[:8]:
        copy.wait()
    total = lambda ref: (
        ref[0].astype(F32) + ref[1].astype(F32) + ref[2].astype(F32) + ref[3].astype(F32))
    win[...] = total(held[0])[0]
    wout[...] = total(held[1])[0]
    cross = total(held[2])
    cross_q[...] = cross[0]
    cross_kv[...] = cross[1:3]
    out_two[...] = cross[3]
    out_one[...] = total(held[3])[0]
    for index in range(3):
        qkv[index] = total(held[4 + index])[0]
    small = jnp.transpose(total(held[7])[0])
    bias_one[...] = small[SELF_BQ : SELF_BQ + 3]
    norm_one[...] = small[SELF_G : SELF_G + 2]
    bias_two[...] = small[CROSS_BQ : CROSS_BQ + 3]
    norm_two[...] = small[CROSS_G : CROSS_G + 2]
    wout_bias[...] = small[FFN_BO : FFN_BO + 1]
    norm_three[...] = small[FFN_G : FFN_G + 2]
    for k in range(4):
        win_bias[:, k * 16 : k * 16 + 16] = small[128 + k : 129 + k]
    leaving = [
        pltpu.make_async_copy(buf, ref, sems.at[10 + i])
        for i, (ref, buf) in enumerate(zip((remote_out, source_out), held[8:]))
    ]
    for arrived, copy in zip(copies[8:], leaving):
        arrived.wait()
        copy.start()
    for copy in leaving:
        copy.wait()


def fixed(shape):
    return pl.BlockSpec(shape, lambda i: (0,) * len(shape), pipeline_mode=pl.Buffered(1))


def shape_of(*shape, dtype=BF16):
    return jax.ShapeDtypeStruct(shape, dtype)


def params(limit, collective=None):
    if collective is None:
        return pltpu.CompilerParams(vmem_limit_bytes=limit, dimension_semantics=("arbitrary",))
    return pltpu.CompilerParams(
        vmem_limit_bytes=limit, dimension_semantics=("arbitrary",), collective_id=collective,
        has_side_effects=True)


ANYWHERE = pl.BlockSpec(memory_space=pl.ANY)
SQUARES = (4,) + BLOCKS + (16, 512)
WIN_BLOCKS = (1,) + BLOCKS + (64, 512)
WOUT_BLOCKS = (1,) + BLOCKS + (16, 2048)
SMALL_BLOCKS = (1,) + BLOCKS + (16, 256)


ONE_BLOCKS = (1,) + BLOCKS + (16, 512)


def layer(decoder_in, memory, out_grad, tgt_len, src_len, shards=None, weights=None):
    rows, slots, width = decoder_in.shape
    tokens = rows * slots
    block = STEP_ROWS * slots
    steps = rows // STEP_ROWS
    shares_block = (STEP_ROWS * HEADS, slots, slots)
    source = decoder_in.reshape(tokens, width)
    remote = memory.reshape(tokens, width)
    low, full = shape_of(tokens, width), shape_of(tokens, width, dtype=F32)
    vm = pltpu.VMEM
    dma = pltpu.SemaphoreType.DMA
    part = lambda first: (lambda i: jnp.clip(i - first, 0, steps - 1))
    tok = lambda when: pl.BlockSpec((block, width), lambda i: (when(i), 0))
    shares = lambda when: pl.BlockSpec(shares_block, lambda i: (when(i), 0, 0))
    shares_shape = shape_of(2 * rows * HEADS, slots, slots)
    table_shape = shape_of(TABLE, width, dtype=F32)
    table_spec = fixed((TABLE, width))
    ins = [source, remote, tgt_len, src_len]
    early, late = part(1), part(1 + steps)
    in_specs = [fixed(source.shape), tok(late), fixed(tgt_len.shape), fixed(src_len.shape)]
    out_shape = [low, low, low, low, full] * 2 + [shares_shape]
    out_specs = [ANYWHERE] * 3 + [tok(early)] * 2 + [tok(late)] * 5
    out_specs += [shares(lambda i: jnp.clip(i - 1, 0, 2 * steps - 1))]
    scratch = []
    if shards is not None:
        big, small = shards
        ins += [*big, *small]
        in_specs += [ANYWHERE] * 7 + [fixed(array.shape) for array in small]
        out_shape += [table_shape, shape_of(*SQUARES), shape_of(*SQUARES), shape_of(*WIN_BLOCKS), shape_of(*WOUT_BLOCKS)]
        out_specs += [table_spec] + [ANYWHERE] * 4
        scratch += [vm(SQUARES, BF16), vm(SQUARES, BF16), vm(SMALL_BLOCKS, BF16), vm((1, 16, 256), BF16), vm((256, 128), F32)]
        scratch += [dma((GATHER_SLOTS,)), dma((GATHER_SLOTS,)), dma((GATHER_SLOTS,))]
    else:
        ws, wc, win, wout, table = weights
        ws, wc = ws.reshape(SQUARES), wc.reshape(SQUARES)
        ins += [ws, wc, table]
        in_specs += [fixed(SQUARES), fixed(SQUARES), table_spec]
    scratch += [vm((2, rows, slots, slots), F32), vm((block, width), F32), vm((steps, block, width), F32), vm((rows, 2, slots), F32)]
    scratch += [vm((tokens, width), BF16)] * 3 + [dma((5,))]
    outs = pl.pallas_call(
        functools.partial(first_kernel, shards is not None, steps),
        grid=(1 + 2 * steps,), in_specs=in_specs, out_specs=out_specs, out_shape=out_shape, scratch_shapes=scratch,
        compiler_params=params(60 << 20, None if shards is None else 1), name="first",
    )(*ins)
    q1, k1, v1, m1, s1, q2, k2, v2, m2, s2, both = outs[:FIRST_OUT]
    if shards is not None:
        table, ws, wc, win, wout = outs[FIRST_OUT:]
        win = win.reshape(-1, width)
        wout = wout.reshape(width, -1)
    hidden = win.shape[0]
    now = part(0)
    result, sum_two, dwin, dwout, dtable = pl.pallas_call(
        ffn_kernel,
        grid=(steps,),
        in_specs=[tok(now), tok(now), ANYWHERE, ANYWHERE, table_spec],
        out_specs=[tok(now), tok(now), fixed(win.shape), fixed(wout.shape), table_spec],
        out_shape=[low, full, shape_of(*win.shape), shape_of(*wout.shape), table_shape],
        scratch_shapes=[
            vm((block, width), F32), vm((block, width), F32), vm((block, hidden), BF16), vm((block, hidden), BF16),
            vm((block, width), F32), vm((block, width), BF16), vm((block, width), BF16),
            vm(win.shape, F32), vm(wout.shape, F32), vm((TABLE, width), F32),
            vm(win.shape, BF16), vm(wout.shape, BF16), dma((2,)),
        ],
        compiler_params=params(60 << 20), name="feed_forward",
    )(s2, out_grad.reshape(tokens, width), win, wout, table)

    early, late = part(0), part(steps)
    ins = [sum_two, s1, remote, m2, q2, k2, v2, both, m1, source, q1, k1, v1, ws, wc, table]
    in_specs = [tok(early)] * 7 + [shares(lambda i: jnp.where(i < steps, i + steps, jnp.minimum(i - steps, steps - 1)))]
    in_specs += [tok(early), ANYWHERE] + [tok(late)] * 3
    in_specs += [ANYWHERE, fixed(SQUARES), table_spec]
    out_shape, out_specs = [low, low], [ANYWHERE, ANYWHERE]
    scratch = [vm((block, width), BF16), vm((3, tokens, width), BF16)] + [vm((tokens, width), BF16)] * 2 + [
        vm((steps, block, width), F32), vm(ONE_BLOCKS, F32), vm(SQUARES, F32), vm((TABLE, width), F32), dma((2 * steps,)),
        vm((tokens, width), BF16), vm(SQUARES, BF16), dma((2,))]
    if shards is not None:
        ins += [dwin.reshape(WIN_BLOCKS), dwout.reshape(WOUT_BLOCKS), dtable]
        in_specs += [ANYWHERE, ANYWHERE, table_spec]
        every = (WIN_BLOCKS, WOUT_BLOCKS, SQUARES, ONE_BLOCKS, ONE_BLOCKS, ONE_BLOCKS, ONE_BLOCKS, SMALL_BLOCKS)
        unit_shapes = [(4, s[0], s[5], s[6]) for s in every]
        out_shape += [shape_of(*s) for s in unit_shapes]
        out_specs += [ANYWHERE] * 8
        scratch += [vm(s[:4] + s[5:], BF16) for s in every[2:]]
        scratch += [vm(ONE_BLOCKS, BF16), vm(SMALL_BLOCKS, BF16)]
        cut = ((1, 2, 1), (1, 1, 2), (2, 1, 1)) + ((1, 1, 2),) * 5
        for s, (m, r, l) in zip(every, cut):
            scratch += [
                vm(s[:4] + s[5:], BF16), vm(s[:4] + s[5:], BF16),
                vm((2, s[0] // m, 4, s[5] // r, s[6] // l), BF16), vm((2, s[0], 4, s[5], s[6]), BF16)]
        scratch += [dma((8 * SCATTER_SLOTS,))] * 3
    else:
        out_shape += [shape_of(*SQUARES), shape_of(*SQUARES), table_shape]
        out_specs += [fixed(SQUARES), fixed(SQUARES), table_spec]
    grad_remote, grad_source, *tail = pl.pallas_call(
        functools.partial(last_kernel, shards is not None, steps),
        grid=(2 * steps + 1,), in_specs=in_specs, out_specs=out_specs, out_shape=out_shape, scratch_shapes=scratch,
        compiler_params=params(63 << 20, None if shards is None else 2), name="last",
    )(*ins)
    as_rows = lambda array: array.reshape(rows, slots, width)
    if shards is None:
        dself, dcross, dtable_last = tail
        grads = (dself.reshape(4, 512, 512), dcross.reshape(4, 512, 512), dwin, dwout, dtable + dtable_last)
    else:
        f = lambda *shape: shape_of(*shape, dtype=F32)
        in_vm = pl.BlockSpec(memory_space=pltpu.VMEM)
        *grads, grad_remote, grad_source = pl.pallas_call(
            sum_kernel,
            in_specs=[pl.BlockSpec(memory_space=pltpu.HBM)] * 10,
            out_specs=[in_vm] * 14 + [pl.BlockSpec(memory_space=pltpu.HBM)] * 2,
            out_shape=[f(3, 16, 512), f(3, 16), f(16, 512), f(2, 16), f(16, 512), f(2, 16, 512), f(3, 16), f(16, 512),
                       f(2, 16), f(64, 512), f(1, 64), f(16, 2048), f(1, 16), f(2, 16), low, low],
            scratch_shapes=[vm(s, BF16) for s in unit_shapes] + [vm((tokens, width), BF16)] * 2 + [dma((12,))],
            compiler_params=pltpu.CompilerParams(vmem_limit_bytes=63 << 20), name="sum_planes",
        )(*tail, grad_remote, grad_source)
    return as_rows(result), as_rows(grad_source), as_rows(grad_remote), grads


def turn(array):
    return jnp.swapaxes(array, -1, -2)


AXES = ("dp", "fsdp")


def gather_plain(parts, count):
    (self_qkv, self_bias, self_out, self_norm, cross_q, cross_kv, cross_bias, cross_out, cross_norm,
     ffn_in, ffn_in_bias, ffn_out, ffn_out_bias, ffn_norm) = parts
    cols = self_out.shape[1]
    width = self_out.shape[0]
    chunks = ffn_out.shape[0] // width
    small = jnp.concatenate(
        [self_bias, self_norm, cross_bias, cross_norm, ffn_out_bias[None], ffn_norm,
         ffn_in_bias.reshape(chunks, cols)], axis=0)
    small = jnp.pad(turn(small), ((0, 0), (0, width - small.shape[0])))
    packed = jnp.concatenate([
        turn(self_qkv).reshape(-1, width), turn(self_out), turn(cross_q),
        turn(cross_kv).reshape(-1, width), turn(cross_out), turn(ffn_in),
        turn(ffn_out).reshape(cols, chunks, width).swapaxes(0, 1).reshape(-1, width), small], axis=0)
    whole_set = lax.all_gather(packed, AXES, axis=0, tiled=False)
    square = whole_set[:, : 8 * cols].reshape(count, 8, cols, width).swapaxes(0, 1)
    square = square.reshape(8, width, width)
    low = 8 * cols
    win = whole_set[:, low : low + chunks * cols].reshape(chunks * width, width)
    low += chunks * cols
    wout = whole_set[:, low : low + chunks * cols].reshape(count, chunks, cols, width)
    wout = wout.transpose(0, 2, 1, 3).reshape(width, chunks * width)
    low += chunks * cols
    table = whole_set[:, low:]
    first = table[:, :, :13].transpose(2, 0, 1).reshape(13, width)
    second = table[:, :, 13 : 13 + chunks].transpose(0, 2, 1).reshape(chunks, width)
    table = jnp.concatenate([first, second], axis=0).astype(F32)
    table = jnp.pad(table, ((0, TABLE - table.shape[0]), (0, 0)))
    return square[:4], square[4:], win, wout, table


def scatter_plain(dself, dcross, dwin, dwout, dtable, count):
    width = dself.shape[1]
    cols = width // count
    chunks = dwin.shape[0] // width
    squares = jnp.concatenate([dself, dcross], axis=0).reshape(8, count, cols, width).swapaxes(0, 1)
    first = dtable[:13].reshape(13, count, cols).transpose(1, 2, 0)
    second = dtable[13 : 13 + chunks].reshape(count, chunks, cols).transpose(0, 2, 1)
    small = jnp.concatenate([first, second], axis=2)
    small = jnp.pad(small, ((0, 0), (0, 0), (0, width - small.shape[2]))).astype(BF16)
    packed = jnp.concatenate([
        squares.reshape(count, 8 * cols, width), dwin.reshape(count, chunks * cols, width),
        dwout.reshape(count, cols, chunks, width).swapaxes(1, 2).reshape(count, -1, width), small],
        axis=1)
    mine = lax.psum_scatter(packed, AXES, scatter_dimension=0, tiled=False).astype(F32)
    square = turn(mine[: 8 * cols].reshape(8, cols, width))
    low = 8 * cols
    ffn_in = turn(mine[low : low + chunks * cols])
    low += chunks * cols
    ffn_out = mine[low : low + chunks * cols].reshape(chunks, cols, width).swapaxes(0, 1)
    ffn_out = turn(ffn_out.reshape(cols, chunks * width))
    low += chunks * cols
    small = turn(mine[low:, : 13 + chunks])
    return (square[:3], small[0:3], square[3], small[3:5], square[4], square[5:7], small[5:8], square[7],
            small[8:10], ffn_in, small[13:].reshape(-1), ffn_out, small[10], small[11:13])


def on_device(count, direct, decoder_in, memory, out_grad, tgt_len, src_len, *parts):
    if not direct:
        weights = gather_plain(parts, count)
        result, grad_source, grad_remote, grads = layer(
            decoder_in, memory, out_grad, tgt_len, src_len, weights=weights)
        return (result, grad_source, grad_remote, *scatter_plain(*grads, count))
    (self_qkv, self_bias, self_out, self_norm, cross_q, cross_kv, cross_bias, cross_out, cross_norm,
     ffn_in, ffn_in_bias, ffn_out, ffn_out_bias, ffn_norm) = parts
    big = [turn(part) for part in (self_qkv, self_out, cross_q, cross_kv, cross_out, ffn_in, ffn_out)]
    big = [part.reshape((-1,) + part.shape[-2:]) for part in big]
    small = [self_bias, self_norm, cross_bias, cross_norm, ffn_out_bias.reshape(1, -1), ffn_norm, ffn_in_bias.reshape(1, -1)]
    shards = big, small
    result, grad_source, grad_remote, grads = layer(
        decoder_in, memory, out_grad, tgt_len, src_len, shards=shards)
    (qkv, bias_one, out_one, norm_one, query, pair, bias_two, out_two, norm_two, win, win_bias, wout, wout_bias,
     norm_three) = grads
    return (result, grad_source, grad_remote, turn(qkv), bias_one, turn(out_one), norm_one, turn(query), turn(pair),
            bias_two, turn(out_two), norm_two, turn(win), win_bias.reshape(-1), turn(wout), wout_bias.reshape(-1),
            norm_three)


def solution(mesh):
    count = mesh.shape["dp"] * mesh.shape["fsdp"]
    direct = mesh.shape["dp"] == 4 and mesh.shape["fsdp"] == 8
    rows = P(AXES, None, None)
    lens = P(AXES, None)
    cube = P(None, None, AXES)
    flat = P(None, AXES)
    line = P(AXES)
    params_in = (cube, flat, flat, flat, flat, cube, flat, flat, flat, flat, line, flat, line, flat)
    return jax.shard_map(
        functools.partial(on_device, count, direct),
        mesh=mesh,
        in_specs=(rows, rows, rows, lens, lens) + params_in,
        out_specs=(rows, rows, rows) + params_in,
        check_vma=False,
    )
```
